256 devices in a mesh: branch: 8 (over x, y_lo), expert: 32 (over z, y_hi, core).
Axes of the slice: x: 4, y: 4 (y_hi: 2, y_lo: 2; y = y_hi * 2 + y_lo), z: 8, core: 2. Of those that a mesh axis runs over, the one named last changes fastest.
Arguments:
- residual: bfloat16 [2048, 4096], P('branch', 'expert'), may hold values from -6 to 6
- heads_out: bfloat16 [2048, 4096], P('branch', 'expert'), may hold values from -6 to 6
- out_proj: bfloat16 [8, 4096, 4096], P('branch', 'expert'), may hold values from -0.25 to 0.25
- norm_gain: bfloat16 [4096], P('expert'), may hold values from 0.5 to 2
- gate_w: bfloat16 [8, 4096, 8192], P('branch', None, 'expert'), may hold values from -0.09375 to 0.09375
- up_w: bfloat16 [8, 4096, 8192], P('branch', None, 'expert'), may hold values from -0.09375 to 0.09375
- down_w: bfloat16 [8, 8192, 4096], P('branch', 'expert'), may hold values from -0.0625 to 0.0625
- expert_ids: int32 [2048, 2], P('branch'), may hold values from 0 to 7, all different within a row; in each aligned block of 256 rows (0 to 255, 256 to 511, ...) at most 96 rows name the same one
- gate_slots: int32 [2048, 2], P('branch'), may hold values from 0 to 63
- gate_table: float32 [64], replicated, may hold values from 0.25 to 4
Outputs:
- layer_out: bfloat16 [2048, 4096], P('branch', 'expert')
The draws below stay inside these ranges and needn't reach their ends.
Inputs may be any that keep to these rules, and one draw needn't show every extreme that they name: `expert_ids`: each token names two different experts. In each aligned block of 256 tokens no expert is named by more than 96 tokens, a bound that some block reaches.
All inputs are finite; a program needn't handle non-finite values.
Results may differ from the reference program's by a relative error of at most 0.02.
Values may be sent and summed in bfloat16 or wider, within the bound.
A program may use at most 64 MiB of HBM per device.

```python
import math
import jax
import jax.numpy as jnp
import numpy as np
from jax import lax

D = 4096
FFW = 8192
TOK_DEV = 256
SLOTS = 64
BRANCHES = 8
TOKENS = 2048
CAP = 96
N_EXPERT = 32


def set_ends(drawn, stream_key, smallest, high):
    index_at = [jax.random.randint(jax.random.fold_in(stream_key, axis), (), 0, length) for axis, length in enumerate(drawn.shape)]
    widest = drawn.shape.index(max(drawn.shape))
    next_to = index_at[:widest] + [(index_at[widest] + 1) % drawn.shape[widest]] + index_at[widest + 1:]
    return drawn.at[tuple(index_at)].set(smallest).at[tuple(next_to)].set(high)


def steps_of(rng, extent, pieces, low, high):
    loudness = 1.0
    for axis_at, shards_of in pieces:
        steps = jax.random.uniform(jax.random.fold_in(jax.random.fold_in(rng, 6), axis_at), (shards_of,), jnp.float32, low / len(pieces), high / len(pieces))
        loudness = loudness * jnp.repeat(jnp.exp(steps), extent[axis_at] // shards_of).reshape((-1,) + (1,) * (len(extent) - 1 - axis_at))
    return loudness


def routed_block(rng, own, number, rows, number_of, top, reach, slope):
    order = jax.random.permutation(rng, number_of)
    heavy_load, ordinary = portions_of(number_of, rows * top, reach, slope, True), portions_of(number_of, rows * top, reach, slope, False)
    places = jnp.arange(number_of)

    def named(sizes, turn):
        used = int((sizes > 0).sum())
        fixed = max(1, used // 4)
        moved = fixed + (places - fixed + turn * (used - fixed)) % max(1, number_of - fixed)
        return jnp.zeros((number_of,), jnp.int32).at[order[jnp.where(places < fixed, places, moved)]].set(jnp.asarray(sizes, jnp.int32))

    sizes = jnp.where(number % 4 == 0, named(heavy_load, number // 4), named(ordinary, number - number // 4 - 1))
    mixed = jax.random.permutation(jax.random.fold_in(own, 3), number_of)
    donor, receiver = mixed[0:number_of // 2 * 2:2], mixed[1:number_of // 2 * 2:2]
    margin = jnp.minimum(sizes[donor] - 1, reach - sizes[receiver]) // 2
    margin = jnp.where((donor == order[0]) | (receiver == order[0]) | (sizes[receiver] == 0), 0, jnp.maximum(margin, 0))
    moved = jax.random.randint(jax.random.fold_in(own, 4), (number_of // 2,), 0, 1 << 20) % (margin + 1)
    sizes = sizes.at[donor].add(-moved).at[receiver].add(moved)
    items = jnp.searchsorted(jnp.cumsum(sizes), jnp.arange(rows * top), side="right").astype(jnp.int32)
    listing = items.reshape(top, rows).T
    listing = listing[jax.random.permutation(jax.random.fold_in(own, 1), rows)]
    turn = jax.random.randint(jax.random.fold_in(own, 2), (rows, 1), 0, top)
    return jnp.take_along_axis(listing, (jnp.arange(top)[None, :] + turn) % top, axis=1)


def portions_of(amount, total, bound, skew, full):
    weights = [(1 << 20) // math.isqrt(grade ** skew) + 1 for grade in range(1, amount + 1)]
    largest = bound if full else min(bound, max(-(-total // amount), total * weights[0] // sum(weights)))
    least = 1 if total - largest >= amount - 1 else 0
    given, spare = [largest] + [least] * (amount - 1), total - largest - least * (amount - 1)
    while spare > 0:
        free = [i for i in range(1, amount) if given[i] < largest] or [i for i in range(1, amount) if given[i] < bound]
        whole, remaining = sum([weights[i] for i in free]), spare
        for i in free:
            addition = min(bound - given[i], max(1, remaining * weights[i] // whole), spare)
            given[i] = given[i] + addition
            spare = spare - addition
    return np.array(given)


def noise(key, extent, width, most, pieces=(), kind=jnp.bfloat16):
    gain = steps_of(key, extent, pieces, -0.22, 0.18) if pieces else 1.0
    drawn = jax.random.normal(key, extent, jnp.float32) * width * gain
    return jnp.minimum(jnp.maximum(drawn, -most), most).astype(kind)


def setup_inputs(seed: int = 0) -> dict:
    streams_of = jax.random.split(jax.random.key(seed), 11)
    residual = noise(streams_of[0], (TOKENS, D), 1.0, 6.0, ((0, 8), (1, 32)))
    heads_out = noise(streams_of[1], (TOKENS, D), 1.0, 6.0, ((0, 8), (1, 32)))
    out_proj = noise(streams_of[2], (BRANCHES, D, D), (D // BRANCHES) ** -0.5, 0.25, ((0, 8), (1, 32)))
    norm_gain = jnp.clip(jnp.exp(math.log(2.0) - 1.3862944 * jax.random.uniform(streams_of[3], (D,), jnp.float32) ** steps_of(streams_of[3], (D,), ((0, 32),), -0.2, 0.2)), 0.5, 2.0).astype(jnp.bfloat16)
    gate_w = noise(streams_of[4], (BRANCHES, D, FFW), D ** -0.5, 0.09375, ((0, 8), (2, 32)))
    up_w = noise(streams_of[5], (BRANCHES, D, FFW), D ** -0.5, 0.09375, ((0, 8), (2, 32)))
    down_w = noise(streams_of[6], (BRANCHES, FFW, D), FFW ** -0.5, 0.0625, ((0, 8), (1, 32)))
    expert_ids_keys = jax.random.split(jax.random.fold_in(streams_of[7], 1), TOKENS // TOK_DEV)
    expert_ids_turns = jax.random.permutation(jax.random.fold_in(streams_of[7], 3), TOKENS // TOK_DEV)
    expert_ids = jax.vmap(lambda own, number: routed_block(jax.random.fold_in(streams_of[7], 2), own, number, TOK_DEV, BRANCHES, 2, CAP, 2))(expert_ids_keys, expert_ids_turns).reshape((TOKENS, 2))
    gate_slots = set_ends(jax.random.randint(streams_of[8], (TOKENS, 2), 0, SLOTS), jax.random.fold_in(streams_of[8], 1), 0, SLOTS - 1).astype(jnp.int32)
    gate_table = jnp.clip(jnp.exp(jax.random.uniform(streams_of[9], (SLOTS,), jnp.float32, math.log(0.25), math.log(4.0))), 0.25, 4.0)
    return dict(residual=residual, heads_out=heads_out, out_proj=out_proj, norm_gain=norm_gain, gate_w=gate_w, up_w=up_w, down_w=down_w, expert_ids=expert_ids, gate_slots=gate_slots, gate_table=gate_table)


def reference(residual, heads_out, out_proj, norm_gain, gate_w, up_w, down_w, expert_ids, gate_slots, gate_table):
    merged = (lax.optimization_barrier(jnp.sum(out_proj.astype(jnp.float32), axis=0)) / BRANCHES).astype(jnp.bfloat16)
    stream = residual.astype(jnp.float32) + jnp.dot(heads_out, merged, preferred_element_type=jnp.float32)
    mean_sq = lax.optimization_barrier(jnp.mean(stream * stream, axis=1, keepdims=True))
    normed = (stream * lax.rsqrt(mean_sq + 1e-05) * norm_gain.astype(jnp.float32)[None, :]).astype(jnp.bfloat16)
    grouped = expert_ids.reshape(BRANCHES, TOK_DEV * 2)
    onehot = (grouped[:, :, None] == jnp.arange(BRANCHES, dtype=jnp.int32)[None, None, :]).astype(jnp.int32)
    ranks = jnp.cumsum(onehot, axis=1) - 1
    slot = lax.optimization_barrier(jnp.sum(ranks * onehot, axis=2))
    source = jnp.arange(BRANCHES, dtype=jnp.int32)[:, None]
    row_index = (source * CAP + slot).reshape(-1).astype(jnp.int32)
    flat_expert = grouped.reshape(-1).astype(jnp.int32)
    token_index = (jnp.arange(TOKENS * 2, dtype=jnp.int32) // 2).astype(jnp.int32)
    buffers = jnp.zeros((BRANCHES, BRANCHES * CAP, D), jnp.bfloat16)
    buffers = buffers.at[flat_expert, row_index].set(normed[token_index])
    shard_width = FFW // N_EXPERT

    def expert_out(operands):
        rows, wgate, wup, wdown = operands
        gate_shards = wgate.reshape(D, N_EXPERT, shard_width).transpose(1, 0, 2)
        up_shards = wup.reshape(D, N_EXPERT, shard_width).transpose(1, 0, 2)
        down_shards = wdown.reshape(N_EXPERT, shard_width, D)

        def shard_step(total, shard):
            g_part, u_part, d_part = shard
            gate = jnp.dot(rows, g_part, preferred_element_type=jnp.float32)
            upper = jnp.dot(rows, u_part, preferred_element_type=jnp.float32)
            hidden = (jax.nn.silu(gate) * upper).astype(jnp.bfloat16)
            partial_out = lax.optimization_barrier(jnp.dot(hidden, d_part, preferred_element_type=jnp.float32).astype(jnp.bfloat16))
            return (total + partial_out.astype(jnp.float32), None)
        total, _ = lax.scan(shard_step, jnp.zeros((BRANCHES * CAP, D), jnp.float32), (gate_shards, up_shards, down_shards))
        return total
    expert_rows = lax.map(expert_out, (buffers, gate_w, up_w, down_w))
    picked = expert_rows[flat_expert, row_index].reshape(TOKENS, 2, D)
    raw_gates = gate_table[gate_slots]
    gates = raw_gates / lax.optimization_barrier(jnp.sum(raw_gates, axis=1, keepdims=True))
    ffn = lax.optimization_barrier(jnp.sum(gates[:, :, None] * picked, axis=1))
    return (stream + ffn).astype(jnp.bfloat16)
```

```python
import jax
import jax.numpy as jnp
from jax import lax
from jax.experimental import pallas as pl
from jax.experimental.pallas import tpu as pltpu
from jax.sharding import PartitionSpec as P

MESH = pl.DeviceIdType.MESH
F32, BF16 = jnp.float32, jnp.bfloat16
D = 4096
SLOTS = 64
NB = 8
NZ = 8
TOK = 256
CAP = 96
ROWS = 4 * CAP
GROWS = 16
BLK = ROWS + GROWS
FW = 128
CW = 256
HALF_A = 208
HALF_E = ROWS // 2


def rcopy(src, dst, send_sem, recv_sem, dev):
    return pltpu.make_async_remote_copy(
        src_ref=src, dst_ref=dst, send_sem=send_sem, recv_sem=recv_sem,
        device_id=dev, device_id_type=MESH)


def kernel(res_hbm, heads_hbm, op_hbm, gain_ref, gate_hbm, up_hbm, down_hbm, idst_ref, slots_ref,
           table_ref, out_ref,
           res_v, heads_v, op_in, merged, w4, dn, s0, s1, b_snd, b_rcv, tot, y_snd, y_rcv, t_snd, t_rcv,
           stream, dsp, xg, acc, sq, hid, e_part, e_snd, e_rcv, e_keep, ey_snd, ey_rcv, ret_snd, ret_v,
           loc, w_s, w_r, h_s, h_r, hf_s, hf_r, op_s, op_r, b_s, b_r, yt_s, yt_r, g_s, g_r,
           c_s, c_r, ag_s, ag_r, agy_s, agy_r, e_s, e_r, ey_s, ey_r, f_s, f_r):
    b = lax.axis_index("branch")
    e = lax.axis_index("expert")
    z = e // 4
    yh = (e // 2) % 2
    c = e % 2
    half = b // 4
    sib = (b, e + 1 - 2 * c)
    right = (b, ((z + 1) % NZ) * 4 + yh * 2 + c)
    left = (b, ((z + NZ - 1) % NZ) * 4 + yh * 2 + c)
    ypart = (b, z * 4 + (1 - yh) * 2 + c)
    tpart = (z, b * 4 + c * 2 + yh)
    t_self = jnp.logical_and(z == b, yh == c)
    dirs = (right, left)

    def chip_dev(j, core):
        return (j, z * 4 + yh * 2 + core)

    loads = [
        pltpu.make_async_copy(res_hbm, res_v, loc.at[0]),
        pltpu.make_async_copy(
            heads_hbm,
            heads_v.at[pl.ds(pl.multiple_of(b * TOK, TOK), TOK), pl.ds(pl.multiple_of(c * FW, FW), FW)],
            loc.at[1]),
        pltpu.make_async_copy(
            op_hbm.at[:, pl.ds(pl.multiple_of((b * 2 + c) * CW, CW), CW)], op_in.at[b * 2 + c], loc.at[2]),
        pltpu.make_async_copy(gate_hbm, w4.at[0], loc.at[3]),
        pltpu.make_async_copy(up_hbm, w4.at[2], loc.at[4]),
        pltpu.make_async_copy(down_hbm, dn.at[0], loc.at[5]),
    ]
    for ld in loads:
        ld.start()

    barrier = pltpu.get_barrier_semaphore()
    for kb in range(NB):
        for kc in range(2):
            if kb or kc:
                pl.semaphore_signal(barrier, inc=1, device_id=chip_dev((b + kb) % NB, (c + kc) % 2),
                                    device_id_type=MESH)
    for dev in (right, left, ypart):
        pl.semaphore_signal(barrier, inc=1, device_id=dev, device_id_type=MESH)

    @pl.when(jnp.logical_not(t_self))
    def _():
        pl.semaphore_signal(barrier, inc=1, device_id=tpart, device_id_type=MESH)

    pl.semaphore_wait(barrier, jnp.where(t_self, 18, 19))

    pend = []
    my_heads = heads_v.at[pl.ds(pl.multiple_of(b * TOK, TOK), TOK), pl.ds(pl.multiple_of(c * FW, FW), FW)]
    for k in range(1, NB):
        cp = rcopy(heads_hbm, my_heads, h_s.at[k - 1], h_r.at[k - 1], chip_dev((b + k) % NB, c))
        cp.start()
        pend.append(cp)
    for kb in range(NB):
        for kc in range(2):
            if kb or kc:
                j, cc = (b + kb) % NB, (c + kc) % 2
                cp = rcopy(op_hbm.at[:, pl.ds(pl.multiple_of((j * 2 + cc) * CW, CW), CW)],
                           op_in.at[b * 2 + c], op_s.at[kb * 2 + kc], op_r.at[kb * 2 + kc], chip_dev(j, cc))
                cp.start()
                pend.append(cp)
    for i, (src, dst) in enumerate(((gate_hbm, w4.at[1]), (up_hbm, w4.at[3]), (down_hbm, dn.at[1]))):
        cp = rcopy(src, dst, w_s.at[i], w_r.at[i], sib)
        cp.start()
        pend.append(cp)

    me = z * 2 + yh
    gain_at = (me, pl.ds(ROWS, GROWS), pl.ds(pl.multiple_of(c * FW, FW), FW))
    xg[gain_at] = jnp.broadcast_to(gain_ref[...], (GROWS, FW))
    gain_cp = rcopy(xg.at[gain_at], xg.at[gain_at], g_s, g_r, sib)
    gain_cp.start()
    pend.append(gain_cp)

    ids = idst_ref[...]
    xi = lax.broadcasted_iota(jnp.int32, (16, TOK), 0)
    named = ((ids[0:1] == xi) | (ids[1:2] == xi)).astype(BF16)
    before = (lax.broadcasted_iota(jnp.int32, (TOK, TOK), 0)
              < lax.broadcasted_iota(jnp.int32, (TOK, TOK), 1)).astype(BF16)
    rank = jnp.dot(named, before, preferred_element_type=F32).astype(jnp.int32)
    ci = lax.broadcasted_iota(jnp.int32, (CAP, TOK), 0)
    for x in range(NB):
        hit = rank[x:x + 1] == ci
        s0[x * CAP:(x + 1) * CAP] = (hit & (ids[0:1] == x)).astype(BF16)
        s1[x * CAP:(x + 1) * CAP] = (hit & (ids[1:2] == x)).astype(BF16)
    acc[...] = jnp.zeros_like(acc)
    sq[...] = jnp.zeros_like(sq)

    loads[1].wait()
    for k in range(1, NB):
        src_b = (b + NB - k) % NB
        rcopy(heads_hbm,
              heads_v.at[pl.ds(pl.multiple_of(src_b * TOK, TOK), TOK), pl.ds(pl.multiple_of(c * FW, FW), FW)],
              h_s.at[k - 1], h_r.at[k - 1], sib).wait_recv()
    mine_cols = heads_v.at[:, pl.ds(pl.multiple_of(c * FW, FW), FW)]
    their_cols = heads_v.at[:, pl.ds(pl.multiple_of((1 - c) * FW, FW), FW)]
    cp = rcopy(mine_cols, mine_cols, hf_s, hf_r, sib)
    cp.start()
    pend.append(cp)

    loads[2].wait()
    for kb in range(NB):
        for kc in range(2):
            if kb or kc:
                rcopy(op_hbm.at[:, pl.ds(0, CW)], op_in.at[((b + NB - kb) % NB) * 2 + (c + kc) % 2],
                      op_s.at[kb * 2 + kc], op_r.at[kb * 2 + kc], sib).wait_recv()
    for cc in range(2):
        total = op_in[cc].astype(F32)
        for j in range(1, NB):
            total = total + op_in[j * 2 + cc].astype(F32)
        merged[cc * FW:(cc + 1) * FW] = (total / NB).astype(BF16)
    rcopy(their_cols, their_cols, hf_s, hf_r, sib).wait_recv()

    def attn_part(zd):
        return jnp.dot(heads_v[pl.ds(pl.multiple_of(zd * TOK, TOK), TOK), :], merged[...],
                       preferred_element_type=F32)

    def b_copy(d, s):
        if s == 0:
            rows = pl.ds(d * 128, 128)
            return rcopy(b_snd.at[d, 0, rows], b_rcv.at[d, 0, rows], b_s.at[d, s], b_r.at[d, s], dirs[d])
        return rcopy(b_snd.at[d, s], b_rcv.at[d, s], b_s.at[d, s], b_r.at[d, s], dirs[d])

    p = attn_part((z + 4) % NZ)
    b_snd[0, 0, 0:128] = p[0:128].astype(BF16)
    b_snd[1, 0, 128:256] = p[128:256].astype(BF16)
    for d in range(2):
        b_copy(d, 0).start()
    for s in range(1, 4):
        for d in range(2):
            zd = (z + (4 - s)) % NZ if d == 0 else (z + NZ - (4 - s)) % NZ
            tot[d] = attn_part(zd)
        for d in range(2):
            b_copy(d, s - 1).wait_recv()
            if s == 1:
                lo, hi = (0, 128) if d == 0 else (128, 256)
                b_snd[d, s, lo:hi] = (tot[d, lo:hi] + b_rcv[d, 0, lo:hi].astype(F32)).astype(BF16)
                b_snd[d, s, 128 - lo:384 - hi] = tot[d, 128 - lo:384 - hi].astype(BF16)
            else:
                b_snd[d, s] = (tot[d] + b_rcv[d, s - 1].astype(F32)).astype(BF16)
            b_copy(d, s).start()
    tot[0] = attn_part(z)
    for d in range(2):
        b_copy(d, 3).wait_recv()
    tot[0] = tot[0] + b_rcv[0, 3].astype(F32) + b_rcv[1, 3].astype(F32)
    for d in range(2):
        for s in range(4):
            pend.append(b_copy(d, s))
    y_snd[...] = tot[0, :, pl.ds(pl.multiple_of((1 - yh) * FW, FW), FW)].astype(BF16)
    cp = rcopy(y_snd, y_rcv, yt_s.at[0], yt_r.at[0], ypart)
    cp.start()
    pend.append(cp)
    cp.wait_recv()
    t_snd[...] = (tot[0, :, pl.ds(pl.multiple_of(yh * FW, FW), FW)] + y_rcv[...].astype(F32)).astype(BF16)
    t_copy = rcopy(t_snd, t_rcv, yt_s.at[1], yt_r.at[1], tpart)

    @pl.when(t_self)
    def _():
        t_rcv[...] = t_snd[...]

    @pl.when(jnp.logical_not(t_self))
    def _():
        t_copy.start()
        t_copy.wait_recv()

    loads[0].wait()
    st = res_v[...].astype(F32) + t_rcv[...].astype(F32)
    stream[...] = st
    scaled = (st * gain_ref[...].astype(F32)).astype(BF16)
    dsp[...] = jnp.dot(s0[...] + s1[...], scaled, preferred_element_type=F32).astype(BF16)
    blk_at = (me, pl.ds(pl.multiple_of((b % 4) * CAP, CAP), CAP), pl.ds(pl.multiple_of(c * FW, FW), FW))
    my_src = half == c

    def c_copy(k):
        x = (b + k) % NB
        return rcopy(dsp.at[pl.ds(pl.multiple_of(x * CAP, CAP), CAP)], xg.at[blk_at], c_s.at[k],
                     c_r.at[(b % 4) * 2 + c], chip_dev(x, half))

    own_blk = pltpu.make_async_copy(dsp.at[pl.ds(pl.multiple_of(b * CAP, CAP), CAP)], xg.at[blk_at], loc.at[6])
    for k in range(1, NB):
        c_copy(k).start()
        pend.append(c_copy(k))

    @pl.when(my_src)
    def _():
        own_blk.start()

    @pl.when(jnp.logical_not(my_src))
    def _():
        c_copy(0).start()

    for i in range(8):
        @pl.when(jnp.logical_not(jnp.logical_and(my_src, (b % 4) * 2 + c == i)))
        def _(i=i):
            rcopy(dsp.at[pl.ds(0, CAP)], xg.at[me, pl.ds((i // 2) * CAP, CAP), pl.ds((i % 2) * FW, FW)],
                  c_s.at[0], c_r.at[i], sib).wait_recv()

    @pl.when(my_src)
    def _():
        own_blk.wait()

    sib_gain = xg.at[me, pl.ds(ROWS, GROWS), pl.ds(pl.multiple_of((1 - c) * FW, FW), FW)]
    rcopy(sib_gain, sib_gain, g_s, g_r, sib).wait_recv()

    def ag_copy(d, t, s, slot):
        if s == 3:
            ref = xg.at[slot, pl.ds(0, HALF_A)] if d == 0 else xg.at[slot, pl.ds(HALF_A, BLK - HALF_A)]
        else:
            ref = xg.at[slot]
        return rcopy(ref, ref, ag_s.at[d, t, s], ag_r.at[d, t, s], dirs[d])

    def gate_up(slot):
        blk = xg[slot, 0:ROWS]
        inv = 1.0 / xg[slot, ROWS:BLK][0:1].astype(F32)
        v = blk.astype(F32) * inv
        sq[...] += v * v
        rows = pl.ds(pl.multiple_of(slot * CW, CW), CW)

        def part(i, carry):
            acc[i] += jnp.dot(xg[slot, 0:ROWS], w4[i, rows, :], preferred_element_type=F32)
            return carry
        lax.fori_loop(0, 4, part, 0)

    def start(cp):
        cp.start()
        pend.append(cp)

    other = z * 2 + 1 - yh
    start(rcopy(xg.at[me], xg.at[me], agy_s, agy_r, ypart))
    for d in range(2):
        start(ag_copy(d, 0, 0, me))
    loads[3].wait()
    loads[4].wait()
    for i in range(2):
        rcopy(gate_hbm, w4.at[1 + 2 * i], w_s.at[i], w_r.at[i], sib).wait_recv()
    gate_up(me)
    rcopy(xg.at[other], xg.at[other], agy_s, agy_r, ypart).wait_recv()
    for d in range(2):
        start(ag_copy(d, 1, 0, other))
    gate_up(other)
    for s in range(1, 4):
        for t in range(2):
            yy = yh if t == 0 else 1 - yh
            slots = [((z + NZ - s) % NZ) * 2 + yy, ((z + s) % NZ) * 2 + yy]
            for d in range(2):
                ag_copy(d, t, s - 1, slots[d]).wait_recv()
                start(ag_copy(d, t, s, slots[d]))
            for d in range(2):
                gate_up(slots[d])
    for t in range(2):
        yy = yh if t == 0 else 1 - yh
        slot = ((z + 4) % NZ) * 2 + yy
        for d in range(2):
            ag_copy(d, t, 3, slot).wait_recv()
        gate_up(slot)

    scale = lax.rsqrt(jnp.sum(sq[...], axis=1, keepdims=True) / D + 1e-05)
    for i in range(2):
        g = acc[i] * scale
        hid[i] = (g / (1.0 + jnp.exp(-g)) * (acc[2 + i] * scale)).astype(BF16)
    loads[5].wait()
    rcopy(down_hbm, dn.at[1], w_s.at[2], w_r.at[2], sib).wait_recv()

    def down_part(zd, t):
        yy = 1 - yh if t == 0 else yh
        cols = pl.ds(pl.multiple_of((zd * 2 + yy) * CW, CW), CW)
        return (jnp.dot(hid[0], dn[0, :, cols], preferred_element_type=F32)
                + jnp.dot(hid[1], dn[1, :, cols], preferred_element_type=F32))

    def e_copy(d, t, s):
        if s == 0:
            rows = pl.ds(d * HALF_E, HALF_E)
            return rcopy(e_snd.at[d, t, 0, rows], e_rcv.at[d, t, 0, rows], e_s.at[d, t, s], e_r.at[d, t, s],
                         dirs[d])
        return rcopy(e_snd.at[d, t, s], e_rcv.at[d, t, s], e_s.at[d, t, s], e_r.at[d, t, s], dirs[d])

    for t in range(2):
        p = down_part((z + 4) % NZ, t)
        e_snd[0, t, 0, 0:HALF_E] = p[0:HALF_E].astype(BF16)
        e_snd[1, t, 0, HALF_E:ROWS] = p[HALF_E:ROWS].astype(BF16)
        for d in range(2):
            start(e_copy(d, t, 0))
    for s in range(1, 4):
        for t in range(2):
            for d in range(2):
                e_part[d, t] = down_part((z + (4 - s)) % NZ if d == 0 else (z + NZ - (4 - s)) % NZ, t)
        for t in range(2):
            for d in range(2):
                e_copy(d, t, s - 1).wait_recv()
                if s == 1:
                    lo, hi = (0, HALF_E) if d == 0 else (HALF_E, ROWS)
                    e_snd[d, t, s, lo:hi] = (e_part[d, t, lo:hi] + e_rcv[d, t, 0, lo:hi].astype(F32)).astype(BF16)
                    lo, hi = HALF_E - lo, ROWS + HALF_E - hi
                    e_snd[d, t, s, lo:hi] = e_part[d, t, lo:hi].astype(BF16)
                else:
                    e_snd[d, t, s] = (e_part[d, t] + e_rcv[d, t, s - 1].astype(F32)).astype(BF16)
                start(e_copy(d, t, s))
    for t in range(2):
        e_part[0, t] = down_part(z, t)
    for t in range(2):
        for d in range(2):
            e_copy(d, t, 3).wait_recv()
        tail = e_part[0, t] + e_rcv[0, t, 3].astype(F32) + e_rcv[1, t, 3].astype(F32)
        if t == 0:
            ey_snd[...] = tail.astype(BF16)
            ey = rcopy(ey_snd, ey_rcv, ey_s, ey_r, ypart)
            start(ey)
        else:
            e_keep[...] = tail
    ey.wait_recv()
    ret_snd[...] = (e_keep[...] + ey_rcv[...].astype(F32)).astype(BF16)

    def f_copy(i, cc):
        return rcopy(ret_snd.at[pl.ds(i * CAP, CAP), pl.ds(cc * FW, FW)],
                     ret_v.at[pl.ds(pl.multiple_of(b * CAP, CAP), CAP)],
                     f_s.at[i * 2 + cc], f_r.at[b], chip_dev(4 * c + i, cc))

    for i in range(4):
        for cc in range(2):
            to_self = jnp.logical_and(4 * c + i == b, cc == c)
            mine = pltpu.make_async_copy(ret_snd.at[pl.ds(i * CAP, CAP), pl.ds(cc * FW, FW)],
                                         ret_v.at[pl.ds(pl.multiple_of(b * CAP, CAP), CAP)], loc.at[7])

            @pl.when(to_self)
            def _(mine=mine):
                mine.start()
                mine.wait()

            @pl.when(jnp.logical_not(to_self))
            def _(i=i, cc=cc):
                f_copy(i, cc).start()

    slot_i = lax.broadcasted_iota(jnp.int32, (TOK, SLOTS), 1)
    raw = [jnp.sum(jnp.where(slots_ref[:, k:k + 1] == slot_i, table_ref[...], 0.0), axis=1, keepdims=True)
           for k in range(2)]
    norm = raw[0] + raw[1]

    for x in range(NB):
        @pl.when(jnp.logical_not(jnp.logical_and(my_src, b == x)))
        def _(x=x):
            rcopy(ret_snd.at[pl.ds(0, CAP), pl.ds(0, FW)], ret_v.at[pl.ds(x * CAP, CAP)], f_s.at[0], f_r.at[x],
                  sib).wait_recv()
    result = stream[...]
    for k, sel in enumerate((s0, s1)):
        picked = lax.dot_general(sel[...], ret_v[...], (((0,), (0,)), ((), ())), preferred_element_type=F32)
        result = result + raw[k] / norm * picked
    out_ref[...] = result.astype(BF16)

    for cp in pend:
        cp.wait_send()

    @pl.when(jnp.logical_not(t_self))
    def _():
        t_copy.wait_send()

    @pl.when(jnp.logical_not(my_src))
    def _():
        c_copy(0).wait_send()

    for i in range(4):
        for cc in range(2):
            @pl.when(jnp.logical_not(jnp.logical_and(4 * c + i == b, cc == c)))
            def _(i=i, cc=cc):
                f_copy(i, cc).wait_send()


def per_device(residual, heads_out, out_proj, norm_gain, gate_w, up_w, down_w, expert_ids, gate_slots, gate_table):
    any_, vmem = pl.BlockSpec(memory_space=pl.ANY), pl.BlockSpec(memory_space=pltpu.VMEM)
    dma, v = pltpu.SemaphoreType.DMA, pltpu.VMEM
    return pl.pallas_call(
        kernel,
        out_shape=jax.ShapeDtypeStruct((TOK, FW), BF16),
        in_specs=[any_, any_, any_, vmem, any_, any_, any_, vmem, vmem, vmem],
        out_specs=vmem,
        scratch_shapes=[
            v((TOK, FW), BF16), v((NB * TOK, CW), BF16), v((16, FW, CW), BF16), v((CW, CW), BF16),
            v((4, D, CW), BF16), v((2, CW, D), BF16), v((NB * CAP, TOK), BF16), v((NB * CAP, TOK), BF16),
            v((2, 4, TOK, CW), BF16), v((2, 4, TOK, CW), BF16), v((2, TOK, CW), F32),
            v((TOK, FW), BF16), v((TOK, FW), BF16), v((TOK, FW), BF16), v((TOK, FW), BF16),
            v((TOK, FW), F32), v((NB * CAP, FW), BF16), v((16, BLK, CW), BF16), v((4, ROWS, CW), F32),
            v((ROWS, CW), F32), v((2, ROWS, CW), BF16), v((2, 2, ROWS, CW), F32),
            v((2, 2, 4, ROWS, CW), BF16), v((2, 2, 4, ROWS, CW), BF16), v((ROWS, CW), F32),
            v((ROWS, CW), BF16), v((ROWS, CW), BF16), v((ROWS, CW), BF16), v((NB * CAP, FW), BF16),
            dma((8,)), dma((3,)), dma((3,)), dma((7,)), dma((7,)), dma, dma, dma((16,)), dma((16,)),
            dma((2, 4)), dma((2, 4)), dma((2,)), dma((2,)), dma, dma,
            dma((8,)), dma((8,)), dma((2, 2, 4)), dma((2, 2, 4)), dma, dma,
            dma((2, 2, 4)), dma((2, 2, 4)), dma, dma, dma((8,)), dma((8,)),
        ],
        compiler_params=pltpu.CompilerParams(
            collective_id=0, has_side_effects=True, vmem_limit_bytes=60 * 1024 * 1024),
        name="merge_moe",
    )(residual, heads_out, out_proj[0], norm_gain.reshape(1, FW), gate_w[0], up_w[0], down_w[0],
      expert_ids.T, gate_slots, gate_table.reshape(1, SLOTS))


def solution(mesh):
    return jax.shard_map(
        per_device,
        mesh=mesh,
        in_specs=(
            P("branch", "expert"), P("branch", "expert"), P("branch", "expert", None), P("expert"),
            P("branch", None, "expert"), P("branch", None, "expert"), P("branch", "expert", None),
            P("branch", None), P("branch", None), P(),
        ),
        out_specs=P("branch", "expert"),
        check_vma=False,
    )
```

```python
import jax
import jax.numpy as jnp
from jax import lax
from jax.experimental import pallas as pl
from jax.experimental.pallas import tpu as pltpu
from jax.sharding import PartitionSpec as P

MESH = pl.DeviceIdType.MESH
F32, BF16 = jnp.float32, jnp.bfloat16
D = 4096
SLOTS = 64
NB = 8
NZ = 8
TOK = 256
CAP = 96
ROWS = 4 * CAP
GROWS = 16
BLK = ROWS + GROWS
FW = 128
CW = 256
RD = 176
RE = 160
HALF_1, HALF_2 = RE // 2, (ROWS - RE) // 2


def rcopy(src, dst, send_sem, recv_sem, dev):
    return pltpu.make_async_remote_copy(
        src_ref=src, dst_ref=dst, send_sem=send_sem, recv_sem=recv_sem,
        device_id=dev, device_id_type=MESH)


def kernel(res_hbm, heads_hbm, op_hbm, gain_ref, gate_hbm, up_hbm, down_hbm, idst_ref, slots_ref,
           table_ref, out_ref,
           res_v, heads_v, op_in, merged, w4, dn, sel, gsum, g_hi, g_lo, b_snd, b_rcv, b_tot, y_snd, y_rcv,
           t_snd, t_rcv, stream, dsp, xg, acc, sq, hid, e0, e1, e0_snd, e0_rcv, e1_snd, e1_rcv, ey_snd, ey_rcv,
           ez_snd, ez_rcv, ret_snd, ret_v,
           loc, w_s, w_r, h_s, h_r, hf_s, hf_r, op_s, op_r, b_s, b_r, yt_s, yt_r, g_s, g_r,
           c_s, c_r, ag_s, ag_r, agy_s, agy_r, e_s, e_r, ex_s, ex_r, ey_s, ey_r, f_s, f_r):
    b = lax.axis_index("branch")
    e = lax.axis_index("expert")
    z = e // 4
    yh = (e // 2) % 2
    c = e % 2
    half = b // 4
    sib = (b, e + 1 - 2 * c)
    right = (b, ((z + 1) % NZ) * 4 + yh * 2 + c)
    left = (b, ((z + NZ - 1) % NZ) * 4 + yh * 2 + c)
    ypart = (b, z * 4 + (1 - yh) * 2 + c)
    grp = (z + b) % NB
    tpart = (grp, b * 4 + c * 2 + yh)
    tsrc = (z, ((b + NZ - z) % NZ) * 4 + c * 2 + yh)
    t_self = (b == 0) & (z == 0) & (yh == c)
    dirs = (right, left)

    def chip_dev(j, core):
        return (j, z * 4 + yh * 2 + core)

    def op_cols(j, core, t):
        first = (j * 2 + core) * CW + (1 - yh if t == 0 else yh) * FW
        return pl.ds(pl.multiple_of(first, FW), FW)

    loads = [
        pltpu.make_async_copy(res_hbm, res_v, loc.at[0]),
        pltpu.make_async_copy(
            heads_hbm,
            heads_v.at[pl.ds(pl.multiple_of(b * TOK, TOK), TOK), pl.ds(pl.multiple_of(c * FW, FW), FW)],
            loc.at[1]),
        pltpu.make_async_copy(op_hbm.at[:, op_cols(b, c, 0)], op_in.at[0, b * 2 + c], loc.at[2]),
        pltpu.make_async_copy(op_hbm.at[:, op_cols(b, c, 1)], op_in.at[1, b * 2 + c], loc.at[8]),
        pltpu.make_async_copy(gate_hbm, w4.at[0], loc.at[3]),
        pltpu.make_async_copy(up_hbm, w4.at[2], loc.at[4]),
        pltpu.make_async_copy(down_hbm, dn.at[0], loc.at[5]),
    ]
    for ld in loads:
        ld.start()

    barrier = pltpu.get_barrier_semaphore()
    for kb in range(NB):
        for kc in range(2):
            if kb or kc:
                pl.semaphore_signal(barrier, inc=1, device_id=chip_dev((b + kb) % NB, (c + kc) % 2),
                                    device_id_type=MESH)
    for dev in (right, left, ypart):
        pl.semaphore_signal(barrier, inc=1, device_id=dev, device_id_type=MESH)

    @pl.when(jnp.logical_not(t_self))
    def _():
        pl.semaphore_signal(barrier, inc=1, device_id=tsrc, device_id_type=MESH)

    pl.semaphore_wait(barrier, jnp.where(t_self, 18, 19))

    pend = []
    my_heads = heads_v.at[pl.ds(pl.multiple_of(b * TOK, TOK), TOK), pl.ds(pl.multiple_of(c * FW, FW), FW)]
    for k in range(1, NB):
        cp = rcopy(heads_hbm, my_heads, h_s.at[k - 1], h_r.at[k - 1], chip_dev((b + k) % NB, c))
        cp.start()
        pend.append(cp)
    for t in range(2):
        for kb in range(NB):
            for kc in range(2):
                if kb or kc:
                    j, cc = (b + kb) % NB, (c + kc) % 2
                    cp = rcopy(op_hbm.at[:, op_cols(j, cc, t)], op_in.at[t, b * 2 + c],
                               op_s.at[t, kb * 2 + kc], op_r.at[t, kb * 2 + kc], chip_dev(j, cc))
                    cp.start()
                    pend.append(cp)
    for i, (src, dst) in enumerate(((gate_hbm, w4.at[1]), (up_hbm, w4.at[3]), (down_hbm, dn.at[1]))):
        cp = rcopy(src, dst, w_s.at[i], w_r.at[i], sib)
        cp.start()
        pend.append(cp)

    me = z * 2 + yh
    gain_at = (me, pl.ds(ROWS, GROWS), pl.ds(pl.multiple_of(c * FW, FW), FW))
    xg[gain_at] = jnp.broadcast_to(gain_ref[...], (GROWS, FW))
    gain_cp = rcopy(xg.at[gain_at], xg.at[gain_at], g_s, g_r, sib)
    gain_cp.start()
    pend.append(gain_cp)

    ids = idst_ref[...]
    xi = lax.broadcasted_iota(jnp.int32, (16, TOK), 0)
    named = ((ids[0:1] == xi) | (ids[1:2] == xi)).astype(BF16)
    before = (lax.broadcasted_iota(jnp.int32, (TOK, TOK), 0)
              < lax.broadcasted_iota(jnp.int32, (TOK, TOK), 1)).astype(BF16)
    rank = jnp.dot(named, before, preferred_element_type=F32).astype(jnp.int32)
    ci = lax.broadcasted_iota(jnp.int32, (CAP, TOK), 0)
    eye = lax.broadcasted_iota(jnp.int32, (SLOTS, SLOTS), 0) == lax.broadcasted_iota(jnp.int32, (SLOTS, SLOTS), 1)
    table = jnp.sum(jnp.where(eye, table_ref[...], 0.0), axis=1, keepdims=True)
    slot_i = lax.broadcasted_iota(jnp.int32, (SLOTS, TOK), 0)
    raw = [jnp.sum(jnp.where(slots_ref[k:k + 1] == slot_i, table, 0.0), axis=0, keepdims=True) for k in range(2)]
    gates = [raw[k] / (raw[0] + raw[1]) for k in range(2)]
    for x in range(NB):
        hit = rank[x:x + 1] == ci
        first, second = hit & (ids[0:1] == x), hit & (ids[1:2] == x)
        sel[x * CAP:(x + 1) * CAP] = (first | second).astype(BF16)
        gsum[x * CAP:(x + 1) * CAP] = jnp.where(first, gates[0], 0.0) + jnp.where(second, gates[1], 0.0)
    gt = gsum[...].T
    hi = gt.astype(BF16)
    g_hi[...] = hi
    g_lo[...] = (gt - hi.astype(F32)).astype(BF16)
    acc[...] = jnp.zeros_like(acc)
    sq[...] = jnp.zeros_like(sq)

    loads[1].wait()
    for k in range(1, NB):
        src_b = (b + NB - k) % NB
        rcopy(heads_hbm,
              heads_v.at[pl.ds(pl.multiple_of(src_b * TOK, TOK), TOK), pl.ds(pl.multiple_of(c * FW, FW), FW)],
              h_s.at[k - 1], h_r.at[k - 1], sib).wait_recv()
    mine_cols = heads_v.at[:, pl.ds(pl.multiple_of(c * FW, FW), FW)]
    their_cols = heads_v.at[:, pl.ds(pl.multiple_of((1 - c) * FW, FW), FW)]
    cp = rcopy(mine_cols, mine_cols, hf_s, hf_r, sib)
    cp.start()
    pend.append(cp)

    def merge(t):
        loads[2 + t].wait()
        for kb in range(NB):
            for kc in range(2):
                if kb or kc:
                    rcopy(op_hbm.at[:, pl.ds(0, FW)], op_in.at[t, ((b + NB - kb) % NB) * 2 + (c + kc) % 2],
                          op_s.at[t, kb * 2 + kc], op_r.at[t, kb * 2 + kc], sib).wait_recv()
        for cc in range(2):
            total = op_in[t, cc].astype(F32)
            for j in range(1, NB):
                total = total + op_in[t, j * 2 + cc].astype(F32)
            merged[t, cc * FW:(cc + 1) * FW] = (total / NB).astype(BF16)

    def attn_part(zd, t):
        g = (zd + b) % NB
        return jnp.dot(heads_v[pl.ds(pl.multiple_of(g * TOK, TOK), TOK), :], merged[t],
                       preferred_element_type=F32)

    def b_rows(d, u):
        return pl.ds(((d + u) % 2) * 128, 128)

    def b_copy(d, t, s, u):
        rows = b_rows(d, u)
        return rcopy(b_snd.at[d, t, s, rows], b_rcv.at[d, t, s, rows], b_s.at[d, t, s, u], b_r.at[d, t, s, u],
                     dirs[d])

    def start(cp):
        cp.start()
        pend.append(cp)

    def b_first(t):
        p = attn_part((z + 4) % NZ, t)
        for d in range(2):
            b_snd[d, t, 0, b_rows(d, 0)] = p[d * 128:(d + 1) * 128].astype(BF16)
            start(b_copy(d, t, 0, 0))

    def b_step(t, s):
        for d in range(2):
            b_tot[d] = attn_part((z + (4 - s)) % NZ if d == 0 else (z + NZ - (4 - s)) % NZ, t)
        for u in range(2):
            for d in range(2):
                rows = b_rows(d, u)
                if s > 1 or u == 0:
                    b_copy(d, t, s - 1, u).wait_recv()
                    b_snd[d, t, s, rows] = (b_tot[d, rows] + b_rcv[d, t, s - 1, rows].astype(F32)).astype(BF16)
                else:
                    b_snd[d, t, s, rows] = b_tot[d, rows].astype(BF16)
                start(b_copy(d, t, s, u))

    def b_last(t):
        b_tot[0] = attn_part(z, t)
        for u in range(2):
            for d in range(2):
                b_copy(d, t, 3, u).wait_recv()
        return b_tot[0] + b_rcv[0, t, 3].astype(F32) + b_rcv[1, t, 3].astype(F32)

    merge(0)
    rcopy(their_cols, their_cols, hf_s, hf_r, sib).wait_recv()
    b_first(0)
    b_step(0, 1)
    b_step(0, 2)
    merge(1)
    b_first(1)
    b_step(0, 3)
    b_step(1, 1)
    y_snd[...] = b_last(0).astype(BF16)
    y_copy = rcopy(y_snd, y_rcv, yt_s.at[0], yt_r.at[0], ypart)
    start(y_copy)
    b_step(1, 2)
    b_step(1, 3)
    kept = b_last(1)
    y_copy.wait_recv()
    t_snd[...] = (kept + y_rcv[...].astype(F32)).astype(BF16)
    t_copy = rcopy(t_snd, t_rcv, yt_s.at[1], yt_r.at[1], tpart)

    @pl.when(t_self)
    def _():
        t_rcv[...] = t_snd[...]

    @pl.when(jnp.logical_not(t_self))
    def _():
        t_copy.start()
        t_copy.wait_recv()

    loads[0].wait()
    st = res_v[...].astype(F32) + t_rcv[...].astype(F32)
    stream[...] = st
    scaled = (st * gain_ref[...].astype(F32)).astype(BF16)
    dsp[...] = jnp.dot(sel[...], scaled, preferred_element_type=F32).astype(BF16)
    blk_at = (me, pl.ds(pl.multiple_of((b % 4) * CAP, CAP), CAP), pl.ds(pl.multiple_of(c * FW, FW), FW))
    my_src = half == c

    def c_copy(k):
        x = (b + k) % NB
        return rcopy(dsp.at[pl.ds(pl.multiple_of(x * CAP, CAP), CAP)], xg.at[blk_at], c_s.at[k],
                     c_r.at[(b % 4) * 2 + c], chip_dev(x, half))

    own_blk = pltpu.make_async_copy(dsp.at[pl.ds(pl.multiple_of(b * CAP, CAP), CAP)], xg.at[blk_at], loc.at[6])
    for k in range(1, NB):
        c_copy(k).start()
        pend.append(c_copy(k))

    @pl.when(my_src)
    def _():
        own_blk.start()

    @pl.when(jnp.logical_not(my_src))
    def _():
        c_copy(0).start()

    for i in range(8):
        @pl.when(jnp.logical_not(jnp.logical_and(my_src, (b % 4) * 2 + c == i)))
        def _(i=i):
            rcopy(dsp.at[pl.ds(0, CAP)], xg.at[me, pl.ds((i // 2) * CAP, CAP), pl.ds((i % 2) * FW, FW)],
                  c_s.at[0], c_r.at[i], sib).wait_recv()

    @pl.when(my_src)
    def _():
        own_blk.wait()

    sib_gain = xg.at[me, pl.ds(ROWS, GROWS), pl.ds(pl.multiple_of((1 - c) * FW, FW), FW)]
    rcopy(sib_gain, sib_gain, g_s, g_r, sib).wait_recv()

    def ag_copy(d, t, s, slot):
        lo, n = (RD, BLK - RD) if t == 0 else (0, RD)
        if s == 3:
            cut = n // 32 * 16
            lo, n = (lo, cut) if d == 0 else (lo + cut, n - cut)
        ref = xg.at[slot, pl.ds(lo, n)]
        return rcopy(ref, ref, ag_s.at[d, t, s], ag_r.at[d, t, s], dirs[d])

    def agy_copy(i, slot):
        if i == 0:
            lo, n = 0, RD
        elif i < 8:
            lo, n = RD, BLK - RD
        else:
            cut = (BLK - RD) // 32 * 16
            lo, n = (RD, cut) if i == 8 else (RD + cut, BLK - RD - cut)
        ref = xg.at[slot, pl.ds(lo, n)]
        return rcopy(ref, ref, agy_s.at[i], agy_r.at[i], ypart)

    def gate_up(slot):
        blk = xg[slot, 0:ROWS]
        inv = 1.0 / xg[slot, ROWS:BLK][0:1].astype(F32)
        v = blk.astype(F32) * inv
        sq[...] += v * v
        rows = pl.ds(pl.multiple_of(slot * CW, CW), CW)

        def part(i, carry):
            acc[i] += jnp.dot(xg[slot, 0:ROWS], w4[i, rows, :], preferred_element_type=F32)
            return carry
        lax.fori_loop(0, 4, part, 0)

    def slot_of(d, s, t):
        return ((z + NZ - s) % NZ if d == 0 else (z + s) % NZ) * 2 + (yh if t == 0 else 1 - yh)

    other = z * 2 + 1 - yh
    start(agy_copy(0, me))
    for t in range(2):
        for d in range(2):
            start(ag_copy(d, t, 0, me))
        if t == 0:
            start(agy_copy(1, me))
    loads[4].wait()
    loads[5].wait()
    for i in range(2):
        rcopy(gate_hbm, w4.at[1 + 2 * i], w_s.at[i], w_r.at[i], sib).wait_recv()
    gate_up(me)
    agy_copy(0, other).wait_recv()
    for d in range(2):
        start(ag_copy(d, 2, 0, other))
    for s in range(1, 4):
        for t in range(2):
            for d in range(2):
                slot = slot_of(d, s, 0)
                ag_copy(d, t, s - 1, slot).wait_recv()
                start(ag_copy(d, t, s, slot))
                if t == 0:
                    start(agy_copy(2 * s + d, slot))
        gate_up(slot_of(0, s, 0))
        for d in range(2):
            slot = slot_of(d, s, 1)
            ag_copy(d, 2, s - 1, slot).wait_recv()
            start(ag_copy(d, 2, s, slot))
        gate_up(slot_of(1, s, 0))
        if s == 1:
            agy_copy(1, other).wait_recv()
            gate_up(other)
        else:
            for d in range(2):
                slot = slot_of(d, s - 1, 1)
                agy_copy(2 * (s - 1) + d, slot).wait_recv()
                gate_up(slot)
    far = slot_of(0, 4, 0)
    for d in range(2):
        ag_copy(d, 0, 3, far).wait_recv()
        start(agy_copy(8 + d, far))
    for d in range(2):
        ag_copy(d, 1, 3, far).wait_recv()
    gate_up(far)
    for d in range(2):
        slot = slot_of(d, 3, 1)
        agy_copy(6 + d, slot).wait_recv()
        gate_up(slot)
    far = slot_of(0, 4, 1)
    for d in range(2):
        ag_copy(d, 2, 3, far).wait_recv()
        agy_copy(8 + d, far).wait_recv()
    gate_up(far)

    scale = lax.rsqrt(jnp.sum(sq[...], axis=1, keepdims=True) / D + 1e-05)
    for i in range(2):
        g = acc[i] * scale
        hid[i] = (g / (1.0 + jnp.exp(-g)) * (acc[2 + i] * scale)).astype(BF16)
    loads[6].wait()
    rcopy(down_hbm, dn.at[1], w_s.at[2], w_r.at[2], sib).wait_recv()

    def down_part(zd, t):
        yy = 1 - yh if t == 0 else yh
        cols = pl.ds(pl.multiple_of((zd * 2 + yy) * CW, CW), CW)
        return (jnp.dot(hid[0], dn[0, :, cols], preferred_element_type=F32)
                + jnp.dot(hid[1], dn[1, :, cols], preferred_element_type=F32))

    def target(k):
        if k == 0:
            return (z + 4) % NZ
        dist = 4 - (k + 1) // 2
        return (z + dist) % NZ if k % 2 else (z + NZ - dist) % NZ

    def ey_copy(k):
        return rcopy(ey_snd.at[k], ey_rcv.at[k], ey_s.at[k], ey_r.at[k], ypart)

    def e0_copy(d, s):
        rows = pl.ds(d * HALF_1, HALF_1) if s == 0 else pl.ds(0, RE)
        return rcopy(e0_snd.at[d, s, rows], e0_rcv.at[d, s, rows], e_s.at[d, 0, s], e_r.at[d, 0, s], dirs[d])

    def e1_copy(d, t, s):
        lo, n = (0, RE) if t == 1 else (RE, ROWS - RE)
        rows = pl.ds(lo + d * (n // 2), n // 2) if s == 0 else pl.ds(lo, n)
        return rcopy(e1_snd.at[d, s, rows], e1_rcv.at[d, s, rows], e_s.at[d, t, s], e_r.at[d, t, s], dirs[d])

    def other_part(k):
        p = down_part(target(k), 0)
        ey_snd[k] = p[RE:ROWS].astype(BF16)
        start(ey_copy(k))
        e0[k] = p[0:RE]

    other_part(0)
    for d in range(2):
        rows = slice(d * HALF_1, (d + 1) * HALF_1)
        e0_snd[d, 0, rows] = e0[0, rows].astype(BF16)
        start(e0_copy(d, 0))
    e1[0] = down_part(target(0), 1)
    for d in range(2):
        rows = slice(d * HALF_1, (d + 1) * HALF_1)
        e1_snd[d, 0, rows] = e1[0, rows].astype(BF16)
        start(e1_copy(d, 1, 0))
    other_part(1)
    other_part(2)
    ey_copy(0).wait_recv()
    for d in range(2):
        rows = slice(RE + d * HALF_2, RE + (d + 1) * HALF_2)
        e1_snd[d, 0, rows] = (e1[0, rows] + ey_rcv[0, d * HALF_2:(d + 1) * HALF_2].astype(F32)).astype(BF16)
        start(e1_copy(d, 2, 0))
    for s in range(1, 4):
        for d in range(2):
            e1[d] = down_part(target(2 * s - 1 + d), 1)
        for d in range(2):
            k = 2 * s - 1 + d
            e0_copy(d, s - 1).wait_recv()
            if s == 1:
                rows = slice(d * HALF_1, (d + 1) * HALF_1)
                rest = slice((1 - d) * HALF_1, (2 - d) * HALF_1)
                e0_snd[d, s, rows] = (e0[k, rows] + e0_rcv[d, 0, rows].astype(F32)).astype(BF16)
                e0_snd[d, s, rest] = e0[k, rest].astype(BF16)
            else:
                e0_snd[d, s] = (e0[k] + e0_rcv[d, s - 1].astype(F32)).astype(BF16)
            start(e0_copy(d, s))
        for t, lo, n in ((1, 0, RE), (2, RE, ROWS - RE)):
            for d in range(2):
                if t == 2:
                    k = 2 * s - 1 + d
                    ey_copy(k).wait_recv()
                    e1[d, RE:ROWS] += ey_rcv[k].astype(F32)
                e1_copy(d, t, s - 1).wait_recv()
                if s == 1:
                    rows = slice(lo + d * (n // 2), lo + (d + 1) * (n // 2))
                    rest = slice(lo + (1 - d) * (n // 2), lo + (2 - d) * (n // 2))
                    e1_snd[d, s, rows] = (e1[d, rows] + e1_rcv[d, 0, rows].astype(F32)).astype(BF16)
                    e1_snd[d, s, rest] = e1[d, rest].astype(BF16)
                else:
                    rows = slice(lo, lo + n)
                    e1_snd[d, s, rows] = (e1[d, rows] + e1_rcv[d, s - 1, rows].astype(F32)).astype(BF16)
                start(e1_copy(d, t, s))
            if t == 1:
                for d in range(2):
                    if 2 * s + 1 + d < NZ:
                        other_part(2 * s + 1 + d)
    e1[0] = down_part(z, 1)
    for d in range(2):
        e0_copy(d, 3).wait_recv()
    ez_snd[...] = (e0[7] + e0_rcv[0, 3].astype(F32) + e0_rcv[1, 3].astype(F32)).astype(BF16)
    ez = rcopy(ez_snd, ez_rcv, ex_s, ex_r, ypart)
    start(ez)
    ey_copy(7).wait_recv()
    e1[0, RE:ROWS] += ey_rcv[7].astype(F32)
    for t in (1, 2):
        for d in range(2):
            e1_copy(d, t, 3).wait_recv()
    e1[0] = e1[0] + e1_rcv[0, 3].astype(F32) + e1_rcv[1, 3].astype(F32)

    def f_copy(i, cc):
        return rcopy(ret_snd.at[pl.ds(i * CAP, CAP), pl.ds(cc * FW, FW)],
                     ret_v.at[pl.ds(pl.multiple_of(b * CAP, CAP), CAP)],
                     f_s.at[i * 2 + cc], f_r.at[b], chip_dev(4 * c + i, cc))

    for i in (2, 3, 0, 1):
        rows = slice(i * CAP, (i + 1) * CAP)
        if i == 0:
            ez.wait_recv()
            e1[0, 0:RE] += ez_rcv[...].astype(F32)
        ret_snd[rows] = e1[0, rows].astype(BF16)
        for cc in range(2):
            to_self = jnp.logical_and(4 * c + i == b, cc == c)
            mine = pltpu.make_async_copy(ret_snd.at[pl.ds(i * CAP, CAP), pl.ds(cc * FW, FW)],
                                         ret_v.at[pl.ds(pl.multiple_of(b * CAP, CAP), CAP)], loc.at[7])

            @pl.when(to_self)
            def _(mine=mine):
                mine.start()
                mine.wait()

            @pl.when(jnp.logical_not(to_self))
            def _(i=i, cc=cc):
                f_copy(i, cc).start()

    for x in range(NB):
        @pl.when(jnp.logical_not(jnp.logical_and(my_src, b == x)))
        def _(x=x):
            rcopy(ret_snd.at[pl.ds(0, CAP), pl.ds(0, FW)], ret_v.at[pl.ds(x * CAP, CAP)], f_s.at[0], f_r.at[x],
                  sib).wait_recv()
    out_ref[...] = (stream[...] + jnp.dot(g_hi[...], ret_v[...], preferred_element_type=F32)
                    + jnp.dot(g_lo[...], ret_v[...], preferred_element_type=F32)).astype(BF16)

    for cp in pend:
        cp.wait_send()

    @pl.when(jnp.logical_not(t_self))
    def _():
        t_copy.wait_send()

    @pl.when(jnp.logical_not(my_src))
    def _():
        c_copy(0).wait_send()

    for i in range(4):
        for cc in range(2):
            @pl.when(jnp.logical_not(jnp.logical_and(4 * c + i == b, cc == c)))
            def _(i=i, cc=cc):
                f_copy(i, cc).wait_send()


def per_device(residual, heads_out, out_proj, norm_gain, gate_w, up_w, down_w, expert_ids, gate_slots, gate_table):
    any_, vmem = pl.BlockSpec(memory_space=pl.ANY), pl.BlockSpec(memory_space=pltpu.VMEM)
    dma, v = pltpu.SemaphoreType.DMA, pltpu.VMEM
    return pl.pallas_call(
        kernel,
        out_shape=jax.ShapeDtypeStruct((TOK, FW), BF16),
        in_specs=[any_, any_, any_, vmem, any_, any_, any_, vmem, vmem, vmem],
        out_specs=vmem,
        scratch_shapes=[
            v((TOK, FW), BF16), v((NB * TOK, CW), BF16), v((2, 16, FW, FW), BF16), v((2, CW, FW), BF16),
            v((4, D, CW), BF16), v((2, CW, D), BF16), v((NB * CAP, TOK), BF16), v((NB * CAP, TOK), F32),
            v((TOK, NB * CAP), BF16), v((TOK, NB * CAP), BF16),
            v((2, 2, 4, TOK, FW), BF16), v((2, 2, 4, TOK, FW), BF16), v((2, TOK, FW), F32),
            v((TOK, FW), BF16), v((TOK, FW), BF16), v((TOK, FW), BF16), v((TOK, FW), BF16),
            v((TOK, FW), F32), v((NB * CAP, FW), BF16), v((16, BLK, CW), BF16), v((4, ROWS, CW), F32),
            v((ROWS, CW), F32), v((2, ROWS, CW), BF16), v((NZ, RE, CW), F32), v((2, ROWS, CW), F32),
            v((2, 4, RE, CW), BF16), v((2, 4, RE, CW), BF16), v((2, 4, ROWS, CW), BF16), v((2, 4, ROWS, CW), BF16),
            v((NZ, ROWS - RE, CW), BF16), v((NZ, ROWS - RE, CW), BF16), v((RE, CW), BF16), v((RE, CW), BF16),
            v((ROWS, CW), BF16), v((NB * CAP, FW), BF16),
            dma((9,)), dma((3,)), dma((3,)), dma((7,)), dma((7,)), dma, dma, dma((2, 16)), dma((2, 16)),
            dma((2, 2, 4, 2)), dma((2, 2, 4, 2)), dma((2,)), dma((2,)), dma, dma,
            dma((8,)), dma((8,)), dma((2, 3, 4)), dma((2, 3, 4)), dma((10,)), dma((10,)),
            dma((2, 3, 4)), dma((2, 3, 4)), dma, dma, dma((8,)), dma((8,)), dma((8,)), dma((8,)),
        ],
        compiler_params=pltpu.CompilerParams(
            collective_id=0, has_side_effects=True, vmem_limit_bytes=60 * 1024 * 1024),
        name="merge_moe",
    )(residual, heads_out, out_proj[0], norm_gain.reshape(1, FW), gate_w[0], up_w[0], down_w[0],
      expert_ids.T, gate_slots.T, gate_table.reshape(1, SLOTS))


def solution(mesh):
    return jax.shard_map(
        per_device,
        mesh=mesh,
        in_specs=(
            P("branch", "expert"), P("branch", "expert"), P("branch", "expert", None), P("expert"),
            P("branch", None, "expert"), P("branch", None, "expert"), P("branch", "expert", None),
            P("branch", None), P("branch", None), P(),
        ),
        out_specs=P("branch", "expert"),
        check_vma=False,
    )
```

```python
import jax
import jax.numpy as jnp
from jax import lax
from jax.experimental import pallas as pl
from jax.experimental.pallas import tpu as pltpu
from jax.sharding import PartitionSpec as P

MESH = pl.DeviceIdType.MESH
F32, BF16 = jnp.float32, jnp.bfloat16
D = 4096
SLOTS = 64
NB = 8
NZ = 8
TOK = 256
CAP = 96
ROWS = 4 * CAP
GROWS = 16
BLK = ROWS + GROWS
FW = 128
CW = 256
KR = 16
GROUPS = ((0, 3), (3, 2), (5, 2), (7, 1))
RD = 176
RE = 160
HALF_1, HALF_2 = RE // 2, (ROWS - RE) // 2


def rcopy(src, dst, send_sem, recv_sem, dev):
    return pltpu.make_async_remote_copy(
        src_ref=src, dst_ref=dst, send_sem=send_sem, recv_sem=recv_sem,
        device_id=dev, device_id_type=MESH)


def kernel(res_hbm, heads_hbm, op_hbm, gain_ref, gate_hbm, up_hbm, down_hbm, idst_ref, slots_ref,
           table_ref, out_ref,
           res_v, heads_v, op_v, op_x, op_in, mg, merged, w4, dn, sel, gsum, g_hi, g_lo, b_snd, b_rcv, b_tot,
           x_snd, x_rcv, stream, dsp, xg, acc, sq, hid, e0, e1, e0_snd, e0_rcv, e1_snd, e1_rcv, ey_snd, ey_rcv,
           ez_snd, ez_rcv, ret_snd, ret_v,
           loc, w_s, w_r, h_s, h_r, op_s, op_r, mg_s, mg_r, b_s, b_r, x_s, x_r, g_s, g_r,
           c_s, c_r, ag_s, ag_r, agy_s, agy_r, e_s, e_r, ex_s, ex_r, ey_s, ey_r, f_s, f_r):
    b = lax.axis_index("branch")
    e = lax.axis_index("expert")
    z = e // 4
    yh = (e // 2) % 2
    c = e % 2
    half = b // 4
    sib = (b, e + 1 - 2 * c)
    right = (b, ((z + 1) % NZ) * 4 + yh * 2 + c)
    left = (b, ((z + NZ - 1) % NZ) * 4 + yh * 2 + c)
    ypart = (b, z * 4 + (1 - yh) * 2 + c)
    ydiag = (b, z * 4 + (1 - yh) * 2 + 1 - c)
    dirs = (right, left)

    def chip_dev(j, core):
        return (j, z * 4 + yh * 2 + core)

    def target(k):
        if k == 0:
            return (z + 4) % NZ
        if k == NZ - 1:
            return z
        dist = 4 - (k + 1) // 2
        return (z + dist) % NZ if k % 2 else (z + NZ - dist) % NZ

    my_cols = pl.ds(pl.multiple_of(c * FW, FW), FW)
    loads = [
        pltpu.make_async_copy(op_hbm, op_v, loc.at[2]),
        pltpu.make_async_copy(heads_hbm, heads_v.at[:, my_cols], loc.at[1]),
        pltpu.make_async_copy(res_hbm, res_v, loc.at[0]),
        pltpu.make_async_copy(gate_hbm, w4.at[0], loc.at[3]),
        pltpu.make_async_copy(up_hbm, w4.at[2], loc.at[4]),
        pltpu.make_async_copy(down_hbm, dn.at[0], loc.at[5]),
    ]
    for ld in loads:
        ld.start()

    barrier = pltpu.get_barrier_semaphore()
    for kb in range(NB):
        for kc in range(2):
            if kb or kc:
                pl.semaphore_signal(barrier, inc=1, device_id=chip_dev((b + kb) % NB, (c + kc) % 2),
                                    device_id_type=MESH)
    for dev in (right, left, ypart, ydiag):
        pl.semaphore_signal(barrier, inc=1, device_id=dev, device_id_type=MESH)

    loads[0].wait()
    for k in range(NZ):
        for cc in range(2):
            cols = pl.ds(pl.multiple_of(target(k) * 2 * CW + cc * CW, CW), CW)
            op_x[:, cc, k] = op_v[:, cols].reshape(NB, KR, CW)
    op_in[b * 2 + c] = op_x[b, c]
    pl.semaphore_wait(barrier, 19)

    pend = []

    def start(cp):
        cp.start()
        pend.append(cp)

    def op_send(i):
        q, n = GROUPS[i]
        for kb in range(NB):
            for kc in range(2):
                if kb or kc:
                    j, cc = (b + kb) % NB, (c + kc) % 2
                    start(rcopy(op_x.at[j, cc, pl.ds(q, n)], op_in.at[b * 2 + c, pl.ds(q, n)],
                                op_s.at[i, kb * 2 + kc], op_r.at[i, kb * 2 + kc], chip_dev(j, cc)))

    def mg_copy(i, k, j):
        q, n = GROUPS[i]
        return rcopy(mg.at[pl.ds(q, n)], merged.at[pl.ds(q, n), :, pl.ds(pl.multiple_of(j * KR, KR), KR)],
                     mg_s.at[i, k - 1], mg_r.at[i, k - 1], chip_dev((b + k) % NB, c))

    def merge(i):
        q, n = GROUPS[i]
        for kb in range(NB):
            for kc in range(2):
                if kb or kc:
                    rcopy(op_x.at[0, 0, pl.ds(q, n)],
                          op_in.at[((b + NB - kb) % NB) * 2 + (c + kc) % 2, pl.ds(q, n)],
                          op_s.at[i, kb * 2 + kc], op_r.at[i, kb * 2 + kc], sib).wait_recv()
        for k in range(q, q + n):
            for cc in range(2):
                total = op_in[cc, k].astype(F32)
                for j in range(1, NB):
                    total = total + op_in[j * 2 + cc, k].astype(F32)
                total = (total / NB).astype(BF16)
                mg[k, cc] = total
                merged[k, cc, pl.ds(pl.multiple_of(b * KR, KR), KR)] = total
        for k in range(1, NB):
            start(mg_copy(i, k, b))

    def merged_wait(i):
        for k in range(1, NB):
            mg_copy(i, k, (b + NB - k) % NB).wait_recv()

    op_send(0)
    start(rcopy(heads_hbm, heads_v.at[:, my_cols], h_s, h_r, sib))
    op_send(1)
    for i, (src, dst) in enumerate(((gate_hbm, w4.at[1]), (up_hbm, w4.at[3]), (down_hbm, dn.at[1]))):
        cp = rcopy(src, dst, w_s.at[i], w_r.at[i], sib)
        cp.start()
        pend.append(cp)

    me = z * 2 + yh
    gain_at = (me, pl.ds(ROWS, GROWS), pl.ds(pl.multiple_of(c * FW, FW), FW))
    xg[gain_at] = jnp.broadcast_to(gain_ref[...], (GROWS, FW))
    gain_cp = rcopy(xg.at[gain_at], xg.at[gain_at], g_s, g_r, sib)
    gain_cp.start()
    pend.append(gain_cp)

    ids = idst_ref[...]
    xi = lax.broadcasted_iota(jnp.int32, (16, TOK), 0)
    named = ((ids[0:1] == xi) | (ids[1:2] == xi)).astype(BF16)
    before = (lax.broadcasted_iota(jnp.int32, (TOK, TOK), 0)
              < lax.broadcasted_iota(jnp.int32, (TOK, TOK), 1)).astype(BF16)
    rank = jnp.dot(named, before, preferred_element_type=F32).astype(jnp.int32)
    ci = lax.broadcasted_iota(jnp.int32, (CAP, TOK), 0)
    eye = lax.broadcasted_iota(jnp.int32, (SLOTS, SLOTS), 0) == lax.broadcasted_iota(jnp.int32, (SLOTS, SLOTS), 1)
    table = jnp.sum(jnp.where(eye, table_ref[...], 0.0), axis=1, keepdims=True)
    slot_i = lax.broadcasted_iota(jnp.int32, (SLOTS, TOK), 0)
    raw = [jnp.sum(jnp.where(slots_ref[k:k + 1] == slot_i, table, 0.0), axis=0, keepdims=True) for k in range(2)]
    gates = [raw[k] / (raw[0] + raw[1]) for k in range(2)]
    for x in range(NB):
        hit = rank[x:x + 1] == ci
        first, second = hit & (ids[0:1] == x), hit & (ids[1:2] == x)
        sel[x * CAP:(x + 1) * CAP] = (first | second).astype(BF16)
        gsum[x * CAP:(x + 1) * CAP] = jnp.where(first, gates[0], 0.0) + jnp.where(second, gates[1], 0.0)
    gt = gsum[...].T
    hi = gt.astype(BF16)
    g_hi[...] = hi
    g_lo[...] = (gt - hi.astype(F32)).astype(BF16)
    acc[...] = jnp.zeros_like(acc)
    sq[...] = jnp.zeros_like(sq)

    def attn_part(k):
        return jnp.dot(heads_v[...], merged[k].reshape(CW, CW), preferred_element_type=F32)

    def b_rows(d, u):
        return pl.ds(((d + u) % 2) * 128, 128)

    def b_copy(d, s, u):
        rows = b_rows(d, u)
        return rcopy(b_snd.at[d, s, rows], b_rcv.at[d, s, rows], b_s.at[d, s, u], b_r.at[d, s, u], dirs[d])

    def b_step(s):
        for d in range(2):
            b_tot[d] = attn_part(2 * s - 1 + d)
        for u in range(2):
            for d in range(2):
                rows = b_rows(d, u)
                if s > 1 or u == 0:
                    b_copy(d, s - 1, u).wait_recv()
                    b_snd[d, s, rows] = (b_tot[d, rows] + b_rcv[d, s - 1, rows].astype(F32)).astype(BF16)
                else:
                    b_snd[d, s, rows] = b_tot[d, rows].astype(BF16)
                start(b_copy(d, s, u))

    merge(0)
    op_send(2)
    merge(1)
    op_send(3)
    loads[1].wait()
    their_cols = heads_v.at[:, pl.ds(pl.multiple_of((1 - c) * FW, FW), FW)]
    rcopy(their_cols, their_cols, h_s, h_r, sib).wait_recv()
    merged_wait(0)
    p = attn_part(0)
    for d in range(2):
        b_snd[d, 0, b_rows(d, 0)] = p[d * 128:(d + 1) * 128].astype(BF16)
        start(b_copy(d, 0, 0))
    merge(2)
    b_step(1)
    merge(3)
    merged_wait(1)
    b_step(2)
    merged_wait(2)
    b_step(3)
    merged_wait(3)
    b_tot[0] = attn_part(NZ - 1)
    for u in range(2):
        for d in range(2):
            b_copy(d, 3, u).wait_recv()
    x_snd[...] = (b_tot[0] + b_rcv[0, 3].astype(F32) + b_rcv[1, 3].astype(F32)).astype(BF16)

    def x_copy(w):
        return rcopy(x_snd.at[:, pl.ds(w * FW, FW)], x_rcv.at[jnp.where(yh == c, 0, 1)], x_s.at[w],
                     x_r.at[jnp.where(yh == c, 0, 1)], (b, z * 4 + c * 2 + w))

    for w in range(2):
        keep = (yh == c) & (c == w)

        @pl.when(keep)
        def _(w=w):
            x_rcv[0] = x_snd[:, w * FW:(w + 1) * FW]

        @pl.when(jnp.logical_not(keep))
        def _(w=w):
            x_copy(w).start()

    @pl.when(yh != c)
    def _():
        rcopy(x_rcv.at[0], x_rcv.at[0], x_s.at[0], x_r.at[0], sib).wait_recv()

    rcopy(x_rcv.at[1], x_rcv.at[1], x_s.at[0], x_r.at[1], sib).wait_recv()

    loads[2].wait()
    st = res_v[...].astype(F32) + (x_rcv[0].astype(F32) + x_rcv[1].astype(F32))
    stream[...] = st
    scaled = (st * gain_ref[...].astype(F32)).astype(BF16)
    dsp[...] = jnp.dot(sel[...], scaled, preferred_element_type=F32).astype(BF16)
    blk_at = (me, pl.ds(pl.multiple_of((b % 4) * CAP, CAP), CAP), pl.ds(pl.multiple_of(c * FW, FW), FW))
    my_src = half == c

    def c_copy(k):
        x = (b + k) % NB
        return rcopy(dsp.at[pl.ds(pl.multiple_of(x * CAP, CAP), CAP)], xg.at[blk_at], c_s.at[k],
                     c_r.at[(b % 4) * 2 + c], chip_dev(x, half))

    own_blk = pltpu.make_async_copy(dsp.at[pl.ds(pl.multiple_of(b * CAP, CAP), CAP)], xg.at[blk_at], loc.at[6])
    for k in range(1, NB):
        c_copy(k).start()
        pend.append(c_copy(k))

    @pl.when(my_src)
    def _():
        own_blk.start()

    @pl.when(jnp.logical_not(my_src))
    def _():
        c_copy(0).start()

    for i in range(8):
        @pl.when(jnp.logical_not(jnp.logical_and(my_src, (b % 4) * 2 + c == i)))
        def _(i=i):
            rcopy(dsp.at[pl.ds(0, CAP)], xg.at[me, pl.ds((i // 2) * CAP, CAP), pl.ds((i % 2) * FW, FW)],
                  c_s.at[0], c_r.at[i], sib).wait_recv()

    @pl.when(my_src)
    def _():
        own_blk.wait()

    sib_gain = xg.at[me, pl.ds(ROWS, GROWS), pl.ds(pl.multiple_of((1 - c) * FW, FW), FW)]
    rcopy(sib_gain, sib_gain, g_s, g_r, sib).wait_recv()

    def ag_copy(d, t, s, slot):
        lo, n = (RD, BLK - RD) if t == 0 else (0, RD)
        if s == 3:
            cut = n // 32 * 16
            lo, n = (lo, cut) if d == 0 else (lo + cut, n - cut)
        ref = xg.at[slot, pl.ds(lo, n)]
        return rcopy(ref, ref, ag_s.at[d, t, s], ag_r.at[d, t, s], dirs[d])

    def agy_copy(i, slot):
        if i == 0:
            lo, n = 0, RD
        elif i < 8:
            lo, n = RD, BLK - RD
        else:
            cut = (BLK - RD) // 32 * 16
            lo, n = (RD, cut) if i == 8 else (RD + cut, BLK - RD - cut)
        ref = xg.at[slot, pl.ds(lo, n)]
        return rcopy(ref, ref, agy_s.at[i], agy_r.at[i], ypart)

    def gate_up(slot):
        blk = xg[slot, 0:ROWS]
        inv = 1.0 / xg[slot, ROWS:BLK][0:1].astype(F32)
        v = blk.astype(F32) * inv
        sq[...] += v * v
        rows = pl.ds(pl.multiple_of(slot * CW, CW), CW)

        def part(i, carry):
            acc[i] += jnp.dot(xg[slot, 0:ROWS], w4[i, rows, :], preferred_element_type=F32)
            return carry
        lax.fori_loop(0, 4, part, 0)

    def slot_of(d, s, t):
        return ((z + NZ - s) % NZ if d == 0 else (z + s) % NZ) * 2 + (yh if t == 0 else 1 - yh)

    other = z * 2 + 1 - yh
    start(agy_copy(0, me))
    for t in range(2):
        for d in range(2):
            start(ag_copy(d, t, 0, me))
        if t == 0:
            start(agy_copy(1, me))
    loads[3].wait()
    loads[4].wait()
    for i in range(2):
        rcopy(gate_hbm, w4.at[1 + 2 * i], w_s.at[i], w_r.at[i], sib).wait_recv()
    gate_up(me)
    agy_copy(0, other).wait_recv()
    for d in range(2):
        start(ag_copy(d, 2, 0, other))
    for s in range(1, 4):
        for t in range(2):
            for d in range(2):
                slot = slot_of(d, s, 0)
                ag_copy(d, t, s - 1, slot).wait_recv()
                start(ag_copy(d, t, s, slot))
                if t == 0:
                    start(agy_copy(2 * s + d, slot))
        gate_up(slot_of(0, s, 0))
        for d in range(2):
            slot = slot_of(d, s, 1)
            ag_copy(d, 2, s - 1, slot).wait_recv()
            start(ag_copy(d, 2, s, slot))
        gate_up(slot_of(1, s, 0))
        if s == 1:
            agy_copy(1, other).wait_recv()
            gate_up(other)
        else:
            for d in range(2):
                slot = slot_of(d, s - 1, 1)
                agy_copy(2 * (s - 1) + d, slot).wait_recv()
                gate_up(slot)
    far = slot_of(0, 4, 0)
    for d in range(2):
        ag_copy(d, 0, 3, far).wait_recv()
        start(agy_copy(8 + d, far))
    for d in range(2):
        ag_copy(d, 1, 3, far).wait_recv()
    gate_up(far)
    for d in range(2):
        slot = slot_of(d, 3, 1)
        agy_copy(6 + d, slot).wait_recv()
        gate_up(slot)
    far = slot_of(0, 4, 1)
    for d in range(2):
        ag_copy(d, 2, 3, far).wait_recv()
        agy_copy(8 + d, far).wait_recv()
    gate_up(far)

    scale = lax.rsqrt(jnp.sum(sq[...], axis=1, keepdims=True) / D + 1e-05)
    for i in range(2):
        g = acc[i] * scale
        hid[i] = (g / (1.0 + jnp.exp(-g)) * (acc[2 + i] * scale)).astype(BF16)
    loads[5].wait()
    rcopy(down_hbm, dn.at[1], w_s.at[2], w_r.at[2], sib).wait_recv()

    def down_part(zd, t):
        yy = 1 - yh if t == 0 else yh
        cols = pl.ds(pl.multiple_of((zd * 2 + yy) * CW, CW), CW)
        return (jnp.dot(hid[0], dn[0, :, cols], preferred_element_type=F32)
                + jnp.dot(hid[1], dn[1, :, cols], preferred_element_type=F32))

    def ey_copy(k):
        return rcopy(ey_snd.at[k], ey_rcv.at[k], ey_s.at[k], ey_r.at[k], ypart)

    def e0_copy(d, s):
        rows = pl.ds(d * HALF_1, HALF_1) if s == 0 else pl.ds(0, RE)
        return rcopy(e0_snd.at[d, s, rows], e0_rcv.at[d, s, rows], e_s.at[d, 0, s], e_r.at[d, 0, s], dirs[d])

    def e1_copy(d, t, s):
        lo, n = (0, RE) if t == 1 else (RE, ROWS - RE)
        rows = pl.ds(lo + d * (n // 2), n // 2) if s == 0 else pl.ds(lo, n)
        return rcopy(e1_snd.at[d, s, rows], e1_rcv.at[d, s, rows], e_s.at[d, t, s], e_r.at[d, t, s], dirs[d])

    def other_part(k):
        p = down_part(target(k), 0)
        ey_snd[k] = p[RE:ROWS].astype(BF16)
        start(ey_copy(k))
        e0[k] = p[0:RE]

    other_part(0)
    for d in range(2):
        rows = slice(d * HALF_1, (d + 1) * HALF_1)
        e0_snd[d, 0, rows] = e0[0, rows].astype(BF16)
        start(e0_copy(d, 0))
    e1[0] = down_part(target(0), 1)
    for d in range(2):
        rows = slice(d * HALF_1, (d + 1) * HALF_1)
        e1_snd[d, 0, rows] = e1[0, rows].astype(BF16)
        start(e1_copy(d, 1, 0))
    other_part(1)
    other_part(2)
    ey_copy(0).wait_recv()
    for d in range(2):
        rows = slice(RE + d * HALF_2, RE + (d + 1) * HALF_2)
        e1_snd[d, 0, rows] = (e1[0, rows] + ey_rcv[0, d * HALF_2:(d + 1) * HALF_2].astype(F32)).astype(BF16)
        start(e1_copy(d, 2, 0))
    for s in range(1, 4):
        for d in range(2):
            e1[d] = down_part(target(2 * s - 1 + d), 1)
        for d in range(2):
            k = 2 * s - 1 + d
            e0_copy(d, s - 1).wait_recv()
            if s == 1:
                rows = slice(d * HALF_1, (d + 1) * HALF_1)
                rest = slice((1 - d) * HALF_1, (2 - d) * HALF_1)
                e0_snd[d, s, rows] = (e0[k, rows] + e0_rcv[d, 0, rows].astype(F32)).astype(BF16)
                e0_snd[d, s, rest] = e0[k, rest].astype(BF16)
            else:
                e0_snd[d, s] = (e0[k] + e0_rcv[d, s - 1].astype(F32)).astype(BF16)
            start(e0_copy(d, s))
        for t, lo, n in ((1, 0, RE), (2, RE, ROWS - RE)):
            for d in range(2):
                if t == 2:
                    k = 2 * s - 1 + d
                    ey_copy(k).wait_recv()
                    e1[d, RE:ROWS] += ey_rcv[k].astype(F32)
                e1_copy(d, t, s - 1).wait_recv()
                if s == 1:
                    rows = slice(lo + d * (n // 2), lo + (d + 1) * (n // 2))
                    rest = slice(lo + (1 - d) * (n // 2), lo + (2 - d) * (n // 2))
                    e1_snd[d, s, rows] = (e1[d, rows] + e1_rcv[d, 0, rows].astype(F32)).astype(BF16)
                    e1_snd[d, s, rest] = e1[d, rest].astype(BF16)
                else:
                    rows = slice(lo, lo + n)
                    e1_snd[d, s, rows] = (e1[d, rows] + e1_rcv[d, s - 1, rows].astype(F32)).astype(BF16)
                start(e1_copy(d, t, s))
            if t == 1:
                for d in range(2):
                    if 2 * s + 1 + d < NZ:
                        other_part(2 * s + 1 + d)
    e1[0] = down_part(z, 1)
    for d in range(2):
        e0_copy(d, 3).wait_recv()
    ez_snd[...] = (e0[7] + e0_rcv[0, 3].astype(F32) + e0_rcv[1, 3].astype(F32)).astype(BF16)
    ez = rcopy(ez_snd, ez_rcv, ex_s, ex_r, ypart)
    start(ez)
    ey_copy(7).wait_recv()
    e1[0, RE:ROWS] += ey_rcv[7].astype(F32)
    for t in (1, 2):
        for d in range(2):
            e1_copy(d, t, 3).wait_recv()
    e1[0] = e1[0] + e1_rcv[0, 3].astype(F32) + e1_rcv[1, 3].astype(F32)

    def f_copy(i, cc):
        return rcopy(ret_snd.at[pl.ds(i * CAP, CAP), pl.ds(cc * FW, FW)],
                     ret_v.at[pl.ds(pl.multiple_of(b * CAP, CAP), CAP)],
                     f_s.at[i * 2 + cc], f_r.at[b], chip_dev(4 * c + i, cc))

    for i in (2, 3, 0, 1):
        rows = slice(i * CAP, (i + 1) * CAP)
        if i == 0:
            ez.wait_recv()
            e1[0, 0:RE] += ez_rcv[...].astype(F32)
        ret_snd[rows] = e1[0, rows].astype(BF16)
        for cc in range(2):
            to_self = jnp.logical_and(4 * c + i == b, cc == c)
            mine = pltpu.make_async_copy(ret_snd.at[pl.ds(i * CAP, CAP), pl.ds(cc * FW, FW)],
                                         ret_v.at[pl.ds(pl.multiple_of(b * CAP, CAP), CAP)], loc.at[7])

            @pl.when(to_self)
            def _(mine=mine):
                mine.start()
                mine.wait()

            @pl.when(jnp.logical_not(to_self))
            def _(i=i, cc=cc):
                f_copy(i, cc).start()

    for x in range(NB):
        @pl.when(jnp.logical_not(jnp.logical_and(my_src, b == x)))
        def _(x=x):
            rcopy(ret_snd.at[pl.ds(0, CAP), pl.ds(0, FW)], ret_v.at[pl.ds(x * CAP, CAP)], f_s.at[0], f_r.at[x],
                  sib).wait_recv()
    out_ref[...] = (stream[...] + jnp.dot(g_hi[...], ret_v[...], preferred_element_type=F32)
                    + jnp.dot(g_lo[...], ret_v[...], preferred_element_type=F32)).astype(BF16)

    for cp in pend:
        cp.wait_send()

    for w in range(2):
        @pl.when(jnp.logical_not((yh == c) & (c == w)))
        def _(w=w):
            x_copy(w).wait_send()

    @pl.when(jnp.logical_not(my_src))
    def _():
        c_copy(0).wait_send()

    for i in range(4):
        for cc in range(2):
            @pl.when(jnp.logical_not(jnp.logical_and(4 * c + i == b, cc == c)))
            def _(i=i, cc=cc):
                f_copy(i, cc).wait_send()


def per_device(residual, heads_out, out_proj, norm_gain, gate_w, up_w, down_w, expert_ids, gate_slots, gate_table):
    any_, vmem = pl.BlockSpec(memory_space=pl.ANY), pl.BlockSpec(memory_space=pltpu.VMEM)
    dma, v = pltpu.SemaphoreType.DMA, pltpu.VMEM
    return pl.pallas_call(
        kernel,
        out_shape=jax.ShapeDtypeStruct((TOK, FW), BF16),
        in_specs=[any_, any_, any_, vmem, any_, any_, any_, vmem, vmem, vmem],
        out_specs=vmem,
        scratch_shapes=[
            v((TOK, FW), BF16), v((TOK, CW), BF16), v((FW, D), BF16), v((NB, 2, NZ, KR, CW), BF16),
            v((16, NZ, KR, CW), BF16), v((NZ, 2, KR, CW), BF16), v((NZ, 2, FW, CW), BF16),
            v((4, D, CW), BF16), v((2, CW, D), BF16), v((NB * CAP, TOK), BF16), v((NB * CAP, TOK), F32),
            v((TOK, NB * CAP), BF16), v((TOK, NB * CAP), BF16),
            v((2, 4, TOK, CW), BF16), v((2, 4, TOK, CW), BF16), v((2, TOK, CW), F32),
            v((TOK, CW), BF16), v((2, TOK, FW), BF16),
            v((TOK, FW), F32), v((NB * CAP, FW), BF16), v((16, BLK, CW), BF16), v((4, ROWS, CW), F32),
            v((ROWS, CW), F32), v((2, ROWS, CW), BF16), v((NZ, RE, CW), F32), v((2, ROWS, CW), F32),
            v((2, 4, RE, CW), BF16), v((2, 4, RE, CW), BF16), v((2, 4, ROWS, CW), BF16), v((2, 4, ROWS, CW), BF16),
            v((NZ, ROWS - RE, CW), BF16), v((NZ, ROWS - RE, CW), BF16), v((RE, CW), BF16), v((RE, CW), BF16),
            v((ROWS, CW), BF16), v((NB * CAP, FW), BF16),
            dma((9,)), dma((3,)), dma((3,)), dma, dma, dma((4, 16)), dma((4, 16)), dma((4, 7)), dma((4, 7)),
            dma((2, 4, 2)), dma((2, 4, 2)), dma((2,)), dma((2,)), dma, dma,
            dma((8,)), dma((8,)), dma((2, 3, 4)), dma((2, 3, 4)), dma((10,)), dma((10,)),
            dma((2, 3, 4)), dma((2, 3, 4)), dma, dma, dma((8,)), dma((8,)), dma((8,)), dma((8,)),
        ],
        compiler_params=pltpu.CompilerParams(
            collective_id=0, has_side_effects=True, vmem_limit_bytes=60 * 1024 * 1024),
        name="merge_moe",
    )(residual, heads_out, out_proj[0], norm_gain.reshape(1, FW), gate_w[0], up_w[0], down_w[0],
      expert_ids.T, gate_slots.T, gate_table.reshape(1, SLOTS))


def solution(mesh):
    return jax.shard_map(
        per_device,
        mesh=mesh,
        in_specs=(
            P("branch", "expert"), P("branch", "expert"), P("branch", "expert", None), P("expert"),
            P("branch", None, "expert"), P("branch", None, "expert"), P("branch", "expert", None),
            P("branch", None), P("branch", None), P(),
        ),
        out_specs=P("branch", "expert"),
        check_vma=False,
    )
```

```python
import jax
import jax.numpy as jnp
from jax import lax
from jax.experimental import pallas as pl
from jax.experimental.pallas import tpu as pltpu
from jax.sharding import PartitionSpec as P

MESH = pl.DeviceIdType.MESH
F32, BF16 = jnp.float32, jnp.bfloat16
D = 4096
SLOTS = 64
NB = 8
NZ = 8
TOK = 256
CAP = 96
ROWS = 4 * CAP
GROWS = 16
BLK = ROWS + GROWS
FW = 128
CW = 256
KR = 16
GROUPS = ((0, 3), (3, 2), (5, 2), (7, 1))
RD = 144
RE = 160
HALF_1, HALF_2 = RE // 2, (ROWS - RE) // 2


def rcopy(src, dst, send_sem, recv_sem, dev):
    return pltpu.make_async_remote_copy(
        src_ref=src, dst_ref=dst, send_sem=send_sem, recv_sem=recv_sem,
        device_id=dev, device_id_type=MESH)


def kernel(res_hbm, heads_hbm, op_hbm, gain_ref, gate_hbm, up_hbm, down_hbm, idst_ref, slots_ref,
           table_ref, out_ref,
           res_v, heads_v, op_v, op_x, op_in, mg, merged, w4, dn, sel, gsum, g_hi, g_lo, b_snd, b_rcv, b_tot,
           x_snd, x_rcv, stream, dsp, xg, acc, sq, hid, e0, e1, e0_snd, e0_rcv, e1_snd, e1_rcv, ey_snd, ey_rcv,
           ez_snd, ez_rcv, ret_snd, ret_v,
           loc, w_s, w_r, h_s, h_r, op_s, op_r, mg_s, mg_r, b_s, b_r, x_s, x_r, g_s, g_r,
           c_s, c_r, ag_s, ag_r, agy_s, agy_r, e_s, e_r, ex_s, ex_r, ey_s, ey_r, f_s, f_r):
    b = lax.axis_index("branch")
    e = lax.axis_index("expert")
    z = e // 4
    yh = (e // 2) % 2
    c = e % 2
    half = b // 4
    sib = (b, e + 1 - 2 * c)
    right = (b, ((z + 1) % NZ) * 4 + yh * 2 + c)
    left = (b, ((z + NZ - 1) % NZ) * 4 + yh * 2 + c)
    ypart = (b, z * 4 + (1 - yh) * 2 + c)
    ydiag = (b, z * 4 + (1 - yh) * 2 + 1 - c)
    dirs = (right, left)

    def chip_dev(j, core):
        return (j, z * 4 + yh * 2 + core)

    def target(k):
        if k == 0:
            return (z + 4) % NZ
        if k == NZ - 1:
            return z
        dist = 4 - (k + 1) // 2
        return (z + dist) % NZ if k % 2 else (z + NZ - dist) % NZ

    my_cols = pl.ds(pl.multiple_of(c * FW, FW), FW)
    loads = [
        pltpu.make_async_copy(op_hbm, op_v, loc.at[2]),
        pltpu.make_async_copy(heads_hbm, heads_v.at[:, my_cols], loc.at[1]),
        pltpu.make_async_copy(res_hbm, res_v, loc.at[0]),
        pltpu.make_async_copy(gate_hbm, w4.at[0], loc.at[3]),
        pltpu.make_async_copy(up_hbm, w4.at[2], loc.at[4]),
        pltpu.make_async_copy(down_hbm, dn.at[0], loc.at[5]),
    ]
    for ld in loads:
        ld.start()

    barrier = pltpu.get_barrier_semaphore()
    for kb in range(NB):
        for kc in range(2):
            if kb or kc:
                pl.semaphore_signal(barrier, inc=1, device_id=chip_dev((b + kb) % NB, (c + kc) % 2),
                                    device_id_type=MESH)
    ring_devs = [(b, ((z + dz) % NZ) * 4 + i) for dz in (1, NZ - 1) for i in range(4)]
    for dev in ring_devs + [ypart, ydiag]:
        pl.semaphore_signal(barrier, inc=1, device_id=dev, device_id_type=MESH)

    loads[0].wait()
    for k in range(NZ):
        for cc in range(2):
            cols = pl.ds(pl.multiple_of(target(k) * 2 * CW + cc * CW, CW), CW)
            op_x[:, cc, k] = op_v[:, cols].reshape(NB, KR, CW)
    op_in[b * 2 + c] = op_x[b, c]
    pl.semaphore_wait(barrier, 25)

    pend = []

    def start(cp):
        cp.start()
        pend.append(cp)

    def op_send(i):
        q, n = GROUPS[i]
        for kb in range(NB):
            for kc in range(2):
                if kb or kc:
                    j, cc = (b + kb) % NB, (c + kc) % 2
                    start(rcopy(op_x.at[j, cc, pl.ds(q, n)], op_in.at[b * 2 + c, pl.ds(q, n)],
                                op_s.at[i, kb * 2 + kc], op_r.at[i, kb * 2 + kc], chip_dev(j, cc)))

    def mg_copy(i, k, j):
        q, n = GROUPS[i]
        return rcopy(mg.at[pl.ds(q, n)], merged.at[pl.ds(q, n), :, pl.ds(pl.multiple_of(j * KR, KR), KR)],
                     mg_s.at[i, k - 1], mg_r.at[i, k - 1], chip_dev((b + k) % NB, c))

    def merge(i):
        q, n = GROUPS[i]
        for kb in range(NB):
            for kc in range(2):
                if kb or kc:
                    rcopy(op_x.at[0, 0, pl.ds(q, n)],
                          op_in.at[((b + NB - kb) % NB) * 2 + (c + kc) % 2, pl.ds(q, n)],
                          op_s.at[i, kb * 2 + kc], op_r.at[i, kb * 2 + kc], sib).wait_recv()
        for k in range(q, q + n):
            for cc in range(2):
                total = op_in[cc, k].astype(F32)
                for j in range(1, NB):
                    total = total + op_in[j * 2 + cc, k].astype(F32)
                total = (total / NB).astype(BF16)
                mg[k, cc] = total
                merged[k, cc, pl.ds(pl.multiple_of(b * KR, KR), KR)] = total
        for k in range(1, NB):
            start(mg_copy(i, k, b))

    def merged_wait(i):
        for k in range(1, NB):
            mg_copy(i, k, (b + NB - k) % NB).wait_recv()

    op_send(0)
    start(rcopy(heads_hbm, heads_v.at[:, my_cols], h_s, h_r, sib))
    op_send(1)
    for i, (src, dst) in enumerate(((gate_hbm, w4.at[1]), (up_hbm, w4.at[3]), (down_hbm, dn.at[1]))):
        cp = rcopy(src, dst, w_s.at[i], w_r.at[i], sib)
        cp.start()
        pend.append(cp)

    me = z * 2 + yh
    gain_at = (me, pl.ds(ROWS, GROWS), pl.ds(pl.multiple_of(c * FW, FW), FW))
    xg[gain_at] = jnp.broadcast_to(gain_ref[...], (GROWS, FW))
    gain_cp = rcopy(xg.at[gain_at], xg.at[gain_at], g_s, g_r, sib)
    gain_cp.start()
    pend.append(gain_cp)

    ids = idst_ref[...]
    xi = lax.broadcasted_iota(jnp.int32, (16, TOK), 0)
    named = ((ids[0:1] == xi) | (ids[1:2] == xi)).astype(BF16)
    before = (lax.broadcasted_iota(jnp.int32, (TOK, TOK), 0)
              < lax.broadcasted_iota(jnp.int32, (TOK, TOK), 1)).astype(BF16)
    rank = jnp.dot(named, before, preferred_element_type=F32).astype(jnp.int32)
    ci = lax.broadcasted_iota(jnp.int32, (CAP, TOK), 0)
    eye = lax.broadcasted_iota(jnp.int32, (SLOTS, SLOTS), 0) == lax.broadcasted_iota(jnp.int32, (SLOTS, SLOTS), 1)
    table = jnp.sum(jnp.where(eye, table_ref[...], 0.0), axis=1, keepdims=True)
    slot_i = lax.broadcasted_iota(jnp.int32, (SLOTS, TOK), 0)
    raw = [jnp.sum(jnp.where(slots_ref[k:k + 1] == slot_i, table, 0.0), axis=0, keepdims=True) for k in range(2)]
    gates = [raw[k] / (raw[0] + raw[1]) for k in range(2)]
    for x in range(NB):
        hit = rank[x:x + 1] == ci
        first, second = hit & (ids[0:1] == x), hit & (ids[1:2] == x)
        sel[x * CAP:(x + 1) * CAP] = (first | second).astype(BF16)
        gsum[x * CAP:(x + 1) * CAP] = jnp.where(first, gates[0], 0.0) + jnp.where(second, gates[1], 0.0)
    gt = gsum[...].T
    hi = gt.astype(BF16)
    g_hi[...] = hi
    g_lo[...] = (gt - hi.astype(F32)).astype(BF16)
    acc[...] = jnp.zeros_like(acc)
    sq[...] = jnp.zeros_like(sq)

    def attn_part(k):
        return jnp.dot(heads_v[...], merged[k].reshape(CW, CW), preferred_element_type=F32)

    def b_rows(d, u):
        return pl.ds(((d + u) % 2) * 128, 128)

    def b_copy(d, s, u):
        rows = b_rows(d, u)
        return rcopy(b_snd.at[d, s, rows], b_rcv.at[d, s, rows], b_s.at[d, s, u], b_r.at[d, s, u], dirs[d])

    def x_copy(kind, w, u):
        rows = pl.ds(u * 128, 128) if kind == 2 else b_rows(kind, u)
        src = x_snd.at[rows, pl.ds(w * FW, FW)] if kind == 2 else b_snd.at[kind, 3, rows, pl.ds(w * FW, FW)]
        zt = ((z + 1) % NZ, (z + NZ - 1) % NZ, z)[kind]
        return rcopy(src, x_rcv.at[kind, yh, rows], x_s.at[kind, w, u], x_r.at[kind, yh, u],
                     (b, zt * 4 + c * 2 + w))

    def x_wait(kind, ys, u):
        rows = pl.ds(u * 128, 128) if kind == 2 else b_rows(kind, u)
        ref = x_rcv.at[kind, ys, rows]
        rcopy(ref, ref, x_s.at[0, 0, 0], x_r.at[kind, ys, u], sib).wait_recv()

    def b_step(s):
        for d in range(2):
            b_tot[d] = attn_part(2 * s - 1 + d)
        for u in range(2):
            for d in range(2):
                rows = b_rows(d, u)
                if s > 1 or u == 0:
                    b_copy(d, s - 1, u).wait_recv()
                    b_snd[d, s, rows] = (b_tot[d, rows] + b_rcv[d, s - 1, rows].astype(F32)).astype(BF16)
                else:
                    b_snd[d, s, rows] = b_tot[d, rows].astype(BF16)
                if s < 3:
                    start(b_copy(d, s, u))
                else:
                    for w in range(2):
                        start(x_copy(d, w, u))

    merge(0)
    op_send(2)
    merge(1)
    op_send(3)
    loads[1].wait()
    their_cols = heads_v.at[:, pl.ds(pl.multiple_of((1 - c) * FW, FW), FW)]
    rcopy(their_cols, their_cols, h_s, h_r, sib).wait_recv()
    merged_wait(0)
    p = attn_part(0)
    for d in range(2):
        b_snd[d, 0, b_rows(d, 0)] = p[d * 128:(d + 1) * 128].astype(BF16)
        start(b_copy(d, 0, 0))
    merge(2)
    b_step(1)
    merge(3)
    merged_wait(1)
    b_step(2)
    merged_wait(2)
    b_step(3)
    merged_wait(3)
    x_snd[...] = attn_part(NZ - 1).astype(BF16)
    for u in range(2):
        for w in range(2):
            keep = (yh == c) & (c == w)

            @pl.when(keep)
            def _(u=u, w=w):
                x_rcv[2, yh, u * 128:(u + 1) * 128] = x_snd[u * 128:(u + 1) * 128, w * FW:(w + 1) * FW]

            @pl.when(jnp.logical_not(keep))
            def _(u=u, w=w):
                x_copy(2, w, u).start()

    for u in range(2):
        for kind in range(2):
            for ys in range(2):
                x_wait(kind, ys, u)
    for ys in range(2):
        @pl.when(jnp.logical_not((yh == c) & (yh == ys)))
        def _(ys=ys):
            for u in range(2):
                x_wait(2, ys, u)

    loads[2].wait()
    attn = x_rcv[0, 0].astype(F32)
    for i in range(1, 6):
        attn = attn + x_rcv[i // 2, i % 2].astype(F32)
    st = res_v[...].astype(F32) + attn
    stream[...] = st
    scaled = (st * gain_ref[...].astype(F32)).astype(BF16)
    dsp[...] = jnp.dot(sel[...], scaled, preferred_element_type=F32).astype(BF16)
    blk_at = (me, pl.ds(pl.multiple_of((b % 4) * CAP, CAP), CAP), pl.ds(pl.multiple_of(c * FW, FW), FW))
    my_src = half == c

    def c_copy(k):
        x = (b + k) % NB
        return rcopy(dsp.at[pl.ds(pl.multiple_of(x * CAP, CAP), CAP)], xg.at[blk_at], c_s.at[k],
                     c_r.at[(b % 4) * 2 + c], chip_dev(x, half))

    own_blk = pltpu.make_async_copy(dsp.at[pl.ds(pl.multiple_of(b * CAP, CAP), CAP)], xg.at[blk_at], loc.at[6])
    for k in range(1, NB):
        c_copy(k).start()
        pend.append(c_copy(k))

    @pl.when(my_src)
    def _():
        own_blk.start()

    @pl.when(jnp.logical_not(my_src))
    def _():
        c_copy(0).start()

    for i in range(8):
        @pl.when(jnp.logical_not(jnp.logical_and(my_src, (b % 4) * 2 + c == i)))
        def _(i=i):
            rcopy(dsp.at[pl.ds(0, CAP)], xg.at[me, pl.ds((i // 2) * CAP, CAP), pl.ds((i % 2) * FW, FW)],
                  c_s.at[0], c_r.at[i], sib).wait_recv()

    @pl.when(my_src)
    def _():
        own_blk.wait()

    sib_gain = xg.at[me, pl.ds(ROWS, GROWS), pl.ds(pl.multiple_of((1 - c) * FW, FW), FW)]
    rcopy(sib_gain, sib_gain, g_s, g_r, sib).wait_recv()

    def ag_copy(d, t, s, slot):
        lo, n = (RD, BLK - RD) if t == 0 else (0, RD)
        if s == 3:
            cut = n // 32 * 16
            lo, n = (lo, cut) if d == 0 else (lo + cut, n - cut)
        ref = xg.at[slot, pl.ds(lo, n)]
        return rcopy(ref, ref, ag_s.at[d, t, s], ag_r.at[d, t, s], dirs[d])

    def agy_copy(i, slot):
        if i == 0:
            lo, n = 0, RD
        elif i < 8:
            lo, n = RD, BLK - RD
        else:
            cut = (BLK - RD) // 32 * 16
            lo, n = (RD, cut) if i == 8 else (RD + cut, BLK - RD - cut)
        ref = xg.at[slot, pl.ds(lo, n)]
        return rcopy(ref, ref, agy_s.at[i], agy_r.at[i], ypart)

    def gate_up(slot):
        blk = xg[slot, 0:ROWS]
        inv = 1.0 / xg[slot, ROWS:BLK][0:1].astype(F32)
        v = blk.astype(F32) * inv
        sq[...] += v * v
        rows = pl.ds(pl.multiple_of(slot * CW, CW), CW)

        def part(i, carry):
            acc[i] += jnp.dot(xg[slot, 0:ROWS], w4[i, rows, :], preferred_element_type=F32)
            return carry
        lax.fori_loop(0, 4, part, 0)

    def slot_of(d, s, t):
        return ((z + NZ - s) % NZ if d == 0 else (z + s) % NZ) * 2 + (yh if t == 0 else 1 - yh)

    other = z * 2 + 1 - yh
    start(agy_copy(0, me))
    for t in range(2):
        for d in range(2):
            start(ag_copy(d, t, 0, me))
        if t == 0:
            start(agy_copy(1, me))
    loads[3].wait()
    loads[4].wait()
    for i in range(2):
        rcopy(gate_hbm, w4.at[1 + 2 * i], w_s.at[i], w_r.at[i], sib).wait_recv()
    gate_up(me)
    agy_copy(0, other).wait_recv()
    for d in range(2):
        start(ag_copy(d, 2, 0, other))
    for s in range(1, 4):
        for t in range(2):
            for d in range(2):
                slot = slot_of(d, s, 0)
                ag_copy(d, t, s - 1, slot).wait_recv()
                start(ag_copy(d, t, s, slot))
                if t == 0:
                    start(agy_copy(2 * s + d, slot))
        gate_up(slot_of(0, s, 0))
        for d in range(2):
            slot = slot_of(d, s, 1)
            ag_copy(d, 2, s - 1, slot).wait_recv()
            start(ag_copy(d, 2, s, slot))
        gate_up(slot_of(1, s, 0))
        if s == 1:
            agy_copy(1, other).wait_recv()
            gate_up(other)
        else:
            for d in range(2):
                slot = slot_of(d, s - 1, 1)
                agy_copy(2 * (s - 1) + d, slot).wait_recv()
                gate_up(slot)
    far = slot_of(0, 4, 0)
    for d in range(2):
        ag_copy(d, 0, 3, far).wait_recv()
        start(agy_copy(8 + d, far))
    for d in range(2):
        ag_copy(d, 1, 3, far).wait_recv()
    gate_up(far)
    for d in range(2):
        slot = slot_of(d, 3, 1)
        agy_copy(6 + d, slot).wait_recv()
        gate_up(slot)
    far = slot_of(0, 4, 1)
    for d in range(2):
        ag_copy(d, 2, 3, far).wait_recv()
        agy_copy(8 + d, far).wait_recv()
    gate_up(far)

    scale = lax.rsqrt(jnp.sum(sq[...], axis=1, keepdims=True) / D + 1e-05)
    for i in range(2):
        g = acc[i] * scale
        hid[i] = (g / (1.0 + jnp.exp(-g)) * (acc[2 + i] * scale)).astype(BF16)
    loads[5].wait()
    rcopy(down_hbm, dn.at[1], w_s.at[2], w_r.at[2], sib).wait_recv()

    def down_part(zd, t):
        yy = 1 - yh if t == 0 else yh
        cols = pl.ds(pl.multiple_of((zd * 2 + yy) * CW, CW), CW)
        return (jnp.dot(hid[0], dn[0, :, cols], preferred_element_type=F32)
                + jnp.dot(hid[1], dn[1, :, cols], preferred_element_type=F32))

    def ey_copy(k):
        return rcopy(ey_snd.at[k], ey_rcv.at[k], ey_s.at[k], ey_r.at[k], ypart)

    def e0_copy(d, s):
        rows = pl.ds(d * HALF_1, HALF_1) if s == 0 else pl.ds(0, RE)
        return rcopy(e0_snd.at[d, s, rows], e0_rcv.at[d, s, rows], e_s.at[d, 0, s], e_r.at[d, 0, s], dirs[d])

    def e1_copy(d, t, s):
        lo, n = (0, RE) if t == 1 else (RE, ROWS - RE)
        rows = pl.ds(lo + d * (n // 2), n // 2) if s == 0 else pl.ds(lo, n)
        return rcopy(e1_snd.at[d, s, rows], e1_rcv.at[d, s, rows], e_s.at[d, t, s], e_r.at[d, t, s], dirs[d])

    def other_part(k):
        p = down_part(target(k), 0)
        ey_snd[k] = p[RE:ROWS].astype(BF16)
        start(ey_copy(k))
        e0[k] = p[0:RE]

    other_part(0)
    for d in range(2):
        rows = slice(d * HALF_1, (d + 1) * HALF_1)
        e0_snd[d, 0, rows] = e0[0, rows].astype(BF16)
        start(e0_copy(d, 0))
    e1[0] = down_part(target(0), 1)
    for d in range(2):
        rows = slice(d * HALF_1, (d + 1) * HALF_1)
        e1_snd[d, 0, rows] = e1[0, rows].astype(BF16)
        start(e1_copy(d, 1, 0))
    other_part(1)
    other_part(2)
    ey_copy(0).wait_recv()
    for d in range(2):
        rows = slice(RE + d * HALF_2, RE + (d + 1) * HALF_2)
        e1_snd[d, 0, rows] = (e1[0, rows] + ey_rcv[0, d * HALF_2:(d + 1) * HALF_2].astype(F32)).astype(BF16)
        start(e1_copy(d, 2, 0))
    for s in range(1, 4):
        for d in range(2):
            e1[d] = down_part(target(2 * s - 1 + d), 1)
        for d in range(2):
            k = 2 * s - 1 + d
            e0_copy(d, s - 1).wait_recv()
            if s == 1:
                rows = slice(d * HALF_1, (d + 1) * HALF_1)
                rest = slice((1 - d) * HALF_1, (2 - d) * HALF_1)
                e0_snd[d, s, rows] = (e0[k, rows] + e0_rcv[d, 0, rows].astype(F32)).astype(BF16)
                e0_snd[d, s, rest] = e0[k, rest].astype(BF16)
            else:
                e0_snd[d, s] = (e0[k] + e0_rcv[d, s - 1].astype(F32)).astype(BF16)
            start(e0_copy(d, s))
        for t, lo, n in ((1, 0, RE), (2, RE, ROWS - RE)):
            for d in range(2):
                if t == 2:
                    k = 2 * s - 1 + d
                    ey_copy(k).wait_recv()
                    e1[d, RE:ROWS] += ey_rcv[k].astype(F32)
                e1_copy(d, t, s - 1).wait_recv()
                if s == 1:
                    rows = slice(lo + d * (n // 2), lo + (d + 1) * (n // 2))
                    rest = slice(lo + (1 - d) * (n // 2), lo + (2 - d) * (n // 2))
                    e1_snd[d, s, rows] = (e1[d, rows] + e1_rcv[d, 0, rows].astype(F32)).astype(BF16)
                    e1_snd[d, s, rest] = e1[d, rest].astype(BF16)
                else:
                    rows = slice(lo, lo + n)
                    e1_snd[d, s, rows] = (e1[d, rows] + e1_rcv[d, s - 1, rows].astype(F32)).astype(BF16)
                start(e1_copy(d, t, s))
            if t == 1:
                for d in range(2):
                    if 2 * s + 1 + d < NZ:
                        other_part(2 * s + 1 + d)
    e1[0] = down_part(z, 1)
    for d in range(2):
        e0_copy(d, 3).wait_recv()
    ez_snd[...] = (e0[7] + e0_rcv[0, 3].astype(F32) + e0_rcv[1, 3].astype(F32)).astype(BF16)
    ez = rcopy(ez_snd, ez_rcv, ex_s, ex_r, ypart)
    start(ez)
    ey_copy(7).wait_recv()
    e1[0, RE:ROWS] += ey_rcv[7].astype(F32)
    for t in (1, 2):
        for d in range(2):
            e1_copy(d, t, 3).wait_recv()
    e1[0] = e1[0] + e1_rcv[0, 3].astype(F32) + e1_rcv[1, 3].astype(F32)

    def f_copy(i, cc):
        return rcopy(ret_snd.at[pl.ds(i * CAP, CAP), pl.ds(cc * FW, FW)],
                     ret_v.at[pl.ds(pl.multiple_of(b * CAP, CAP), CAP)],
                     f_s.at[i * 2 + cc], f_r.at[b], chip_dev(4 * c + i, cc))

    for i in (2, 3, 0, 1):
        rows = slice(i * CAP, (i + 1) * CAP)
        if i == 0:
            ez.wait_recv()
            e1[0, 0:RE] += ez_rcv[...].astype(F32)
        ret_snd[rows] = e1[0, rows].astype(BF16)
        for cc in range(2):
            to_self = jnp.logical_and(4 * c + i == b, cc == c)
            mine = pltpu.make_async_copy(ret_snd.at[pl.ds(i * CAP, CAP), pl.ds(cc * FW, FW)],
                                         ret_v.at[pl.ds(pl.multiple_of(b * CAP, CAP), CAP)], loc.at[7])

            @pl.when(to_self)
            def _(mine=mine):
                mine.start()
                mine.wait()

            @pl.when(jnp.logical_not(to_self))
            def _(i=i, cc=cc):
                f_copy(i, cc).start()

    for x in range(NB):
        @pl.when(jnp.logical_not(jnp.logical_and(my_src, b == x)))
        def _(x=x):
            rcopy(ret_snd.at[pl.ds(0, CAP), pl.ds(0, FW)], ret_v.at[pl.ds(x * CAP, CAP)], f_s.at[0], f_r.at[x],
                  sib).wait_recv()
    out_ref[...] = (stream[...] + jnp.dot(g_hi[...], ret_v[...], preferred_element_type=F32)
                    + jnp.dot(g_lo[...], ret_v[...], preferred_element_type=F32)).astype(BF16)

    for cp in pend:
        cp.wait_send()

    for w in range(2):
        @pl.when(jnp.logical_not((yh == c) & (c == w)))
        def _(w=w):
            for u in range(2):
                x_copy(2, w, u).wait_send()

    @pl.when(jnp.logical_not(my_src))
    def _():
        c_copy(0).wait_send()

    for i in range(4):
        for cc in range(2):
            @pl.when(jnp.logical_not(jnp.logical_and(4 * c + i == b, cc == c)))
            def _(i=i, cc=cc):
                f_copy(i, cc).wait_send()


def per_device(residual, heads_out, out_proj, norm_gain, gate_w, up_w, down_w, expert_ids, gate_slots, gate_table):
    any_, vmem = pl.BlockSpec(memory_space=pl.ANY), pl.BlockSpec(memory_space=pltpu.VMEM)
    dma, v = pltpu.SemaphoreType.DMA, pltpu.VMEM
    return pl.pallas_call(
        kernel,
        out_shape=jax.ShapeDtypeStruct((TOK, FW), BF16),
        in_specs=[any_, any_, any_, vmem, any_, any_, any_, vmem, vmem, vmem],
        out_specs=vmem,
        scratch_shapes=[
            v((TOK, FW), BF16), v((TOK, CW), BF16), v((FW, D), BF16), v((NB, 2, NZ, KR, CW), BF16),
            v((16, NZ, KR, CW), BF16), v((NZ, 2, KR, CW), BF16), v((NZ, 2, FW, CW), BF16),
            v((4, D, CW), BF16), v((2, CW, D), BF16), v((NB * CAP, TOK), BF16), v((NB * CAP, TOK), F32),
            v((TOK, NB * CAP), BF16), v((TOK, NB * CAP), BF16),
            v((2, 4, TOK, CW), BF16), v((2, 4, TOK, CW), BF16), v((2, TOK, CW), F32),
            v((TOK, CW), BF16), v((3, 2, TOK, FW), BF16),
            v((TOK, FW), F32), v((NB * CAP, FW), BF16), v((16, BLK, CW), BF16), v((4, ROWS, CW), F32),
            v((ROWS, CW), F32), v((2, ROWS, CW), BF16), v((NZ, RE, CW), F32), v((2, ROWS, CW), F32),
            v((2, 4, RE, CW), BF16), v((2, 4, RE, CW), BF16), v((2, 4, ROWS, CW), BF16), v((2, 4, ROWS, CW), BF16),
            v((NZ, ROWS - RE, CW), BF16), v((NZ, ROWS - RE, CW), BF16), v((RE, CW), BF16), v((RE, CW), BF16),
            v((ROWS, CW), BF16), v((NB * CAP, FW), BF16),
            dma((9,)), dma((3,)), dma((3,)), dma, dma, dma((4, 16)), dma((4, 16)), dma((4, 7)), dma((4, 7)),
            dma((2, 3, 2)), dma((2, 3, 2)), dma((3, 2, 2)), dma((3, 2, 2)), dma, dma,
            dma((8,)), dma((8,)), dma((2, 3, 4)), dma((2, 3, 4)), dma((10,)), dma((10,)),
            dma((2, 3, 4)), dma((2, 3, 4)), dma, dma, dma((8,)), dma((8,)), dma((8,)), dma((8,)),
        ],
        compiler_params=pltpu.CompilerParams(
            collective_id=0, has_side_effects=True, vmem_limit_bytes=60 * 1024 * 1024),
        name="merge_moe",
    )(residual, heads_out, out_proj[0], norm_gain.reshape(1, FW), gate_w[0], up_w[0], down_w[0],
      expert_ids.T, gate_slots.T, gate_table.reshape(1, SLOTS))


def solution(mesh):
    return jax.shard_map(
        per_device,
        mesh=mesh,
        in_specs=(
            P("branch", "expert"), P("branch", "expert"), P("branch", "expert", None), P("expert"),
            P("branch", None, "expert"), P("branch", None, "expert"), P("branch", "expert", None),
            P("branch", None), P("branch", None), P(),
        ),
        out_specs=P("branch", "expert"),
        check_vma=False,
    )
```

```python
import jax
import jax.numpy as jnp
from jax import lax
from jax.experimental import pallas as pl
from jax.experimental.pallas import tpu as pltpu
from jax.sharding import PartitionSpec as P

MESH = pl.DeviceIdType.MESH
F32, BF16 = jnp.float32, jnp.bfloat16
D = 4096
SLOTS = 64
NB = 8
NZ = 8
TOK = 256
CAP = 96
ROWS = 4 * CAP
GROWS = 16
BLK = ROWS + GROWS
FW = 128
CW = 256
KR = 16
GROUPS = ((0, 1), (1, 2), (3, 2), (5, 2), (7, 1))
RD = 144
RE = 160
HALF_1, HALF_2 = RE // 2, (ROWS - RE) // 2


def rcopy(src, dst, send_sem, recv_sem, dev):
    return pltpu.make_async_remote_copy(
        src_ref=src, dst_ref=dst, send_sem=send_sem, recv_sem=recv_sem,
        device_id=dev, device_id_type=MESH)


def kernel(res_hbm, heads_hbm, op_hbm, gain_ref, gate_hbm, up_hbm, down_hbm, idst_ref, slots_ref,
           table_ref, out_ref,
           res_v, heads_v, op_v, op_x, op_in, mg, merged, w4, dn, sel, gsum, g_hi, g_lo, b_snd, b_rcv, b_tot,
           x_snd, x_rcv, stream, dsp, xg, acc, sq, hid, e0, e1, e0_snd, e0_rcv, e1_snd, e1_rcv, ey_snd, ey_rcv,
           ez_snd, ez_rcv, ret_snd, ret_v,
           loc, w_s, w_r, h_s, h_r, op_s, op_r, mg_s, mg_r, b_s, b_r, x_s, x_r, g_s, g_r,
           c_s, c_r, ag_s, ag_r, agy_s, agy_r, e_s, e_r, ex_s, ex_r, ey_s, ey_r, f_s, f_r):
    b = lax.axis_index("branch")
    e = lax.axis_index("expert")
    z = e // 4
    yh = (e // 2) % 2
    c = e % 2
    half = b // 4
    sib = (b, e + 1 - 2 * c)
    right = (b, ((z + 1) % NZ) * 4 + yh * 2 + c)
    left = (b, ((z + NZ - 1) % NZ) * 4 + yh * 2 + c)
    ypart = (b, z * 4 + (1 - yh) * 2 + c)
    ydiag = (b, z * 4 + (1 - yh) * 2 + 1 - c)
    dirs = (right, left)

    def chip_dev(j, core):
        return (j, z * 4 + yh * 2 + core)

    def target(k):
        if k == 0:
            return (z + 4) % NZ
        if k == NZ - 1:
            return z
        dist = 4 - (k + 1) // 2
        return (z + dist) % NZ if k % 2 else (z + NZ - dist) % NZ

    my_cols = pl.ds(pl.multiple_of(c * FW, FW), FW)
    loads = [
        pltpu.make_async_copy(op_hbm, op_v, loc.at[2]),
        pltpu.make_async_copy(heads_hbm, heads_v.at[:, my_cols], loc.at[1]),
        pltpu.make_async_copy(res_hbm, res_v, loc.at[0]),
        pltpu.make_async_copy(gate_hbm, w4.at[0], loc.at[3]),
        pltpu.make_async_copy(up_hbm, w4.at[2], loc.at[4]),
        pltpu.make_async_copy(down_hbm, dn.at[0], loc.at[5]),
    ]
    for ld in loads:
        ld.start()

    barrier = pltpu.get_barrier_semaphore()
    for kb in range(NB):
        for kc in range(2):
            if kb or kc:
                pl.semaphore_signal(barrier, inc=1, device_id=chip_dev((b + kb) % NB, (c + kc) % 2),
                                    device_id_type=MESH)
    ring_devs = [(b, ((z + dz) % NZ) * 4 + i) for dz in (1, NZ - 1) for i in range(4)]
    for dev in ring_devs + [ypart, ydiag]:
        pl.semaphore_signal(barrier, inc=1, device_id=dev, device_id_type=MESH)

    loads[0].wait()
    for k in range(NZ):
        for cc in range(2):
            cols = pl.ds(pl.multiple_of(target(k) * 2 * CW + cc * CW, CW), CW)
            op_x[:, cc, k] = op_v[:, cols].reshape(NB, KR, CW)
    op_in[b * 2 + c] = op_x[b, c]
    pl.semaphore_wait(barrier, 25)

    pend = []

    def start(cp):
        cp.start()
        pend.append(cp)

    def op_send(i):
        q, n = GROUPS[i]
        for kb in range(NB):
            for kc in range(2):
                if kb or kc:
                    j, cc = (b + kb) % NB, (c + kc) % 2
                    start(rcopy(op_x.at[j, cc, pl.ds(q, n)], op_in.at[b * 2 + c, pl.ds(q, n)],
                                op_s.at[i, kb * 2 + kc], op_r.at[i, kb * 2 + kc], chip_dev(j, cc)))

    def mg_copy(i, k, j):
        q, n = GROUPS[i]
        return rcopy(mg.at[pl.ds(q, n)], merged.at[pl.ds(q, n), :, pl.ds(pl.multiple_of(j * KR, KR), KR)],
                     mg_s.at[i, k - 1], mg_r.at[i, k - 1], chip_dev((b + k) % NB, c))

    def merge(i):
        q, n = GROUPS[i]
        for kb in range(NB):
            for kc in range(2):
                if kb or kc:
                    rcopy(op_x.at[0, 0, pl.ds(q, n)],
                          op_in.at[((b + NB - kb) % NB) * 2 + (c + kc) % 2, pl.ds(q, n)],
                          op_s.at[i, kb * 2 + kc], op_r.at[i, kb * 2 + kc], sib).wait_recv()
        for k in range(q, q + n):
            for cc in range(2):
                total = op_in[cc, k].astype(F32)
                for j in range(1, NB):
                    total = total + op_in[j * 2 + cc, k].astype(F32)
                total = (total / NB).astype(BF16)
                mg[k, cc] = total
                merged[k, cc, pl.ds(pl.multiple_of(b * KR, KR), KR)] = total
        for k in range(1, NB):
            start(mg_copy(i, k, b))

    def merged_wait(i):
        for k in range(1, NB):
            mg_copy(i, k, (b + NB - k) % NB).wait_recv()

    op_send(0)
    start(rcopy(heads_hbm, heads_v.at[:, my_cols], h_s, h_r, sib))
    op_send(1)
    for i, (src, dst) in enumerate(((gate_hbm, w4.at[1]), (up_hbm, w4.at[3]), (down_hbm, dn.at[1]))):
        cp = rcopy(src, dst, w_s.at[i], w_r.at[i], sib)
        cp.start()
        pend.append(cp)

    me = z * 2 + yh
    gain_at = (me, pl.ds(ROWS, GROWS), pl.ds(pl.multiple_of(c * FW, FW), FW))
    xg[gain_at] = jnp.broadcast_to(gain_ref[...], (GROWS, FW))
    gain_cp = rcopy(xg.at[gain_at], xg.at[gain_at], g_s, g_r, sib)
    gain_cp.start()
    pend.append(gain_cp)

    ids = idst_ref[...]
    xi = lax.broadcasted_iota(jnp.int32, (16, TOK), 0)
    named = ((ids[0:1] == xi) | (ids[1:2] == xi)).astype(BF16)
    before = (lax.broadcasted_iota(jnp.int32, (TOK, TOK), 0)
              < lax.broadcasted_iota(jnp.int32, (TOK, TOK), 1)).astype(BF16)
    rank = jnp.dot(named, before, preferred_element_type=F32).astype(jnp.int32)
    ci = lax.broadcasted_iota(jnp.int32, (CAP, TOK), 0)
    eye = lax.broadcasted_iota(jnp.int32, (SLOTS, SLOTS), 0) == lax.broadcasted_iota(jnp.int32, (SLOTS, SLOTS), 1)
    table = jnp.sum(jnp.where(eye, table_ref[...], 0.0), axis=1, keepdims=True)
    slot_i = lax.broadcasted_iota(jnp.int32, (SLOTS, TOK), 0)
    raw = [jnp.sum(jnp.where(slots_ref[k:k + 1] == slot_i, table, 0.0), axis=0, keepdims=True) for k in range(2)]
    gates = [raw[k] / (raw[0] + raw[1]) for k in range(2)]
    for x in range(NB):
        hit = rank[x:x + 1] == ci
        first, second = hit & (ids[0:1] == x), hit & (ids[1:2] == x)
        sel[x * CAP:(x + 1) * CAP] = (first | second).astype(BF16)
        gsum[x * CAP:(x + 1) * CAP] = jnp.where(first, gates[0], 0.0) + jnp.where(second, gates[1], 0.0)
    gt = gsum[...].T
    hi = gt.astype(BF16)
    g_hi[...] = hi
    g_lo[...] = (gt - hi.astype(F32)).astype(BF16)
    acc[...] = jnp.zeros_like(acc)
    sq[...] = jnp.zeros_like(sq)

    def attn_part(k):
        return jnp.dot(heads_v[...], merged[k].reshape(CW, CW), preferred_element_type=F32)

    def b_rows(d, u):
        return pl.ds(((d + u) % 2) * 128, 128)

    def b_copy(d, s, u):
        rows = b_rows(d, u)
        return rcopy(b_snd.at[d, s, rows], b_rcv.at[d, s, rows], b_s.at[d, s, u], b_r.at[d, s, u], dirs[d])

    def x_copy(kind, w, u):
        rows = pl.ds(u * 128, 128) if kind == 2 else b_rows(kind, u)
        src = x_snd.at[rows, pl.ds(w * FW, FW)] if kind == 2 else b_snd.at[kind, 3, rows, pl.ds(w * FW, FW)]
        zt = ((z + 1) % NZ, (z + NZ - 1) % NZ, z)[kind]
        return rcopy(src, x_rcv.at[kind, yh, rows], x_s.at[kind, w, u], x_r.at[kind, yh, u],
                     (b, zt * 4 + c * 2 + w))

    def x_wait(kind, ys, u):
        rows = pl.ds(u * 128, 128) if kind == 2 else b_rows(kind, u)
        ref = x_rcv.at[kind, ys, rows]
        rcopy(ref, ref, x_s.at[0, 0, 0], x_r.at[kind, ys, u], sib).wait_recv()

    def b_step(s):
        for d in range(2):
            b_tot[d] = attn_part(2 * s - 1 + d)
        for u in range(2):
            for d in range(2):
                rows = b_rows(d, u)
                if s > 1 or u == 0:
                    b_copy(d, s - 1, u).wait_recv()
                    b_snd[d, s, rows] = (b_tot[d, rows] + b_rcv[d, s - 1, rows].astype(F32)).astype(BF16)
                else:
                    b_snd[d, s, rows] = b_tot[d, rows].astype(BF16)
                if s < 3:
                    start(b_copy(d, s, u))
                else:
                    for w in range(2):
                        start(x_copy(d, w, u))

    merge(0)
    op_send(2)
    merge(1)
    op_send(3)
    loads[1].wait()
    their_cols = heads_v.at[:, pl.ds(pl.multiple_of((1 - c) * FW, FW), FW)]
    rcopy(their_cols, their_cols, h_s, h_r, sib).wait_recv()
    merged_wait(0)
    p = attn_part(0)
    for d in range(2):
        b_snd[d, 0, b_rows(d, 0)] = p[d * 128:(d + 1) * 128].astype(BF16)
        start(b_copy(d, 0, 0))
    merge(2)
    op_send(4)
    merged_wait(1)
    b_step(1)
    merge(3)
    merged_wait(2)
    b_step(2)
    merge(4)
    merged_wait(3)
    b_step(3)
    merged_wait(4)
    x_snd[...] = attn_part(NZ - 1).astype(BF16)
    for u in range(2):
        for w in range(2):
            keep = (yh == c) & (c == w)

            @pl.when(keep)
            def _(u=u, w=w):
                x_rcv[2, yh, u * 128:(u + 1) * 128] = x_snd[u * 128:(u + 1) * 128, w * FW:(w + 1) * FW]

            @pl.when(jnp.logical_not(keep))
            def _(u=u, w=w):
                x_copy(2, w, u).start()

    for u in range(2):
        for kind in range(2):
            for ys in range(2):
                x_wait(kind, ys, u)
    for ys in range(2):
        @pl.when(jnp.logical_not((yh == c) & (yh == ys)))
        def _(ys=ys):
            for u in range(2):
                x_wait(2, ys, u)

    loads[2].wait()
    attn = x_rcv[0, 0].astype(F32)
    for i in range(1, 6):
        attn = attn + x_rcv[i // 2, i % 2].astype(F32)
    st = res_v[...].astype(F32) + attn
    stream[...] = st
    scaled = (st * gain_ref[...].astype(F32)).astype(BF16)
    dsp[...] = jnp.dot(sel[...], scaled, preferred_element_type=F32).astype(BF16)
    blk_at = (me, pl.ds(pl.multiple_of((b % 4) * CAP, CAP), CAP), pl.ds(pl.multiple_of(c * FW, FW), FW))
    my_src = half == c

    def c_copy(k):
        x = (b + k) % NB
        return rcopy(dsp.at[pl.ds(pl.multiple_of(x * CAP, CAP), CAP)], xg.at[blk_at], c_s.at[k],
                     c_r.at[(b % 4) * 2 + c], chip_dev(x, half))

    own_blk = pltpu.make_async_copy(dsp.at[pl.ds(pl.multiple_of(b * CAP, CAP), CAP)], xg.at[blk_at], loc.at[6])
    for k in range(1, NB):
        c_copy(k).start()
        pend.append(c_copy(k))

    @pl.when(my_src)
    def _():
        own_blk.start()

    @pl.when(jnp.logical_not(my_src))
    def _():
        c_copy(0).start()

    for i in range(8):
        @pl.when(jnp.logical_not(jnp.logical_and(my_src, (b % 4) * 2 + c == i)))
        def _(i=i):
            rcopy(dsp.at[pl.ds(0, CAP)], xg.at[me, pl.ds((i // 2) * CAP, CAP), pl.ds((i % 2) * FW, FW)],
                  c_s.at[0], c_r.at[i], sib).wait_recv()

    @pl.when(my_src)
    def _():
        own_blk.wait()

    sib_gain = xg.at[me, pl.ds(ROWS, GROWS), pl.ds(pl.multiple_of((1 - c) * FW, FW), FW)]
    rcopy(sib_gain, sib_gain, g_s, g_r, sib).wait_recv()

    def ag_copy(d, t, s, slot):
        lo, n = (RD, BLK - RD) if t == 0 else (0, RD)
        if s == 3:
            cut = n // 32 * 16
            lo, n = (lo, cut) if d == 0 else (lo + cut, n - cut)
        ref = xg.at[slot, pl.ds(lo, n)]
        return rcopy(ref, ref, ag_s.at[d, t, s], ag_r.at[d, t, s], dirs[d])

    def agy_copy(i, slot):
        if i == 0:
            lo, n = 0, RD
        elif i < 8:
            lo, n = RD, BLK - RD
        else:
            cut = (BLK - RD) // 32 * 16
            lo, n = (RD, cut) if i == 8 else (RD + cut, BLK - RD - cut)
        ref = xg.at[slot, pl.ds(lo, n)]
        return rcopy(ref, ref, agy_s.at[i], agy_r.at[i], ypart)

    def gate_up(slot):
        blk = xg[slot, 0:ROWS]
        inv = 1.0 / xg[slot, ROWS:BLK][0:1].astype(F32)
        v = blk.astype(F32) * inv
        sq[...] += v * v
        rows = pl.ds(pl.multiple_of(slot * CW, CW), CW)

        def part(i, carry):
            acc[i] += jnp.dot(xg[slot, 0:ROWS], w4[i, rows, :], preferred_element_type=F32)
            return carry
        lax.fori_loop(0, 4, part, 0)

    def slot_of(d, s, t):
        return ((z + NZ - s) % NZ if d == 0 else (z + s) % NZ) * 2 + (yh if t == 0 else 1 - yh)

    other = z * 2 + 1 - yh
    start(agy_copy(0, me))
    for t in range(2):
        for d in range(2):
            start(ag_copy(d, t, 0, me))
        if t == 0:
            start(agy_copy(1, me))
    loads[3].wait()
    loads[4].wait()
    for i in range(2):
        rcopy(gate_hbm, w4.at[1 + 2 * i], w_s.at[i], w_r.at[i], sib).wait_recv()
    gate_up(me)
    agy_copy(0, other).wait_recv()
    for d in range(2):
        start(ag_copy(d, 2, 0, other))
    for s in range(1, 4):
        for t in range(2):
            for d in range(2):
                slot = slot_of(d, s, 0)
                ag_copy(d, t, s - 1, slot).wait_recv()
                start(ag_copy(d, t, s, slot))
                if t == 0:
                    start(agy_copy(2 * s + d, slot))
        gate_up(slot_of(0, s, 0))
        for d in range(2):
            slot = slot_of(d, s, 1)
            ag_copy(d, 2, s - 1, slot).wait_recv()
            start(ag_copy(d, 2, s, slot))
        gate_up(slot_of(1, s, 0))
        if s == 1:
            agy_copy(1, other).wait_recv()
            gate_up(other)
        else:
            for d in range(2):
                slot = slot_of(d, s - 1, 1)
                agy_copy(2 * (s - 1) + d, slot).wait_recv()
                gate_up(slot)
    far = slot_of(0, 4, 0)
    for d in range(2):
        ag_copy(d, 0, 3, far).wait_recv()
        start(agy_copy(8 + d, far))
    for d in range(2):
        ag_copy(d, 1, 3, far).wait_recv()
    gate_up(far)
    for d in range(2):
        slot = slot_of(d, 3, 1)
        agy_copy(6 + d, slot).wait_recv()
        gate_up(slot)
    far = slot_of(0, 4, 1)
    for d in range(2):
        ag_copy(d, 2, 3, far).wait_recv()
        agy_copy(8 + d, far).wait_recv()
    gate_up(far)

    scale = lax.rsqrt(jnp.sum(sq[...], axis=1, keepdims=True) / D + 1e-05)
    for i in range(2):
        g = acc[i] * scale
        hid[i] = (g / (1.0 + jnp.exp(-g)) * (acc[2 + i] * scale)).astype(BF16)
    loads[5].wait()
    rcopy(down_hbm, dn.at[1], w_s.at[2], w_r.at[2], sib).wait_recv()

    def down_part(zd, t):
        yy = 1 - yh if t == 0 else yh
        cols = pl.ds(pl.multiple_of((zd * 2 + yy) * CW, CW), CW)
        return (jnp.dot(hid[0], dn[0, :, cols], preferred_element_type=F32)
                + jnp.dot(hid[1], dn[1, :, cols], preferred_element_type=F32))

    def ey_copy(k):
        return rcopy(ey_snd.at[k], ey_rcv.at[k], ey_s.at[k], ey_r.at[k], ypart)

    def e0_copy(d, s):
        rows = pl.ds(d * HALF_1, HALF_1) if s == 0 else pl.ds(0, RE)
        return rcopy(e0_snd.at[d, s, rows], e0_rcv.at[d, s, rows], e_s.at[d, 0, s], e_r.at[d, 0, s], dirs[d])

    def e1_copy(d, t, s):
        lo, n = (0, RE) if t == 1 else (RE, ROWS - RE)
        rows = pl.ds(lo + d * (n // 2), n // 2) if s == 0 else pl.ds(lo, n)
        return rcopy(e1_snd.at[d, s, rows], e1_rcv.at[d, s, rows], e_s.at[d, t, s], e_r.at[d, t, s], dirs[d])

    def other_part(k):
        p = down_part(target(k), 0)
        ey_snd[k] = p[RE:ROWS].astype(BF16)
        start(ey_copy(k))
        e0[k] = p[0:RE]

    other_part(0)
    for d in range(2):
        rows = slice(d * HALF_1, (d + 1) * HALF_1)
        e0_snd[d, 0, rows] = e0[0, rows].astype(BF16)
        start(e0_copy(d, 0))
    e1[0] = down_part(target(0), 1)
    for d in range(2):
        rows = slice(d * HALF_1, (d + 1) * HALF_1)
        e1_snd[d, 0, rows] = e1[0, rows].astype(BF16)
        start(e1_copy(d, 1, 0))
    other_part(1)
    other_part(2)
    ey_copy(0).wait_recv()
    for d in range(2):
        rows = slice(RE + d * HALF_2, RE + (d + 1) * HALF_2)
        e1_snd[d, 0, rows] = (e1[0, rows] + ey_rcv[0, d * HALF_2:(d + 1) * HALF_2].astype(F32)).astype(BF16)
        start(e1_copy(d, 2, 0))
    for s in range(1, 4):
        for d in range(2):
            e1[d] = down_part(target(2 * s - 1 + d), 1)
        for d in range(2):
            k = 2 * s - 1 + d
            e0_copy(d, s - 1).wait_recv()
            if s == 1:
                rows = slice(d * HALF_1, (d + 1) * HALF_1)
                rest = slice((1 - d) * HALF_1, (2 - d) * HALF_1)
                e0_snd[d, s, rows] = (e0[k, rows] + e0_rcv[d, 0, rows].astype(F32)).astype(BF16)
                e0_snd[d, s, rest] = e0[k, rest].astype(BF16)
            else:
                e0_snd[d, s] = (e0[k] + e0_rcv[d, s - 1].astype(F32)).astype(BF16)
            start(e0_copy(d, s))
        for t, lo, n in ((1, 0, RE), (2, RE, ROWS - RE)):
            for d in range(2):
                if t == 2:
                    k = 2 * s - 1 + d
                    ey_copy(k).wait_recv()
                    e1[d, RE:ROWS] += ey_rcv[k].astype(F32)
                e1_copy(d, t, s - 1).wait_recv()
                if s == 1:
                    rows = slice(lo + d * (n // 2), lo + (d + 1) * (n // 2))
                    rest = slice(lo + (1 - d) * (n // 2), lo + (2 - d) * (n // 2))
                    e1_snd[d, s, rows] = (e1[d, rows] + e1_rcv[d, 0, rows].astype(F32)).astype(BF16)
                    e1_snd[d, s, rest] = e1[d, rest].astype(BF16)
                else:
                    rows = slice(lo, lo + n)
                    e1_snd[d, s, rows] = (e1[d, rows] + e1_rcv[d, s - 1, rows].astype(F32)).astype(BF16)
                start(e1_copy(d, t, s))
            if t == 1:
                for d in range(2):
                    if 2 * s + 1 + d < NZ:
                        other_part(2 * s + 1 + d)
    e1[0] = down_part(z, 1)
    for d in range(2):
        e0_copy(d, 3).wait_recv()
    ez_snd[...] = (e0[7] + e0_rcv[0, 3].astype(F32) + e0_rcv[1, 3].astype(F32)).astype(BF16)
    ez = rcopy(ez_snd, ez_rcv, ex_s, ex_r, ypart)
    start(ez)
    ey_copy(7).wait_recv()
    e1[0, RE:ROWS] += ey_rcv[7].astype(F32)
    for t in (1, 2):
        for d in range(2):
            e1_copy(d, t, 3).wait_recv()
    e1[0] = e1[0] + e1_rcv[0, 3].astype(F32) + e1_rcv[1, 3].astype(F32)

    def f_copy(i, cc):
        return rcopy(ret_snd.at[pl.ds(i * CAP, CAP), pl.ds(cc * FW, FW)],
                     ret_v.at[pl.ds(pl.multiple_of(b * CAP, CAP), CAP)],
                     f_s.at[i * 2 + cc], f_r.at[b], chip_dev(4 * c + i, cc))

    for i in (2, 3, 0, 1):
        rows = slice(i * CAP, (i + 1) * CAP)
        if i == 0:
            ez.wait_recv()
            e1[0, 0:RE] += ez_rcv[...].astype(F32)
        ret_snd[rows] = e1[0, rows].astype(BF16)
        for cc in range(2):
            to_self = jnp.logical_and(4 * c + i == b, cc == c)
            mine = pltpu.make_async_copy(ret_snd.at[pl.ds(i * CAP, CAP), pl.ds(cc * FW, FW)],
                                         ret_v.at[pl.ds(pl.multiple_of(b * CAP, CAP), CAP)], loc.at[7])

            @pl.when(to_self)
            def _(mine=mine):
                mine.start()
                mine.wait()

            @pl.when(jnp.logical_not(to_self))
            def _(i=i, cc=cc):
                f_copy(i, cc).start()

    for x in range(NB):
        @pl.when(jnp.logical_not(jnp.logical_and(my_src, b == x)))
        def _(x=x):
            rcopy(ret_snd.at[pl.ds(0, CAP), pl.ds(0, FW)], ret_v.at[pl.ds(x * CAP, CAP)], f_s.at[0], f_r.at[x],
                  sib).wait_recv()
    out_ref[...] = (stream[...] + jnp.dot(g_hi[...], ret_v[...], preferred_element_type=F32)
                    + jnp.dot(g_lo[...], ret_v[...], preferred_element_type=F32)).astype(BF16)

    for cp in pend:
        cp.wait_send()

    for w in range(2):
        @pl.when(jnp.logical_not((yh == c) & (c == w)))
        def _(w=w):
            for u in range(2):
                x_copy(2, w, u).wait_send()

    @pl.when(jnp.logical_not(my_src))
    def _():
        c_copy(0).wait_send()

    for i in range(4):
        for cc in range(2):
            @pl.when(jnp.logical_not(jnp.logical_and(4 * c + i == b, cc == c)))
            def _(i=i, cc=cc):
                f_copy(i, cc).wait_send()


def per_device(residual, heads_out, out_proj, norm_gain, gate_w, up_w, down_w, expert_ids, gate_slots, gate_table):
    any_, vmem = pl.BlockSpec(memory_space=pl.ANY), pl.BlockSpec(memory_space=pltpu.VMEM)
    dma, v = pltpu.SemaphoreType.DMA, pltpu.VMEM
    return pl.pallas_call(
        kernel,
        out_shape=jax.ShapeDtypeStruct((TOK, FW), BF16),
        in_specs=[any_, any_, any_, vmem, any_, any_, any_, vmem, vmem, vmem],
        out_specs=vmem,
        scratch_shapes=[
            v((TOK, FW), BF16), v((TOK, CW), BF16), v((FW, D), BF16), v((NB, 2, NZ, KR, CW), BF16),
            v((16, NZ, KR, CW), BF16), v((NZ, 2, KR, CW), BF16), v((NZ, 2, FW, CW), BF16),
            v((4, D, CW), BF16), v((2, CW, D), BF16), v((NB * CAP, TOK), BF16), v((NB * CAP, TOK), F32),
            v((TOK, NB * CAP), BF16), v((TOK, NB * CAP), BF16),
            v((2, 4, TOK, CW), BF16), v((2, 4, TOK, CW), BF16), v((2, TOK, CW), F32),
            v((TOK, CW), BF16), v((3, 2, TOK, FW), BF16),
            v((TOK, FW), F32), v((NB * CAP, FW), BF16), v((16, BLK, CW), BF16), v((4, ROWS, CW), F32),
            v((ROWS, CW), F32), v((2, ROWS, CW), BF16), v((NZ, RE, CW), F32), v((2, ROWS, CW), F32),
            v((2, 4, RE, CW), BF16), v((2, 4, RE, CW), BF16), v((2, 4, ROWS, CW), BF16), v((2, 4, ROWS, CW), BF16),
            v((NZ, ROWS - RE, CW), BF16), v((NZ, ROWS - RE, CW), BF16), v((RE, CW), BF16), v((RE, CW), BF16),
            v((ROWS, CW), BF16), v((NB * CAP, FW), BF16),
            dma((9,)), dma((3,)), dma((3,)), dma, dma, dma((5, 16)), dma((5, 16)), dma((5, 7)), dma((5, 7)),
            dma((2, 3, 2)), dma((2, 3, 2)), dma((3, 2, 2)), dma((3, 2, 2)), dma, dma,
            dma((8,)), dma((8,)), dma((2, 3, 4)), dma((2, 3, 4)), dma((10,)), dma((10,)),
            dma((2, 3, 4)), dma((2, 3, 4)), dma, dma, dma((8,)), dma((8,)), dma((8,)), dma((8,)),
        ],
        compiler_params=pltpu.CompilerParams(
            collective_id=0, has_side_effects=True, vmem_limit_bytes=60 * 1024 * 1024),
        name="merge_moe",
    )(residual, heads_out, out_proj[0], norm_gain.reshape(1, FW), gate_w[0], up_w[0], down_w[0],
      expert_ids.T, gate_slots.T, gate_table.reshape(1, SLOTS))


def solution(mesh):
    return jax.shard_map(
        per_device,
        mesh=mesh,
        in_specs=(
            P("branch", "expert"), P("branch", "expert"), P("branch", "expert", None), P("expert"),
            P("branch", None, "expert"), P("branch", None, "expert"), P("branch", "expert", None),
            P("branch", None), P("branch", None), P(),
        ),
        out_specs=P("branch", "expert"),
        check_vma=False,
    )
```

```python
import jax
import jax.numpy as jnp
from jax import lax
from jax.experimental import pallas as pl
from jax.experimental.pallas import tpu as pltpu
from jax.sharding import PartitionSpec as P

MESH = pl.DeviceIdType.MESH
F32, BF16 = jnp.float32, jnp.bfloat16
D = 4096
SLOTS = 64
NB = 8
NZ = 8
TOK = 256
CAP = 96
ROWS = 4 * CAP
GROWS = 16
BLK = ROWS + GROWS
FW = 128
CW = 256
KR = 16
GROUPS = ((0, 1), (1, 2), (3, 2), (5, 2), (7, 1))
RD = 144
RE = 160
HALF_1, HALF_2 = RE // 2, (ROWS - RE) // 2


def rcopy(src, dst, send_sem, recv_sem, dev):
    return pltpu.make_async_remote_copy(
        src_ref=src, dst_ref=dst, send_sem=send_sem, recv_sem=recv_sem,
        device_id=dev, device_id_type=MESH)


def kernel(res_hbm, heads_hbm, op_hbm, gain_ref, gate_hbm, up_hbm, down_hbm, idst_ref, slots_ref,
           table_ref, out_ref,
           res_v, heads_v, op_v, op_x, op_in, mg, merged, w4, dn, sel, gsum, g_hi, g_lo, b_snd, b_rcv, b_tot,
           x_snd, x_rcv, stream, dsp, xg, acc, sq, hid, e0, e1, e0_snd, e0_rcv, e1_snd, e1_rcv, ey_snd, ey_rcv,
           ez_snd, ez_rcv, ret_snd, ret_v,
           loc, w_s, w_r, h_s, h_r, op_s, op_r, mg_s, mg_r, b_s, b_r, x_s, x_r, g_s, g_r,
           c_s, c_r, ag_s, ag_r, agy_s, agy_r, e_s, e_r, ex_s, ex_r, ey_s, ey_r, f_s, f_r):
    b = lax.axis_index("branch")
    e = lax.axis_index("expert")
    z = e // 4
    yh = (e // 2) % 2
    c = e % 2
    half = b // 4
    sib = (b, e + 1 - 2 * c)
    right = (b, ((z + 1) % NZ) * 4 + yh * 2 + c)
    left = (b, ((z + NZ - 1) % NZ) * 4 + yh * 2 + c)
    ypart = (b, z * 4 + (1 - yh) * 2 + c)
    ydiag = (b, z * 4 + (1 - yh) * 2 + 1 - c)
    dirs = (right, left)

    def chip_dev(j, core):
        return (j, z * 4 + yh * 2 + core)

    def target(k):
        if k == 0:
            return (z + 4) % NZ
        if k == NZ - 1:
            return z
        dist = 4 - (k + 1) // 2
        return (z + dist) % NZ if k % 2 else (z + NZ - dist) % NZ

    my_cols = pl.ds(pl.multiple_of(c * FW, FW), FW)
    loads = [
        pltpu.make_async_copy(op_hbm, op_v, loc.at[2]),
        pltpu.make_async_copy(heads_hbm, heads_v.at[:, my_cols], loc.at[1]),
        pltpu.make_async_copy(res_hbm, res_v, loc.at[0]),
        pltpu.make_async_copy(gate_hbm, w4.at[0], loc.at[3]),
        pltpu.make_async_copy(up_hbm, w4.at[2], loc.at[4]),
        pltpu.make_async_copy(down_hbm, dn.at[0], loc.at[5]),
    ]
    for ld in loads:
        ld.start()

    barrier = pltpu.get_barrier_semaphore()
    for kb in range(NB):
        for kc in range(2):
            if kb or kc:
                pl.semaphore_signal(barrier, inc=1, device_id=chip_dev((b + kb) % NB, (c + kc) % 2),
                                    device_id_type=MESH)
    ring_devs = [(b, ((z + dz) % NZ) * 4 + i) for dz in (1, NZ - 1) for i in range(4)]
    for dev in ring_devs + [ypart, ydiag]:
        pl.semaphore_signal(barrier, inc=1, device_id=dev, device_id_type=MESH)

    loads[0].wait()
    for k in range(NZ):
        for cc in range(2):
            cols = pl.ds(pl.multiple_of(target(k) * 2 * CW + cc * CW, CW), CW)
            op_x[:, cc, k] = op_v[:, cols].reshape(NB, KR, CW)
    op_in[b * 2 + c] = op_x[b, c]
    pl.semaphore_wait(barrier, 25)

    pend = []

    def start(cp):
        cp.start()
        pend.append(cp)

    def drain():
        for cp in pend:
            cp.wait_send()
        pend.clear()

    def op_send(i):
        q, n = GROUPS[i]
        for kb in range(NB):
            for kc in range(2):
                if kb or kc:
                    j, cc = (b + kb) % NB, (c + kc) % 2
                    start(rcopy(op_x.at[j, cc, pl.ds(q, n)], op_in.at[b * 2 + c, pl.ds(q, n)],
                                op_s.at[i, kb * 2 + kc], op_r.at[i, kb * 2 + kc], chip_dev(j, cc)))

    def mg_copy(i, k, j):
        q, n = GROUPS[i]
        return rcopy(mg.at[pl.ds(q, n)], merged.at[pl.ds(q, n), :, pl.ds(pl.multiple_of(j * KR, KR), KR)],
                     mg_s.at[i, k - 1], mg_r.at[i, k - 1], chip_dev((b + k) % NB, c))

    def merge(i):
        q, n = GROUPS[i]
        for kb in range(NB):
            for kc in range(2):
                if kb or kc:
                    rcopy(op_x.at[0, 0, pl.ds(q, n)],
                          op_in.at[((b + NB - kb) % NB) * 2 + (c + kc) % 2, pl.ds(q, n)],
                          op_s.at[i, kb * 2 + kc], op_r.at[i, kb * 2 + kc], sib).wait_recv()
        for k in range(q, q + n):
            for cc in range(2):
                total = op_in[cc, k].astype(F32)
                for j in range(1, NB):
                    total = total + op_in[j * 2 + cc, k].astype(F32)
                total = (total / NB).astype(BF16)
                mg[k, cc] = total
                merged[k, cc, pl.ds(pl.multiple_of(b * KR, KR), KR)] = total
        for k in range(1, NB):
            start(mg_copy(i, k, b))

    def merged_wait(i):
        for k in range(1, NB):
            mg_copy(i, k, (b + NB - k) % NB).wait_recv()

    op_send(0)
    start(rcopy(heads_hbm, heads_v.at[:, my_cols], h_s, h_r, sib))
    op_send(1)
    for i, (src, dst) in enumerate(((gate_hbm, w4.at[1]), (up_hbm, w4.at[3]), (down_hbm, dn.at[1]))):
        cp = rcopy(src, dst, w_s.at[i], w_r.at[i], sib)
        cp.start()
        pend.append(cp)

    me = z * 2 + yh
    gain_at = (me, pl.ds(ROWS, GROWS), pl.ds(pl.multiple_of(c * FW, FW), FW))
    xg[gain_at] = jnp.broadcast_to(gain_ref[...], (GROWS, FW))
    gain_cp = rcopy(xg.at[gain_at], xg.at[gain_at], g_s, g_r, sib)
    gain_cp.start()
    pend.append(gain_cp)

    ids = idst_ref[...]
    xi = lax.broadcasted_iota(jnp.int32, (16, TOK), 0)
    named = ((ids[0:1] == xi) | (ids[1:2] == xi)).astype(BF16)
    before = (lax.broadcasted_iota(jnp.int32, (TOK, TOK), 0)
              < lax.broadcasted_iota(jnp.int32, (TOK, TOK), 1)).astype(BF16)
    rank = jnp.dot(named, before, preferred_element_type=F32).astype(jnp.int32)
    ci = lax.broadcasted_iota(jnp.int32, (CAP, TOK), 0)
    eye = lax.broadcasted_iota(jnp.int32, (SLOTS, SLOTS), 0) == lax.broadcasted_iota(jnp.int32, (SLOTS, SLOTS), 1)
    table = jnp.sum(jnp.where(eye, table_ref[...], 0.0), axis=1, keepdims=True)
    slot_i = lax.broadcasted_iota(jnp.int32, (SLOTS, TOK), 0)
    raw = [jnp.sum(jnp.where(slots_ref[k:k + 1] == slot_i, table, 0.0), axis=0, keepdims=True) for k in range(2)]
    gates = [raw[k] / (raw[0] + raw[1]) for k in range(2)]
    for x in range(NB):
        hit = rank[x:x + 1] == ci
        first, second = hit & (ids[0:1] == x), hit & (ids[1:2] == x)
        sel[x * CAP:(x + 1) * CAP] = (first | second).astype(BF16)
        gsum[x * CAP:(x + 1) * CAP] = jnp.where(first, gates[0], 0.0) + jnp.where(second, gates[1], 0.0)
    gt = gsum[...].T
    hi = gt.astype(BF16)
    g_hi[...] = hi
    g_lo[...] = (gt - hi.astype(F32)).astype(BF16)
    acc[...] = jnp.zeros_like(acc)
    sq[...] = jnp.zeros_like(sq)

    def attn_part(k):
        return jnp.dot(heads_v[...], merged[k].reshape(CW, CW), preferred_element_type=F32)

    def b_rows(d, u):
        return pl.ds(((d + u) % 2) * 128, 128)

    def b_copy(d, s, u):
        rows = b_rows(d, u)
        return rcopy(b_snd.at[d, s, rows], b_rcv.at[d, s, rows], b_s.at[d, s, u], b_r.at[d, s, u], dirs[d])

    def x_copy(kind, w, u):
        rows = pl.ds(u * 128, 128) if kind == 2 else b_rows(kind, u)
        src = x_snd.at[rows, pl.ds(w * FW, FW)] if kind == 2 else b_snd.at[kind, 3, rows, pl.ds(w * FW, FW)]
        zt = ((z + 1) % NZ, (z + NZ - 1) % NZ, z)[kind]
        return rcopy(src, x_rcv.at[kind, yh, rows], x_s.at[kind, w, u], x_r.at[kind, yh, u],
                     (b, zt * 4 + c * 2 + w))

    def x_wait(kind, ys, u):
        rows = pl.ds(u * 128, 128) if kind == 2 else b_rows(kind, u)
        ref = x_rcv.at[kind, ys, rows]
        rcopy(ref, ref, x_s.at[0, 0, 0], x_r.at[kind, ys, u], sib).wait_recv()

    def b_step(s):
        for d in range(2):
            b_tot[d] = attn_part(2 * s - 1 + d)
        for u in range(2):
            for d in range(2):
                rows = b_rows(d, u)
                if s > 1 or u == 0:
                    b_copy(d, s - 1, u).wait_recv()
                    b_snd[d, s, rows] = (b_tot[d, rows] + b_rcv[d, s - 1, rows].astype(F32)).astype(BF16)
                else:
                    b_snd[d, s, rows] = b_tot[d, rows].astype(BF16)
                if s < 3:
                    start(b_copy(d, s, u))
                else:
                    for w in range(2):
                        start(x_copy(d, w, u))

    merge(0)
    op_send(2)
    merge(1)
    op_send(3)
    loads[1].wait()
    their_cols = heads_v.at[:, pl.ds(pl.multiple_of((1 - c) * FW, FW), FW)]
    rcopy(their_cols, their_cols, h_s, h_r, sib).wait_recv()
    merged_wait(0)
    p = attn_part(0)
    for d in range(2):
        b_snd[d, 0, b_rows(d, 0)] = p[d * 128:(d + 1) * 128].astype(BF16)
        start(b_copy(d, 0, 0))
    merge(2)
    op_send(4)
    merged_wait(1)
    b_step(1)
    merge(3)
    merged_wait(2)
    b_step(2)
    merge(4)
    merged_wait(3)
    b_step(3)
    merged_wait(4)
    x_snd[...] = attn_part(NZ - 1).astype(BF16)
    for u in range(2):
        for w in range(2):
            keep = (yh == c) & (c == w)

            @pl.when(keep)
            def _(u=u, w=w):
                x_rcv[2, yh, u * 128:(u + 1) * 128] = x_snd[u * 128:(u + 1) * 128, w * FW:(w + 1) * FW]

            @pl.when(jnp.logical_not(keep))
            def _(u=u, w=w):
                x_copy(2, w, u).start()

    for u in range(2):
        for kind in range(2):
            for ys in range(2):
                x_wait(kind, ys, u)
    for ys in range(2):
        @pl.when(jnp.logical_not((yh == c) & (yh == ys)))
        def _(ys=ys):
            for u in range(2):
                x_wait(2, ys, u)

    loads[2].wait()
    attn = x_rcv[0, 0].astype(F32)
    for i in range(1, 6):
        attn = attn + x_rcv[i // 2, i % 2].astype(F32)
    st = res_v[...].astype(F32) + attn
    stream[...] = st
    scaled = (st * gain_ref[...].astype(F32)).astype(BF16)
    dsp[...] = jnp.dot(sel[...], scaled, preferred_element_type=F32).astype(BF16)
    blk_at = (me, pl.ds(pl.multiple_of((b % 4) * CAP, CAP), CAP), pl.ds(pl.multiple_of(c * FW, FW), FW))
    my_src = half == c

    def c_copy(k):
        x = (b + k) % NB
        return rcopy(dsp.at[pl.ds(pl.multiple_of(x * CAP, CAP), CAP)], xg.at[blk_at], c_s.at[k],
                     c_r.at[(b % 4) * 2 + c], chip_dev(x, half))

    own_blk = pltpu.make_async_copy(dsp.at[pl.ds(pl.multiple_of(b * CAP, CAP), CAP)], xg.at[blk_at], loc.at[6])
    for k in range(1, NB):
        c_copy(k).start()
        pend.append(c_copy(k))

    @pl.when(my_src)
    def _():
        own_blk.start()

    @pl.when(jnp.logical_not(my_src))
    def _():
        c_copy(0).start()

    for i in range(8):
        @pl.when(jnp.logical_not(jnp.logical_and(my_src, (b % 4) * 2 + c == i)))
        def _(i=i):
            rcopy(dsp.at[pl.ds(0, CAP)], xg.at[me, pl.ds((i // 2) * CAP, CAP), pl.ds((i % 2) * FW, FW)],
                  c_s.at[0], c_r.at[i], sib).wait_recv()

    @pl.when(my_src)
    def _():
        own_blk.wait()

    sib_gain = xg.at[me, pl.ds(ROWS, GROWS), pl.ds(pl.multiple_of((1 - c) * FW, FW), FW)]
    rcopy(sib_gain, sib_gain, g_s, g_r, sib).wait_recv()

    def ag_copy(d, t, s, slot):
        lo, n = (RD, BLK - RD) if t == 0 else (0, RD)
        if s == 3:
            cut = n // 32 * 16
            lo, n = (lo, cut) if d == 0 else (lo + cut, n - cut)
        ref = xg.at[slot, pl.ds(lo, n)]
        return rcopy(ref, ref, ag_s.at[d, t, s], ag_r.at[d, t, s], dirs[d])

    def agy_copy(i, slot):
        if i == 0:
            lo, n = 0, RD
        elif i < 8:
            lo, n = RD, BLK - RD
        else:
            cut = (BLK - RD) // 32 * 16
            lo, n = (RD, cut) if i == 8 else (RD + cut, BLK - RD - cut)
        ref = xg.at[slot, pl.ds(lo, n)]
        return rcopy(ref, ref, agy_s.at[i], agy_r.at[i], ypart)

    def gate_up(slot):
        blk = xg[slot, 0:ROWS]
        inv = 1.0 / xg[slot, ROWS:BLK][0:1].astype(F32)
        v = blk.astype(F32) * inv
        sq[...] += v * v
        rows = pl.ds(pl.multiple_of(slot * CW, CW), CW)

        def part(i, carry):
            acc[i] += jnp.dot(xg[slot, 0:ROWS], w4[i, rows, :], preferred_element_type=F32)
            return carry
        lax.fori_loop(0, 4, part, 0)

    def slot_of(d, s, t):
        return ((z + NZ - s) % NZ if d == 0 else (z + s) % NZ) * 2 + (yh if t == 0 else 1 - yh)

    other = z * 2 + 1 - yh
    start(agy_copy(0, me))
    for t in range(2):
        for d in range(2):
            start(ag_copy(d, t, 0, me))
        if t == 0:
            start(agy_copy(1, me))
    loads[3].wait()
    loads[4].wait()
    for i in range(2):
        rcopy(gate_hbm, w4.at[1 + 2 * i], w_s.at[i], w_r.at[i], sib).wait_recv()
    drain_a, pend[:] = pend[:-9], pend[-9:]
    for cp in drain_a:
        cp.wait_send()
    gate_up(me)
    agy_copy(0, other).wait_recv()
    for d in range(2):
        start(ag_copy(d, 2, 0, other))
    for s in range(1, 4):
        for t in range(2):
            for d in range(2):
                slot = slot_of(d, s, 0)
                ag_copy(d, t, s - 1, slot).wait_recv()
                start(ag_copy(d, t, s, slot))
                if t == 0:
                    start(agy_copy(2 * s + d, slot))
        gate_up(slot_of(0, s, 0))
        for d in range(2):
            slot = slot_of(d, s, 1)
            ag_copy(d, 2, s - 1, slot).wait_recv()
            start(ag_copy(d, 2, s, slot))
        gate_up(slot_of(1, s, 0))
        if s == 1:
            agy_copy(1, other).wait_recv()
            gate_up(other)
        else:
            for d in range(2):
                slot = slot_of(d, s - 1, 1)
                agy_copy(2 * (s - 1) + d, slot).wait_recv()
                gate_up(slot)
    far = slot_of(0, 4, 0)
    for d in range(2):
        ag_copy(d, 0, 3, far).wait_recv()
        start(agy_copy(8 + d, far))
    for d in range(2):
        ag_copy(d, 1, 3, far).wait_recv()
    gate_up(far)
    for d in range(2):
        slot = slot_of(d, 3, 1)
        agy_copy(6 + d, slot).wait_recv()
        gate_up(slot)
    far = slot_of(0, 4, 1)
    for d in range(2):
        ag_copy(d, 2, 3, far).wait_recv()
        agy_copy(8 + d, far).wait_recv()
    gate_up(far)

    scale = lax.rsqrt(jnp.sum(sq[...], axis=1, keepdims=True) / D + 1e-05)
    for i in range(2):
        g = acc[i] * scale
        hid[i] = (g / (1.0 + jnp.exp(-g)) * (acc[2 + i] * scale)).astype(BF16)
    loads[5].wait()
    rcopy(down_hbm, dn.at[1], w_s.at[2], w_r.at[2], sib).wait_recv()

    def down_part(zd, t):
        yy = 1 - yh if t == 0 else yh
        cols = pl.ds(pl.multiple_of((zd * 2 + yy) * CW, CW), CW)
        return (jnp.dot(hid[0], dn[0, :, cols], preferred_element_type=F32)
                + jnp.dot(hid[1], dn[1, :, cols], preferred_element_type=F32))

    def ey_copy(k):
        return rcopy(ey_snd.at[k], ey_rcv.at[k], ey_s.at[k], ey_r.at[k], ypart)

    def e0_copy(d, s):
        rows = pl.ds(d * HALF_1, HALF_1) if s == 0 else pl.ds(0, RE)
        return rcopy(e0_snd.at[d, s, rows], e0_rcv.at[d, s, rows], e_s.at[d, 0, s], e_r.at[d, 0, s], dirs[d])

    def e1_copy(d, t, s):
        lo, n = (0, RE) if t == 1 else (RE, ROWS - RE)
        rows = pl.ds(lo + d * (n // 2), n // 2) if s == 0 else pl.ds(lo, n)
        return rcopy(e1_snd.at[d, s, rows], e1_rcv.at[d, s, rows], e_s.at[d, t, s], e_r.at[d, t, s], dirs[d])

    def other_part(k):
        p = down_part(target(k), 0)
        ey_snd[k] = p[RE:ROWS].astype(BF16)
        start(ey_copy(k))
        e0[k] = p[0:RE]

    other_part(0)
    for d in range(2):
        rows = slice(d * HALF_1, (d + 1) * HALF_1)
        e0_snd[d, 0, rows] = e0[0, rows].astype(BF16)
        start(e0_copy(d, 0))
    e1[0] = down_part(target(0), 1)
    for d in range(2):
        rows = slice(d * HALF_1, (d + 1) * HALF_1)
        e1_snd[d, 0, rows] = e1[0, rows].astype(BF16)
        start(e1_copy(d, 1, 0))
    other_part(1)
    other_part(2)
    ey_copy(0).wait_recv()
    for d in range(2):
        rows = slice(RE + d * HALF_2, RE + (d + 1) * HALF_2)
        e1_snd[d, 0, rows] = (e1[0, rows] + ey_rcv[0, d * HALF_2:(d + 1) * HALF_2].astype(F32)).astype(BF16)
        start(e1_copy(d, 2, 0))
    for s in range(1, 4):
        for d in range(2):
            e1[d] = down_part(target(2 * s - 1 + d), 1)
        for d in range(2):
            k = 2 * s - 1 + d
            e0_copy(d, s - 1).wait_recv()
            if s == 1:
                rows = slice(d * HALF_1, (d + 1) * HALF_1)
                rest = slice((1 - d) * HALF_1, (2 - d) * HALF_1)
                e0_snd[d, s, rows] = (e0[k, rows] + e0_rcv[d, 0, rows].astype(F32)).astype(BF16)
                e0_snd[d, s, rest] = e0[k, rest].astype(BF16)
            else:
                e0_snd[d, s] = (e0[k] + e0_rcv[d, s - 1].astype(F32)).astype(BF16)
            start(e0_copy(d, s))
        for t, lo, n in ((1, 0, RE), (2, RE, ROWS - RE)):
            for d in range(2):
                if t == 2:
                    k = 2 * s - 1 + d
                    ey_copy(k).wait_recv()
                    e1[d, RE:ROWS] += ey_rcv[k].astype(F32)
                e1_copy(d, t, s - 1).wait_recv()
                if s == 1:
                    rows = slice(lo + d * (n // 2), lo + (d + 1) * (n // 2))
                    rest = slice(lo + (1 - d) * (n // 2), lo + (2 - d) * (n // 2))
                    e1_snd[d, s, rows] = (e1[d, rows] + e1_rcv[d, 0, rows].astype(F32)).astype(BF16)
                    e1_snd[d, s, rest] = e1[d, rest].astype(BF16)
                else:
                    rows = slice(lo, lo + n)
                    e1_snd[d, s, rows] = (e1[d, rows] + e1_rcv[d, s - 1, rows].astype(F32)).astype(BF16)
                start(e1_copy(d, t, s))
            if t == 1:
                for d in range(2):
                    if 2 * s + 1 + d < NZ:
                        other_part(2 * s + 1 + d)
    drain_e, pend[:] = pend[:-6], pend[-6:]
    for cp in drain_e:
        cp.wait_send()
    e1[0] = down_part(z, 1)
    for d in range(2):
        e0_copy(d, 3).wait_recv()
    ez_snd[...] = (e0[7] + e0_rcv[0, 3].astype(F32) + e0_rcv[1, 3].astype(F32)).astype(BF16)
    ez = rcopy(ez_snd, ez_rcv, ex_s, ex_r, ypart)
    start(ez)
    ey_copy(7).wait_recv()
    e1[0, RE:ROWS] += ey_rcv[7].astype(F32)
    for t in (1, 2):
        for d in range(2):
            e1_copy(d, t, 3).wait_recv()
    e1[0] = e1[0] + e1_rcv[0, 3].astype(F32) + e1_rcv[1, 3].astype(F32)

    def f_copy(i, cc):
        return rcopy(ret_snd.at[pl.ds(i * CAP, CAP), pl.ds(cc * FW, FW)],
                     ret_v.at[pl.ds(pl.multiple_of(b * CAP, CAP), CAP)],
                     f_s.at[i * 2 + cc], f_r.at[b], chip_dev(4 * c + i, cc))

    for i in (2, 3, 0, 1):
        rows = slice(i * CAP, (i + 1) * CAP)
        if i == 0:
            ez.wait_recv()
            e1[0, 0:RE] += ez_rcv[...].astype(F32)
        ret_snd[rows] = e1[0, rows].astype(BF16)
        for cc in range(2):
            to_self = jnp.logical_and(4 * c + i == b, cc == c)
            mine = pltpu.make_async_copy(ret_snd.at[pl.ds(i * CAP, CAP), pl.ds(cc * FW, FW)],
                                         ret_v.at[pl.ds(pl.multiple_of(b * CAP, CAP), CAP)], loc.at[7])

            @pl.when(to_self)
            def _(mine=mine):
                mine.start()
                mine.wait()

            @pl.when(jnp.logical_not(to_self))
            def _(i=i, cc=cc):
                f_copy(i, cc).start()

    drain()
    for x in range(NB):
        @pl.when(jnp.logical_not(jnp.logical_and(my_src, b == x)))
        def _(x=x):
            rcopy(ret_snd.at[pl.ds(0, CAP), pl.ds(0, FW)], ret_v.at[pl.ds(x * CAP, CAP)], f_s.at[0], f_r.at[x],
                  sib).wait_recv()
    out_ref[...] = (stream[...] + jnp.dot(g_hi[...], ret_v[...], preferred_element_type=F32)
                    + jnp.dot(g_lo[...], ret_v[...], preferred_element_type=F32)).astype(BF16)

    for w in range(2):
        @pl.when(jnp.logical_not((yh == c) & (c == w)))
        def _(w=w):
            for u in range(2):
                x_copy(2, w, u).wait_send()

    @pl.when(jnp.logical_not(my_src))
    def _():
        c_copy(0).wait_send()

    for i in range(4):
        for cc in range(2):
            @pl.when(jnp.logical_not(jnp.logical_and(4 * c + i == b, cc == c)))
            def _(i=i, cc=cc):
                f_copy(i, cc).wait_send()


def per_device(residual, heads_out, out_proj, norm_gain, gate_w, up_w, down_w, expert_ids, gate_slots, gate_table):
    any_, vmem = pl.BlockSpec(memory_space=pl.ANY), pl.BlockSpec(memory_space=pltpu.VMEM)
    dma, v = pltpu.SemaphoreType.DMA, pltpu.VMEM
    return pl.pallas_call(
        kernel,
        out_shape=jax.ShapeDtypeStruct((TOK, FW), BF16),
        in_specs=[any_, any_, any_, vmem, any_, any_, any_, vmem, vmem, vmem],
        out_specs=vmem,
        scratch_shapes=[
            v((TOK, FW), BF16), v((TOK, CW), BF16), v((FW, D), BF16), v((NB, 2, NZ, KR, CW), BF16),
            v((16, NZ, KR, CW), BF16), v((NZ, 2, KR, CW), BF16), v((NZ, 2, FW, CW), BF16),
            v((4, D, CW), BF16), v((2, CW, D), BF16), v((NB * CAP, TOK), BF16), v((NB * CAP, TOK), F32),
            v((TOK, NB * CAP), BF16), v((TOK, NB * CAP), BF16),
            v((2, 4, TOK, CW), BF16), v((2, 4, TOK, CW), BF16), v((2, TOK, CW), F32),
            v((TOK, CW), BF16), v((3, 2, TOK, FW), BF16),
            v((TOK, FW), F32), v((NB * CAP, FW), BF16), v((16, BLK, CW), BF16), v((4, ROWS, CW), F32),
            v((ROWS, CW), F32), v((2, ROWS, CW), BF16), v((NZ, RE, CW), F32), v((2, ROWS, CW), F32),
            v((2, 4, RE, CW), BF16), v((2, 4, RE, CW), BF16), v((2, 4, ROWS, CW), BF16), v((2, 4, ROWS, CW), BF16),
            v((NZ, ROWS - RE, CW), BF16), v((NZ, ROWS - RE, CW), BF16), v((RE, CW), BF16), v((RE, CW), BF16),
            v((ROWS, CW), BF16), v((NB * CAP, FW), BF16),
            dma((9,)), dma((3,)), dma((3,)), dma, dma, dma((5, 16)), dma((5, 16)), dma((5, 7)), dma((5, 7)),
            dma((2, 3, 2)), dma((2, 3, 2)), dma((3, 2, 2)), dma((3, 2, 2)), dma, dma,
            dma((8,)), dma((8,)), dma((2, 3, 4)), dma((2, 3, 4)), dma((10,)), dma((10,)),
            dma((2, 3, 4)), dma((2, 3, 4)), dma, dma, dma((8,)), dma((8,)), dma((8,)), dma((8,)),
        ],
        compiler_params=pltpu.CompilerParams(
            collective_id=0, has_side_effects=True, vmem_limit_bytes=60 * 1024 * 1024),
        name="merge_moe",
    )(residual, heads_out, out_proj[0], norm_gain.reshape(1, FW), gate_w[0], up_w[0], down_w[0],
      expert_ids.T, gate_slots.T, gate_table.reshape(1, SLOTS))


def solution(mesh):
    return jax.shard_map(
        per_device,
        mesh=mesh,
        in_specs=(
            P("branch", "expert"), P("branch", "expert"), P("branch", "expert", None), P("expert"),
            P("branch", None, "expert"), P("branch", None, "expert"), P("branch", "expert", None),
            P("branch", None), P("branch", None), P(),
        ),
        out_specs=P("branch", "expert"),
        check_vma=False,
    )
```

```python
import jax
import jax.numpy as jnp
from jax import lax
from jax.experimental import pallas as pl
from jax.experimental.pallas import tpu as pltpu
from jax.sharding import PartitionSpec as P

MESH = pl.DeviceIdType.MESH
F32, BF16 = jnp.float32, jnp.bfloat16
D = 4096
SLOTS = 64
NB = 8
NZ = 8
TOK = 256
CAP = 96
ROWS = 4 * CAP
GROWS = 16
BLK = ROWS + GROWS
FW = 128
CW = 256
KR = 16
GROUPS = ((0, 1), (1, 2), (3, 2), (5, 2), (7, 1))
RD = 144
RE = 160
HALF_1, HALF_2 = RE // 2, (ROWS - RE) // 2


def rcopy(src, dst, send_sem, recv_sem, dev):
    return pltpu.make_async_remote_copy(
        src_ref=src, dst_ref=dst, send_sem=send_sem, recv_sem=recv_sem,
        device_id=dev, device_id_type=MESH)


def kernel(res_hbm, heads_hbm, op_hbm, gain_ref, gate_hbm, up_hbm, down_hbm, idst_ref, slots_ref,
           table_ref, out_ref,
           res_v, heads_v, op_v, op_x, op_in, mg, merged, w4, dn, sel, gsum, g_hi, g_lo, b_snd, b_rcv, b_tot,
           x_snd, x_rcv, stream, dsp, xg, acc, sq, hid, e0, e1, e0_snd, e0_rcv, e1_snd, e1_rcv, ey_snd, ey_rcv,
           ez_snd, ez_rcv, ret_snd, ret_v,
           loc, w_s, w_r, h_s, h_r, op_s, op_r, mg_s, mg_r, b_s, b_r, x_s, x_r, g_s, g_r,
           c_s, c_r, ag_s, ag_r, agy_s, agy_r, e_s, e_r, ex_s, ex_r, ey_s, ey_r, f_s, f_r):
    b = lax.axis_index("branch")
    e = lax.axis_index("expert")
    z = e // 4
    yh = (e // 2) % 2
    c = e % 2
    half = b // 4
    sib = (b, e + 1 - 2 * c)
    right = (b, ((z + 1) % NZ) * 4 + yh * 2 + c)
    left = (b, ((z + NZ - 1) % NZ) * 4 + yh * 2 + c)
    ypart = (b, z * 4 + (1 - yh) * 2 + c)
    ydiag = (b, z * 4 + (1 - yh) * 2 + 1 - c)
    dirs = (right, left)

    def chip_dev(j, core):
        return (j, z * 4 + yh * 2 + core)

    def target(k):
        if k == 0:
            return (z + 4) % NZ
        if k == NZ - 1:
            return z
        dist = 4 - (k + 1) // 2
        return (z + dist) % NZ if k % 2 else (z + NZ - dist) % NZ

    my_cols = pl.ds(pl.multiple_of(c * FW, FW), FW)
    loads = [
        pltpu.make_async_copy(op_hbm, op_v, loc.at[2]),
        pltpu.make_async_copy(heads_hbm, heads_v.at[:, my_cols], loc.at[1]),
        pltpu.make_async_copy(res_hbm, res_v, loc.at[0]),
        pltpu.make_async_copy(gate_hbm, w4.at[0], loc.at[3]),
        pltpu.make_async_copy(up_hbm, w4.at[2], loc.at[4]),
        pltpu.make_async_copy(down_hbm, dn.at[0], loc.at[5]),
    ]
    for ld in loads:
        ld.start()

    barrier = pltpu.get_barrier_semaphore()
    for kb in range(NB):
        for kc in range(2):
            if kb or kc:
                pl.semaphore_signal(barrier, inc=1, device_id=chip_dev((b + kb) % NB, (c + kc) % 2),
                                    device_id_type=MESH)
    ring_devs = [(b, ((z + dz) % NZ) * 4 + i) for dz in (1, NZ - 1) for i in range(4)]
    for dev in ring_devs + [ypart, ydiag]:
        pl.semaphore_signal(barrier, inc=1, device_id=dev, device_id_type=MESH)

    loads[0].wait()
    for k in range(NZ):
        for cc in range(2):
            cols = pl.ds(pl.multiple_of(target(k) * 2 * CW + cc * CW, CW), CW)
            op_x[:, cc, k] = op_v[:, cols].reshape(NB, KR, CW)
    op_in[b * 2 + c] = op_x[b, c]
    pl.semaphore_wait(barrier, 25)

    pend = []

    def start(cp):
        cp.start()
        pend.append(cp)

    def drain():
        for cp in pend:
            cp.wait_send()
        pend.clear()

    def op_send(i):
        q, n = GROUPS[i]
        for kb in range(NB):
            for kc in range(2):
                if kb or kc:
                    j, cc = (b + kb) % NB, (c + kc) % 2
                    start(rcopy(op_x.at[j, cc, pl.ds(q, n)], op_in.at[b * 2 + c, pl.ds(q, n)],
                                op_s.at[i, kb * 2 + kc], op_r.at[i, kb * 2 + kc], chip_dev(j, cc)))

    def mg_copy(i, k, j):
        q, n = GROUPS[i]
        return rcopy(mg.at[pl.ds(q, n)], merged.at[pl.ds(q, n), :, pl.ds(pl.multiple_of(j * KR, KR), KR)],
                     mg_s.at[i, k - 1], mg_r.at[i, k - 1], chip_dev((b + k) % NB, c))

    def merge(i):
        q, n = GROUPS[i]
        for kb in range(NB):
            for kc in range(2):
                if kb or kc:
                    rcopy(op_x.at[0, 0, pl.ds(q, n)],
                          op_in.at[((b + NB - kb) % NB) * 2 + (c + kc) % 2, pl.ds(q, n)],
                          op_s.at[i, kb * 2 + kc], op_r.at[i, kb * 2 + kc], sib).wait_recv()
        for k in range(q, q + n):
            for cc in range(2):
                total = op_in[cc, k].astype(F32)
                for j in range(1, NB):
                    total = total + op_in[j * 2 + cc, k].astype(F32)
                total = (total / NB).astype(BF16)
                mg[k, cc] = total
                merged[k, cc, pl.ds(pl.multiple_of(b * KR, KR), KR)] = total
        for k in range(1, NB):
            start(mg_copy(i, k, b))

    def merged_wait(i):
        for k in range(1, NB):
            mg_copy(i, k, (b + NB - k) % NB).wait_recv()

    op_send(0)
    start(rcopy(heads_hbm, heads_v.at[:, my_cols], h_s, h_r, sib))
    op_send(1)
    for i, (src, dst) in enumerate(((gate_hbm, w4.at[1]), (up_hbm, w4.at[3]), (down_hbm, dn.at[1]))):
        cp = rcopy(src, dst, w_s.at[i], w_r.at[i], sib)
        cp.start()
        pend.append(cp)

    me = z * 2 + yh
    gain_at = (me, pl.ds(ROWS, GROWS), pl.ds(pl.multiple_of(c * FW, FW), FW))
    xg[gain_at] = jnp.broadcast_to(gain_ref[...], (GROWS, FW))
    gain_cp = rcopy(xg.at[gain_at], xg.at[gain_at], g_s, g_r, sib)
    gain_cp.start()
    pend.append(gain_cp)

    ids = idst_ref[...]
    xi = lax.broadcasted_iota(jnp.int32, (16, TOK), 0)
    named = ((ids[0:1] == xi) | (ids[1:2] == xi)).astype(BF16)
    before = (lax.broadcasted_iota(jnp.int32, (TOK, TOK), 0)
              < lax.broadcasted_iota(jnp.int32, (TOK, TOK), 1)).astype(BF16)
    rank = jnp.dot(named, before, preferred_element_type=F32).astype(jnp.int32)
    ci = lax.broadcasted_iota(jnp.int32, (CAP, TOK), 0)
    eye = lax.broadcasted_iota(jnp.int32, (SLOTS, SLOTS), 0) == lax.broadcasted_iota(jnp.int32, (SLOTS, SLOTS), 1)
    table = jnp.sum(jnp.where(eye, table_ref[...], 0.0), axis=1, keepdims=True)
    slot_i = lax.broadcasted_iota(jnp.int32, (SLOTS, TOK), 0)
    raw = [jnp.sum(jnp.where(slots_ref[k:k + 1] == slot_i, table, 0.0), axis=0, keepdims=True) for k in range(2)]
    gates = [raw[k] / (raw[0] + raw[1]) for k in range(2)]
    for x in range(NB):
        hit = rank[x:x + 1] == ci
        first, second = hit & (ids[0:1] == x), hit & (ids[1:2] == x)
        sel[x * CAP:(x + 1) * CAP] = (first | second).astype(BF16)
        gsum[x * CAP:(x + 1) * CAP] = jnp.where(first, gates[0], 0.0) + jnp.where(second, gates[1], 0.0)

    def attn_part(k):
        return jnp.dot(heads_v[...], merged[k].reshape(CW, CW), preferred_element_type=F32)

    def b_rows(d, u):
        return pl.ds(((d + u) % 2) * 128, 128)

    def b_copy(d, s, u):
        rows = b_rows(d, u)
        return rcopy(b_snd.at[d, s, rows], b_rcv.at[d, s, rows], b_s.at[d, s, u], b_r.at[d, s, u], dirs[d])

    def x_copy(kind, w, u):
        rows = pl.ds(u * 128, 128) if kind == 2 else b_rows(kind, u)
        src = x_snd.at[rows, pl.ds(w * FW, FW)] if kind == 2 else b_snd.at[kind, 3, rows, pl.ds(w * FW, FW)]
        zt = ((z + 1) % NZ, (z + NZ - 1) % NZ, z)[kind]
        return rcopy(src, x_rcv.at[kind, yh, rows], x_s.at[kind, w, u], x_r.at[kind, yh, u],
                     (b, zt * 4 + c * 2 + w))

    def x_wait(kind, ys, u):
        rows = pl.ds(u * 128, 128) if kind == 2 else b_rows(kind, u)
        ref = x_rcv.at[kind, ys, rows]
        rcopy(ref, ref, x_s.at[0, 0, 0], x_r.at[kind, ys, u], sib).wait_recv()

    def b_step(s):
        for d in range(2):
            b_tot[d] = attn_part(2 * s - 1 + d)
        for u in range(2):
            for d in range(2):
                rows = b_rows(d, u)
                if s > 1 or u == 0:
                    b_copy(d, s - 1, u).wait_recv()
                    b_snd[d, s, rows] = (b_tot[d, rows] + b_rcv[d, s - 1, rows].astype(F32)).astype(BF16)
                else:
                    b_snd[d, s, rows] = b_tot[d, rows].astype(BF16)
                if s < 3:
                    start(b_copy(d, s, u))
                else:
                    for w in range(2):
                        start(x_copy(d, w, u))

    merge(0)
    op_send(2)
    merge(1)
    op_send(3)
    loads[1].wait()
    their_cols = heads_v.at[:, pl.ds(pl.multiple_of((1 - c) * FW, FW), FW)]
    rcopy(their_cols, their_cols, h_s, h_r, sib).wait_recv()
    merged_wait(0)
    p = attn_part(0)
    for d in range(2):
        b_snd[d, 0, b_rows(d, 0)] = p[d * 128:(d + 1) * 128].astype(BF16)
        start(b_copy(d, 0, 0))
    merge(2)
    op_send(4)
    merged_wait(1)
    b_step(1)
    merge(3)
    merged_wait(2)
    b_step(2)
    merge(4)
    merged_wait(3)
    b_step(3)
    merged_wait(4)
    x_snd[...] = attn_part(NZ - 1).astype(BF16)
    for u in range(2):
        for w in range(2):
            keep = (yh == c) & (c == w)

            @pl.when(keep)
            def _(u=u, w=w):
                x_rcv[2, yh, u * 128:(u + 1) * 128] = x_snd[u * 128:(u + 1) * 128, w * FW:(w + 1) * FW]

            @pl.when(jnp.logical_not(keep))
            def _(u=u, w=w):
                x_copy(2, w, u).start()

    for u in range(2):
        for kind in range(2):
            for ys in range(2):
                x_wait(kind, ys, u)
    for ys in range(2):
        @pl.when(jnp.logical_not((yh == c) & (yh == ys)))
        def _(ys=ys):
            for u in range(2):
                x_wait(2, ys, u)

    loads[2].wait()
    attn = x_rcv[0, 0].astype(F32)
    for i in range(1, 6):
        attn = attn + x_rcv[i // 2, i % 2].astype(F32)
    st = res_v[...].astype(F32) + attn
    stream[...] = st
    scaled = (st * gain_ref[...].astype(F32)).astype(BF16)
    dsp[...] = jnp.dot(sel[...], scaled, preferred_element_type=F32).astype(BF16)
    blk_at = (me, pl.ds(pl.multiple_of((b % 4) * CAP, CAP), CAP), pl.ds(pl.multiple_of(c * FW, FW), FW))
    my_src = half == c

    def c_copy(k):
        x = (b + k) % NB
        return rcopy(dsp.at[pl.ds(pl.multiple_of(x * CAP, CAP), CAP)], xg.at[blk_at], c_s.at[k],
                     c_r.at[(b % 4) * 2 + c], chip_dev(x, half))

    own_blk = pltpu.make_async_copy(dsp.at[pl.ds(pl.multiple_of(b * CAP, CAP), CAP)], xg.at[blk_at], loc.at[6])
    for k in range(1, NB):
        c_copy(k).start()
        pend.append(c_copy(k))

    @pl.when(my_src)
    def _():
        own_blk.start()

    @pl.when(jnp.logical_not(my_src))
    def _():
        c_copy(0).start()

    for i in range(8):
        @pl.when(jnp.logical_not(jnp.logical_and(my_src, (b % 4) * 2 + c == i)))
        def _(i=i):
            rcopy(dsp.at[pl.ds(0, CAP)], xg.at[me, pl.ds((i // 2) * CAP, CAP), pl.ds((i % 2) * FW, FW)],
                  c_s.at[0], c_r.at[i], sib).wait_recv()

    @pl.when(my_src)
    def _():
        own_blk.wait()

    sib_gain = xg.at[me, pl.ds(ROWS, GROWS), pl.ds(pl.multiple_of((1 - c) * FW, FW), FW)]
    rcopy(sib_gain, sib_gain, g_s, g_r, sib).wait_recv()

    def ag_copy(d, t, s, slot):
        lo, n = (RD, BLK - RD) if t == 0 else (0, RD)
        if s == 3:
            cut = n // 32 * 16
            lo, n = (lo, cut) if d == 0 else (lo + cut, n - cut)
        ref = xg.at[slot, pl.ds(lo, n)]
        return rcopy(ref, ref, ag_s.at[d, t, s], ag_r.at[d, t, s], dirs[d])

    def agy_copy(i, slot):
        if i == 0:
            lo, n = 0, RD
        elif i < 8:
            lo, n = RD, BLK - RD
        else:
            cut = (BLK - RD) // 32 * 16
            lo, n = (RD, cut) if i == 8 else (RD + cut, BLK - RD - cut)
        ref = xg.at[slot, pl.ds(lo, n)]
        return rcopy(ref, ref, agy_s.at[i], agy_r.at[i], ypart)

    def gate_up(slot):
        blk = xg[slot, 0:ROWS]
        inv = 1.0 / xg[slot, ROWS:BLK][0:1].astype(F32)
        v = blk.astype(F32) * inv
        sq[...] += v * v
        rows = pl.ds(pl.multiple_of(slot * CW, CW), CW)

        def part(i, carry):
            acc[i] += jnp.dot(xg[slot, 0:ROWS], w4[i, rows, :], preferred_element_type=F32)
            return carry
        lax.fori_loop(0, 4, part, 0)

    def slot_of(d, s, t):
        return ((z + NZ - s) % NZ if d == 0 else (z + s) % NZ) * 2 + (yh if t == 0 else 1 - yh)

    other = z * 2 + 1 - yh
    start(agy_copy(0, me))
    for t in range(2):
        for d in range(2):
            start(ag_copy(d, t, 0, me))
        if t == 0:
            start(agy_copy(1, me))
    loads[3].wait()
    loads[4].wait()
    for i in range(2):
        rcopy(gate_hbm, w4.at[1 + 2 * i], w_s.at[i], w_r.at[i], sib).wait_recv()
    drain_a, pend[:] = pend[:-9], pend[-9:]
    for cp in drain_a:
        cp.wait_send()
    acc[...] = jnp.zeros_like(acc)
    sq[...] = jnp.zeros_like(sq)
    gate_up(me)
    gt = gsum[...].T
    hi = gt.astype(BF16)
    g_hi[...] = hi
    g_lo[...] = (gt - hi.astype(F32)).astype(BF16)
    agy_copy(0, other).wait_recv()
    for d in range(2):
        start(ag_copy(d, 2, 0, other))
    for s in range(1, 4):
        for t in range(2):
            for d in range(2):
                slot = slot_of(d, s, 0)
                ag_copy(d, t, s - 1, slot).wait_recv()
                start(ag_copy(d, t, s, slot))
                if t == 0:
                    start(agy_copy(2 * s + d, slot))
        gate_up(slot_of(0, s, 0))
        for d in range(2):
            slot = slot_of(d, s, 1)
            ag_copy(d, 2, s - 1, slot).wait_recv()
            start(ag_copy(d, 2, s, slot))
        gate_up(slot_of(1, s, 0))
        if s == 1:
            agy_copy(1, other).wait_recv()
            gate_up(other)
        else:
            for d in range(2):
                slot = slot_of(d, s - 1, 1)
                agy_copy(2 * (s - 1) + d, slot).wait_recv()
                gate_up(slot)
    far = slot_of(0, 4, 0)
    for d in range(2):
        ag_copy(d, 0, 3, far).wait_recv()
        start(agy_copy(8 + d, far))
    for d in range(2):
        ag_copy(d, 1, 3, far).wait_recv()
    gate_up(far)
    for d in range(2):
        slot = slot_of(d, 3, 1)
        agy_copy(6 + d, slot).wait_recv()
        gate_up(slot)
    far = slot_of(0, 4, 1)
    for d in range(2):
        ag_copy(d, 2, 3, far).wait_recv()
        agy_copy(8 + d, far).wait_recv()
    gate_up(far)

    scale = lax.rsqrt(jnp.sum(sq[...], axis=1, keepdims=True) / D + 1e-05)
    for i in range(2):
        g = acc[i] * scale
        hid[i] = (g / (1.0 + jnp.exp(-g)) * (acc[2 + i] * scale)).astype(BF16)
    loads[5].wait()
    rcopy(down_hbm, dn.at[1], w_s.at[2], w_r.at[2], sib).wait_recv()

    def down_part(zd, t):
        yy = 1 - yh if t == 0 else yh
        cols = pl.ds(pl.multiple_of((zd * 2 + yy) * CW, CW), CW)
        return (jnp.dot(hid[0], dn[0, :, cols], preferred_element_type=F32)
                + jnp.dot(hid[1], dn[1, :, cols], preferred_element_type=F32))

    def ey_copy(k):
        return rcopy(ey_snd.at[k], ey_rcv.at[k], ey_s.at[k], ey_r.at[k], ypart)

    def e0_copy(d, s):
        rows = pl.ds(d * HALF_1, HALF_1) if s == 0 else pl.ds(0, RE)
        return rcopy(e0_snd.at[d, s, rows], e0_rcv.at[d, s, rows], e_s.at[d, 0, s], e_r.at[d, 0, s], dirs[d])

    def e1_copy(d, t, s):
        lo, n = (0, RE) if t == 1 else (RE, ROWS - RE)
        rows = pl.ds(lo + d * (n // 2), n // 2) if s == 0 else pl.ds(lo, n)
        return rcopy(e1_snd.at[d, s, rows], e1_rcv.at[d, s, rows], e_s.at[d, t, s], e_r.at[d, t, s], dirs[d])

    def other_part(k):
        p = down_part(target(k), 0)
        ey_snd[k] = p[RE:ROWS].astype(BF16)
        start(ey_copy(k))
        e0[k] = p[0:RE]

    other_part(0)
    for d in range(2):
        rows = slice(d * HALF_1, (d + 1) * HALF_1)
        e0_snd[d, 0, rows] = e0[0, rows].astype(BF16)
        start(e0_copy(d, 0))
    e1[0] = down_part(target(0), 1)
    for d in range(2):
        rows = slice(d * HALF_1, (d + 1) * HALF_1)
        e1_snd[d, 0, rows] = e1[0, rows].astype(BF16)
        start(e1_copy(d, 1, 0))
    other_part(1)
    other_part(2)
    ey_copy(0).wait_recv()
    for d in range(2):
        rows = slice(RE + d * HALF_2, RE + (d + 1) * HALF_2)
        e1_snd[d, 0, rows] = (e1[0, rows] + ey_rcv[0, d * HALF_2:(d + 1) * HALF_2].astype(F32)).astype(BF16)
        start(e1_copy(d, 2, 0))
    for s in range(1, 4):
        for d in range(2):
            e1[d] = down_part(target(2 * s - 1 + d), 1)
        for d in range(2):
            k = 2 * s - 1 + d
            e0_copy(d, s - 1).wait_recv()
            if s == 1:
                rows = slice(d * HALF_1, (d + 1) * HALF_1)
                rest = slice((1 - d) * HALF_1, (2 - d) * HALF_1)
                e0_snd[d, s, rows] = (e0[k, rows] + e0_rcv[d, 0, rows].astype(F32)).astype(BF16)
                e0_snd[d, s, rest] = e0[k, rest].astype(BF16)
            else:
                e0_snd[d, s] = (e0[k] + e0_rcv[d, s - 1].astype(F32)).astype(BF16)
            start(e0_copy(d, s))
        for t, lo, n in ((1, 0, RE), (2, RE, ROWS - RE)):
            for d in range(2):
                if t == 2:
                    k = 2 * s - 1 + d
                    ey_copy(k).wait_recv()
                    e1[d, RE:ROWS] += ey_rcv[k].astype(F32)
                e1_copy(d, t, s - 1).wait_recv()
                if s == 1:
                    rows = slice(lo + d * (n // 2), lo + (d + 1) * (n // 2))
                    rest = slice(lo + (1 - d) * (n // 2), lo + (2 - d) * (n // 2))
                    e1_snd[d, s, rows] = (e1[d, rows] + e1_rcv[d, 0, rows].astype(F32)).astype(BF16)
                    e1_snd[d, s, rest] = e1[d, rest].astype(BF16)
                else:
                    rows = slice(lo, lo + n)
                    e1_snd[d, s, rows] = (e1[d, rows] + e1_rcv[d, s - 1, rows].astype(F32)).astype(BF16)
                start(e1_copy(d, t, s))
            if t == 1:
                for d in range(2):
                    if 2 * s + 1 + d < NZ:
                        other_part(2 * s + 1 + d)
    drain_e, pend[:] = pend[:-6], pend[-6:]
    for cp in drain_e:
        cp.wait_send()
    e1[0] = down_part(z, 1)
    for d in range(2):
        e0_copy(d, 3).wait_recv()
    ez_snd[...] = (e0[7] + e0_rcv[0, 3].astype(F32) + e0_rcv[1, 3].astype(F32)).astype(BF16)
    ez = rcopy(ez_snd, ez_rcv, ex_s, ex_r, ypart)
    start(ez)
    ey_copy(7).wait_recv()
    e1[0, RE:ROWS] += ey_rcv[7].astype(F32)
    for t in (1, 2):
        for d in range(2):
            e1_copy(d, t, 3).wait_recv()
    e1[0] = e1[0] + e1_rcv[0, 3].astype(F32) + e1_rcv[1, 3].astype(F32)

    def f_copy(i, cc):
        return rcopy(ret_snd.at[pl.ds(i * CAP, CAP), pl.ds(cc * FW, FW)],
                     ret_v.at[pl.ds(pl.multiple_of(b * CAP, CAP), CAP)],
                     f_s.at[i * 2 + cc], f_r.at[b], chip_dev(4 * c + i, cc))

    for i in (2, 3, 0, 1):
        rows = slice(i * CAP, (i + 1) * CAP)
        if i == 0:
            ez.wait_recv()
            e1[0, 0:RE] += ez_rcv[...].astype(F32)
        ret_snd[rows] = e1[0, rows].astype(BF16)
        for cc in range(2):
            to_self = jnp.logical_and(4 * c + i == b, cc == c)
            mine = pltpu.make_async_copy(ret_snd.at[pl.ds(i * CAP, CAP), pl.ds(cc * FW, FW)],
                                         ret_v.at[pl.ds(pl.multiple_of(b * CAP, CAP), CAP)], loc.at[7])

            @pl.when(to_self)
            def _(mine=mine):
                mine.start()
                mine.wait()

            @pl.when(jnp.logical_not(to_self))
            def _(i=i, cc=cc):
                f_copy(i, cc).start()

    drain()
    for x in range(NB):
        @pl.when(jnp.logical_not(jnp.logical_and(my_src, b == x)))
        def _(x=x):
            rcopy(ret_snd.at[pl.ds(0, CAP), pl.ds(0, FW)], ret_v.at[pl.ds(x * CAP, CAP)], f_s.at[0], f_r.at[x],
                  sib).wait_recv()
    out_ref[...] = (stream[...] + jnp.dot(g_hi[...], ret_v[...], preferred_element_type=F32)
                    + jnp.dot(g_lo[...], ret_v[...], preferred_element_type=F32)).astype(BF16)

    for w in range(2):
        @pl.when(jnp.logical_not((yh == c) & (c == w)))
        def _(w=w):
            for u in range(2):
                x_copy(2, w, u).wait_send()

    @pl.when(jnp.logical_not(my_src))
    def _():
        c_copy(0).wait_send()

    for i in range(4):
        for cc in range(2):
            @pl.when(jnp.logical_not(jnp.logical_and(4 * c + i == b, cc == c)))
            def _(i=i, cc=cc):
                f_copy(i, cc).wait_send()


def per_device(residual, heads_out, out_proj, norm_gain, gate_w, up_w, down_w, expert_ids, gate_slots, gate_table):
    any_, vmem = pl.BlockSpec(memory_space=pl.ANY), pl.BlockSpec(memory_space=pltpu.VMEM)
    dma, v = pltpu.SemaphoreType.DMA, pltpu.VMEM
    return pl.pallas_call(
        kernel,
        out_shape=jax.ShapeDtypeStruct((TOK, FW), BF16),
        in_specs=[any_, any_, any_, vmem, any_, any_, any_, vmem, vmem, vmem],
        out_specs=vmem,
        scratch_shapes=[
            v((TOK, FW), BF16), v((TOK, CW), BF16), v((FW, D), BF16), v((NB, 2, NZ, KR, CW), BF16),
            v((16, NZ, KR, CW), BF16), v((NZ, 2, KR, CW), BF16), v((NZ, 2, FW, CW), BF16),
            v((4, D, CW), BF16), v((2, CW, D), BF16), v((NB * CAP, TOK), BF16), v((NB * CAP, TOK), F32),
            v((TOK, NB * CAP), BF16), v((TOK, NB * CAP), BF16),
            v((2, 4, TOK, CW), BF16), v((2, 4, TOK, CW), BF16), v((2, TOK, CW), F32),
            v((TOK, CW), BF16), v((3, 2, TOK, FW), BF16),
            v((TOK, FW), F32), v((NB * CAP, FW), BF16), v((16, BLK, CW), BF16), v((4, ROWS, CW), F32),
            v((ROWS, CW), F32), v((2, ROWS, CW), BF16), v((NZ, RE, CW), F32), v((2, ROWS, CW), F32),
            v((2, 4, RE, CW), BF16), v((2, 4, RE, CW), BF16), v((2, 4, ROWS, CW), BF16), v((2, 4, ROWS, CW), BF16),
            v((NZ, ROWS - RE, CW), BF16), v((NZ, ROWS - RE, CW), BF16), v((RE, CW), BF16), v((RE, CW), BF16),
            v((ROWS, CW), BF16), v((NB * CAP, FW), BF16),
            dma((9,)), dma((3,)), dma((3,)), dma, dma, dma((5, 16)), dma((5, 16)), dma((5, 7)), dma((5, 7)),
            dma((2, 3, 2)), dma((2, 3, 2)), dma((3, 2, 2)), dma((3, 2, 2)), dma, dma,
            dma((8,)), dma((8,)), dma((2, 3, 4)), dma((2, 3, 4)), dma((10,)), dma((10,)),
            dma((2, 3, 4)), dma((2, 3, 4)), dma, dma, dma((8,)), dma((8,)), dma((8,)), dma((8,)),
        ],
        compiler_params=pltpu.CompilerParams(
            collective_id=0, has_side_effects=True, vmem_limit_bytes=60 * 1024 * 1024),
        name="merge_moe",
    )(residual, heads_out, out_proj[0], norm_gain.reshape(1, FW), gate_w[0], up_w[0], down_w[0],
      expert_ids.T, gate_slots.T, gate_table.reshape(1, SLOTS))


def solution(mesh):
    return jax.shard_map(
        per_device,
        mesh=mesh,
        in_specs=(
            P("branch", "expert"), P("branch", "expert"), P("branch", "expert", None), P("expert"),
            P("branch", None, "expert"), P("branch", None, "expert"), P("branch", "expert", None),
            P("branch", None), P("branch", None), P(),
        ),
        out_specs=P("branch", "expert"),
        check_vma=False,
    )
```
